32 devices in a mesh: gx: 4 (over x, core), gy: 2 (over y), gz: 4 (over z).
Axes of the slice: x: 2, y: 2, z: 4, core: 2. Of those that a mesh axis runs over, the one named last changes fastest.
Arguments:
- intensity: float32 [32, 16, 512], P('gx', 'gy', 'gz'), may hold values from -6 to 6
- cotangent: float32 [32, 16, 512], P('gx', 'gy', 'gz'), may hold values from -6 to 6
- departure_cells: int32 [2, 2, 3, 32, 16, 512], P(None, None, None, 'gx', 'gy', 'gz'), may hold values from -2 to 2
- departure_fracs: float32 [2, 2, 3, 32, 16, 512], P(None, None, None, 'gx', 'gy', 'gz'), may hold values from 0 to 1
Outputs:
- intensity_adjoint: float32 [32, 16, 512], P('gx', 'gy', 'gz')
- velocity_adjoint: float32 [3, 32, 16, 512], P(None, 'gx', 'gy', 'gz')
The draws below stay inside these ranges and needn't reach their ends.
All inputs are finite; a program needn't handle non-finite values.
Results may differ from the reference program's by a relative error of at most 0.00002.
Values sent between devices are 32-bit elements; how exact they have to be, the bound alone decides.
No kernel may reach another device: no remote copies, remote signals or barrier semaphores. Data moves between devices by JAX's collectives and lax.ppermute only.
A program may use at most 128 MiB of HBM per device.

```python
import jax
import jax.numpy as jnp

MARGIN = 4
STEPS = 2
SECTIONS = 2
NX = 32
NY = 16
NZ = 512


def place_ends(entries, stream_key, least, largest):
    longest = entries.shape.index(max(entries.shape))
    spots = []
    for shift in (0, 1):
        where = [jax.random.randint(jax.random.fold_in(stream_key, axis), (), 0, length) for axis, length in enumerate(entries.shape)]
        where[longest] = (where[longest] + shift) % entries.shape[longest]
        spots.append(tuple(where))
    return entries.at[spots[0]].set(least).at[spots[1]].set(largest)


def shard_levels(rng, dims, pieces, least, largest):
    def one(position, blocks):
        heights = jax.random.uniform(jax.random.fold_in(jax.random.fold_in(rng, 6), position), (blocks,), jnp.float32, least / len(pieces), largest / len(pieces))
        return jnp.repeat(jnp.exp(heights), dims[position] // blocks).reshape((-1,) + (1,) * (len(dims) - position - 1))

    level = one(*pieces[0])
    for cut in pieces[1:]:
        level = level * one(*cut)
    return level


def bell_draw(stream_key, shape, scale, reach, pieces=(), held_as=jnp.bfloat16):
    array = scale * jax.random.normal(stream_key, shape, jnp.float32)
    if pieces:
        array = array * shard_levels(stream_key, shape, pieces, -0.22, 0.18)
    return jnp.clip(array, -reach, reach).astype(held_as)


def setup_inputs(seed: int = 0) -> dict:
    keys = jax.random.split(jax.random.key(seed), 5)
    return {
        "intensity": bell_draw(keys[0], (NX, NY, NZ), 1.0, 6.0, ((0, 4), (1, 2), (2, 4)), jnp.float32),
        "cotangent": bell_draw(keys[1], (NX, NY, NZ), 1.0, 6.0, ((0, 4), (1, 2), (2, 4)), jnp.float32),
        "departure_cells": place_ends(jax.random.randint(keys[2], (STEPS, SECTIONS, 3, NX, NY, NZ), -2, 3), jax.random.fold_in(keys[2], 1), -2, 2).astype(jnp.int32),
        "departure_fracs": jnp.clip(1.0 * jax.random.uniform(keys[3], (STEPS, SECTIONS, 3, NX, NY, NZ), jnp.float32) ** shard_levels(keys[3], (STEPS, SECTIONS, 3, NX, NY, NZ), ((3, 4), (4, 2), (5, 4)), -0.2, 0.2), 0.0, 1.0),
    }


def cubic_taps(fraction):
    fraction_squared = fraction * fraction
    fraction_cubed = fraction_squared * fraction
    weights = [0.5 * (2.0 * fraction_squared - fraction_cubed - fraction), 0.5 * (3.0 * fraction_cubed - 5.0 * fraction_squared + 2.0), 0.5 * (4.0 * fraction_squared - 3.0 * fraction_cubed + fraction), 0.5 * (fraction_cubed - fraction_squared)]
    slopes = [0.5 * (4.0 * fraction - 3.0 * fraction_squared - 1.0), 0.5 * (9.0 * fraction_squared - 10.0 * fraction), 0.5 * (8.0 * fraction - 9.0 * fraction_squared + 1.0), 0.5 * (3.0 * fraction_squared - 2.0 * fraction)]
    return (weights, slopes)

def shift_table(offsets, taps):
    layers = []
    for target in range(-3, 5):
        summed = jnp.zeros(offsets.shape, jnp.float32)
        for tap_index in range(4):
            summed = summed + jnp.where(offsets + (tap_index - 1) == target, taps[tap_index], 0.0)
        layers.append(summed)
    return jnp.stack(layers)

def build_tables(cell_part, fraction_part, with_slopes):
    weight_tables = []
    slope_tables = []
    for component in range(3):
        weights, slopes = cubic_taps(fraction_part[component])
        weight_tables.append(shift_table(cell_part[component], weights))
        if with_slopes:
            slope_tables.append(shift_table(cell_part[component], slopes))
    return (weight_tables, slope_tables)

def sample(padded, weight_tables, slope_tables, with_value):
    table_x, table_y, table_z = weight_tables
    with_slopes = len(slope_tables) > 0
    extent_x, extent_y, extent_z = table_x.shape[1:]
    offset_base = MARGIN - 3
    shape_out = (padded.shape[0],) + table_x.shape[1:]
    sampled = jnp.zeros(shape_out, jnp.float32)
    grad_x = jnp.zeros(shape_out, jnp.float32)
    grad_y = jnp.zeros(shape_out, jnp.float32)
    grad_z = jnp.zeros(shape_out, jnp.float32)
    for shift_x in range(8):
        for shift_y in range(8):
            slab_rows = padded[:, offset_base + shift_x:offset_base + shift_x + extent_x, offset_base + shift_y:offset_base + shift_y + extent_y, :]
            column = jnp.zeros(shape_out, jnp.float32)
            slope_column = jnp.zeros(shape_out, jnp.float32)
            for shift_z in range(8):
                window = slab_rows[:, :, :, offset_base + shift_z:offset_base + shift_z + extent_z]
                column = column + table_z[shift_z] * window
                if with_slopes:
                    slope_column = slope_column + slope_tables[2][shift_z] * window
            plane_weight = table_x[shift_x] * table_y[shift_y]
            if with_value:
                sampled = sampled + plane_weight * column
            if with_slopes:
                grad_x = grad_x + slope_tables[0][shift_x] * table_y[shift_y] * column
                grad_y = grad_y + table_x[shift_x] * slope_tables[1][shift_y] * column
                grad_z = grad_z + plane_weight * slope_column
    return (sampled, jnp.concatenate([grad_x, grad_y, grad_z]))

def periodic(field):
    return jnp.pad(field, ((0, 0), (MARGIN, MARGIN), (MARGIN, MARGIN), (MARGIN, MARGIN)), mode='wrap')

def spread(field, weight_tables):
    zeros_field = jnp.zeros(field.shape, jnp.float32)
    _, pullback = jax.vjp(lambda inner: sample(periodic(inner), weight_tables, [], True)[0], zeros_field)
    return pullback(field)[0]

def reference(intensity, cotangent, departure_cells, departure_fracs):
    early_dep = build_tables(departure_cells[0, 1], departure_fracs[0, 1], True)
    late_dep = build_tables(departure_cells[1, 1], departure_fracs[1, 1], True)
    early_mid = build_tables(departure_cells[0, 0], departure_fracs[0, 0], False)
    late_mid = build_tables(departure_cells[1, 0], departure_fracs[1, 0], False)
    image_mid, grad_early = sample(periodic(intensity[None]), early_dep[0], early_dep[1], True)
    _, grad_late = sample(periodic(image_mid), late_dep[0], late_dep[1], False)
    grad_late = cotangent[None] * grad_late
    adjoint_mid = spread(cotangent[None], late_dep[0])
    grad_early = adjoint_mid * grad_early
    intensity_adjoint = spread(adjoint_mid, early_dep[0])[0]
    velocity_adjoint = spread(grad_late, late_mid[0]) + spread(grad_early, early_mid[0])
    return (intensity_adjoint, velocity_adjoint)
```

```python
import functools

import jax
import jax.numpy as jnp
from jax import lax
from jax.experimental import pallas as pl
from jax.experimental.pallas import tpu as pltpu
from jax.sharding import PartitionSpec as P

LO = 3
HI = 4
ROWS = 4
SHIFTS = 8
LANES = 128
F32 = jnp.float32


def lane_of(rows):
    return lax.broadcasted_iota(jnp.int32, (rows, LANES), 1)


def group_of(rows):
    return ((lane_of(rows) + LO) & (LANES - 1)) >> 3


def low_lanes(rows):
    return (lane_of(rows) & 7) < HI


def cubic_weights(t):
    t2 = t * t
    t3 = t2 * t
    return (
        0.5 * (2.0 * t2 - t3 - t),
        0.5 * (3.0 * t3 - 5.0 * t2 + 2.0),
        0.5 * (4.0 * t2 - 3.0 * t3 + t),
        0.5 * (t3 - t2),
    )


def cubic_slopes(t):
    t2 = t * t
    return (
        0.5 * (4.0 * t - 3.0 * t2 - 1.0),
        0.5 * (9.0 * t2 - 10.0 * t),
        0.5 * (8.0 * t - 9.0 * t2 + 1.0),
        0.5 * (3.0 * t2 - 2.0 * t),
    )


def write_tables(cells, fracs, step, section, weights, slopes=None):
    def plane(x, carry):
        for c in range(3):
            k = cells[step, section, c, x]
            t = fracs[step, section, c, x]
            hits = {s: k == s for s in range(-2, 3)}
            for ref, taps in ((weights, cubic_weights), (slopes, cubic_slopes)):
                if ref is None:
                    continue
                values = taps(t)
                for j in range(SHIFTS):
                    entry = jnp.zeros_like(t)
                    for a in range(4):
                        s = j - 3 - (a - 1)
                        if -2 <= s <= 2:
                            entry = jnp.where(hits[s], values[a], entry)
                    ref[c, j, x] = entry
        return carry

    lax.fori_loop(0, cells.shape[3], plane, 0)


def shift_planes(extended, rim, shifted):
    planes, rows, _ = extended.shape
    lane = lane_of(rows)
    for X in range(planes):
        core = extended[X]
        ends = pltpu.roll(rim, (-8 * X) % LANES, 1)
        for j in range(SHIFTS):
            d = j - LO
            if d == 0:
                shifted[j, X] = core
            else:
                wraps = lane >= LANES + d if d < 0 else lane < d
                shifted[j, X] = pltpu.roll(jnp.where(wraps, ends, core), (-d) % LANES, 1)


def interpolate(shifted, weights, slopes, nx, ny, emit):
    def plane(x, carry):
        tz = [weights[2, j, x] for j in range(SHIFTS)]
        sz = None if slopes is None else [slopes[2, j, x] for j in range(SHIFTS)]

        def row(sy, sums):
            ty = weights[1, sy, x]
            a = b = c = None
            for sx in range(SHIFTS):
                window = [shifted[j, x + sx, pl.ds(sy + 1, ny), :] for j in range(SHIFTS)]
                column = total([tz[j] * window[j] for j in range(SHIFTS)])
                tx = weights[0, sx, x]
                a = plus(a, tx * column)
                if slopes is not None:
                    b = plus(b, slopes[0, sx, x] * column)
                    c = plus(c, tx * total([sz[j] * window[j] for j in range(SHIFTS)]))
            if slopes is None:
                return (sums[0] + ty * a,)
            return (sums[0] + ty * b, sums[1] + slopes[1, sy, x] * a, sums[2] + ty * c)

        zero = jnp.zeros((ny, LANES), F32)
        sums = lax.fori_loop(0, SHIFTS, row, (zero,) * (1 if slopes is None else 3))
        emit(x, sums)
        return carry

    lax.fori_loop(0, nx, plane, 0)


def total(terms):
    while len(terms) > 1:
        terms = [terms[i] + terms[i + 1] for i in range(0, len(terms), 2)]
    return terms[0]


def plus(a, b):
    return b if a is None else a + b


def deposit(sources, weights, scaled, piles):
    channels, nx, ny, _ = sources.shape
    planes = piles.shape[2]
    piles[...] = jnp.zeros(piles.shape, F32)

    def row(sy, carry):
        for x in range(nx):
            ty = weights[1, sy, x]
            for c in range(channels):
                scaled[c, x] = sources[c, x] * ty
        for X in range(planes):
            sums = [[None] * SHIFTS for _ in range(channels)]
            for x in range(max(0, X - SHIFTS + 1), min(nx - 1, X) + 1):
                tx = weights[0, X - x, x]
                parts = [scaled[c, x] * tx for c in range(channels)]
                for j in range(SHIFTS):
                    tz = weights[2, j, x]
                    for c in range(channels):
                        sums[c][j] = plus(sums[c][j], parts[c] * tz)
            for c in range(channels):
                for j in range(SHIFTS):
                    piles[c, j, X, pl.ds(sy + 1, ny), :] += sums[c][j]
        return carry

    lax.fori_loop(0, SHIFTS, row, 0)


def settle(piles, out, base=None):
    channels, _, planes, rows, _ = piles.shape
    lane = lane_of(rows)
    group = group_of(rows)
    for c in range(channels):
        rim = jnp.zeros((rows, LANES), F32)
        for X in range(planes):
            core = piles[c, LO, X]
            ends = jnp.zeros((rows, LANES), F32)
            for j in range(SHIFTS):
                d = j - LO
                if d == 0:
                    continue
                moved = pltpu.roll(piles[c, j, X], d % LANES, 1)
                wraps = lane >= LANES + d if d < 0 else lane < d
                core = core + jnp.where(wraps, 0.0, moved)
                ends = ends + jnp.where(wraps, moved, 0.0)
            out[c, X] = core if base is None else core + base[c, X]
            rim = jnp.where(group == X, pltpu.roll(ends, (8 * X) % LANES, 1), rim)
        out[c, planes] = rim if base is None else rim + base[c, planes]


def pack_rim(extended):
    planes, rows, _ = extended.shape
    group = group_of(rows)
    rim = jnp.zeros((rows, LANES), F32)
    for X in range(planes):
        rim = jnp.where(group == X, pltpu.roll(extended[X], (8 * X) % LANES, 1), rim)
    return rim


def unpack_rim(rim, X):
    lane = lane_of(rim.shape[0])
    return jnp.where((lane < HI) | (lane >= LANES - LO), pltpu.roll(rim, (-8 * X) % LANES, 1), 0.0)


def fold_rows(message, ny):
    if ny == 2 * ROWS:
        return pltpu.roll(message, ROWS, 0)
    below, above = message[:ROWS], message[ROWS:]
    if ny == ROWS:
        return below + above
    return jnp.concatenate([above, jnp.zeros((ny - 2 * ROWS, LANES), F32), below], axis=0)


def put_edges(out, at, plane, ny):
    if ny == 2 * ROWS:
        out[at] = plane
    else:
        out[at, 0:ROWS] = plane[0:ROWS]
        out[at, ROWS : 2 * ROWS] = plane[ny - ROWS : ny]


def put_rims(out, at, plane, ny):
    out[at, 0:ROWS] = plane[0:ROWS]
    out[at, ROWS : 2 * ROWS] = plane[ROWS + ny : 2 * ROWS + ny]


def split_deposits(piled, outs, at, nx, ny):
    to_y, to_left, to_right, to_left_y, to_right_y, own = outs
    at_y, at_left, at_right, at_own = at
    planes = nx + LO + HI
    core = slice(ROWS, ROWS + ny)
    for i, X in enumerate(list(range(LO, LO + nx)) + [planes]):
        own[at_own + i] = piled[X, core]
        put_rims(to_y, at_y + i, piled[X], ny)
    for i, X in enumerate(list(range(LO)) + [planes]):
        to_left[at_left + i] = piled[X, core]
        put_rims(to_left_y, at_left + i, piled[X], ny)
    for i, X in enumerate(list(range(LO + nx, planes)) + [planes]):
        to_right[at_right + i] = piled[X, core]
        put_rims(to_right_y, at_right + i, piled[X], ny)


def join_deposits(ins, at, nx, ny, put):
    from_y, from_right, from_left, from_right_y, from_left_y, own = ins
    at_y, at_left, at_right, at_own = at

    def right(i):
        return from_right[at_left + i] + fold_rows(from_right_y[at_left + i], ny)

    def left(i):
        return from_left[at_right + i] + fold_rows(from_left_y[at_right + i], ny)

    for x in range(nx):
        plane = own[at_own + x] + fold_rows(from_y[at_y + x], ny)
        if x >= nx - LO:
            plane = plane + right(x - (nx - LO))
        if x < HI:
            plane = plane + left(x)
        put(x, plane)
    group = group_of(ny)
    rim = own[at_own + nx] + fold_rows(from_y[at_y + nx], ny)
    turn = 8 * nx
    high = pltpu.roll(right(LO), turn % LANES, 1)
    low = pltpu.roll(left(HI), (-turn) % LANES, 1)
    rim = rim + jnp.where((group >= nx) & (group < nx + LO), high, 0.0)
    return rim + jnp.where((group >= LO) & (group < LO + HI), low, 0.0)


def join_halo(field, ins, extended, nx, ny):
    from_y, from_right, from_left, from_right_y, from_left_y = ins

    def place(X, core, edges):
        extended[X, 0:ROWS] = edges[ROWS : 2 * ROWS]
        extended[X, ROWS : ROWS + ny] = core
        extended[X, ROWS + ny : 2 * ROWS + ny] = edges[0:ROWS]

    for x in range(nx):
        place(LO + x, field[x], from_y[x])
    for i in range(HI):
        place(LO + nx + i, from_right[i], from_right_y[i])
    for i in range(LO):
        place(i, from_left[i], from_left_y[i])


def split_halo(field, outs, nx, ny):
    to_y, to_left, to_right, to_left_y, to_right_y = outs
    for x in range(nx):
        put_edges(to_y, x, field[x], ny)
    for i in range(HI):
        to_left[i] = field[i]
        put_edges(to_left_y, i, field[i], ny)
    for i in range(LO):
        to_right[i] = field[nx - LO + i]
        put_edges(to_right_y, i, field[nx - LO + i], ny)


def first_kernel(nx, ny, intensity, cotangent, cells, fracs, to_y, to_l, to_r, to_ly, to_ry, own, weights, scaled, piles, piled):
    write_tables(cells, fracs, 1, 1, weights)
    deposit(cotangent, weights, scaled, piles)
    settle(piles, piled)
    split_halo(intensity, (to_y, to_l, to_r, to_ly, to_ry), nx, ny)
    split_deposits(piled.at[0], (to_y, to_l, to_r, to_ly, to_ry, own), (nx, HI, LO, 0), nx, ny)


def first_join_kernel(nx, ny, intensity, from_y, from_r, from_l, from_ry, from_ly, own, extended, part, rims):
    rows = ny + 2 * ROWS
    join_halo(intensity, (from_y, from_r, from_l, from_ry, from_ly), extended, nx, ny)
    rims[0:rows] = pack_rim(extended)

    def put(x, plane):
        part[x] = plane

    rims[rows : rows + ny] = join_deposits((from_y, from_r, from_l, from_ry, from_ly, own), (nx, HI, LO, 0), nx, ny, put)


def middle_kernel(nx, ny, extended, rims_l, rims_r, part, cells, fracs, image, to_y, to_l, to_r, to_ly, to_ry, shifted, adjoint, weights):
    rows = ny + 2 * ROWS
    rim = jnp.where(low_lanes(rows), rims_r[0:rows], rims_l[0:rows])
    shift_planes(extended, rim, shifted)
    write_tables(cells, fracs, 0, 1, weights)

    def emit(x, sums):
        image[x] = sums[0]

    interpolate(shifted, weights, None, nx, ny, emit)
    split_halo(image, (to_y, to_l, to_r, to_ly, to_ry), nx, ny)
    back = jnp.where(low_lanes(ny), rims_l[rows : rows + ny], rims_r[rows : rows + ny])
    for x in range(nx):
        adjoint[0, x] = part[x] + unpack_rim(back, LO + x)


def early_kernel(nx, ny, shifted, adjoint, cells, fracs, grad, piled, weights, slopes, scaled, piles):
    write_tables(cells, fracs, 0, 1, weights, slopes)

    def emit(x, sums):
        for c in range(3):
            grad[c, x] = adjoint[0, x] * sums[c]

    interpolate(shifted, weights, slopes, nx, ny, emit)
    deposit(adjoint, weights, scaled, piles)
    settle(piles, piled)


def early_spread_kernel(nx, ny, grad, cells, fracs, piled, weights, scaled, piles):
    write_tables(cells, fracs, 0, 0, weights)
    deposit(grad, weights, scaled, piles)
    settle(piles, piled)


def second_join_kernel(nx, ny, image, from_y, from_r, from_l, from_ry, from_ly, extended, rims):
    join_halo(image, (from_y, from_r, from_l, from_ry, from_ly), extended, nx, ny)
    rims[...] = pack_rim(extended)


def late_kernel(
    nx, ny, extended, rims_l, rims_r, cotangent, cells, fracs, piled_adjoint, piled_early,
    to_y, to_l, to_r, to_ly, to_ry, own,
    shifted, weights, slopes, grad, scaled, piles, piled,
):
    rows = ny + 2 * ROWS
    shift_planes(extended, jnp.where(low_lanes(rows), rims_r[...], rims_l[...]), shifted)
    write_tables(cells, fracs, 1, 1, weights, slopes)

    def emit(x, sums):
        for c in range(3):
            grad[c, x] = cotangent[0, x] * sums[c]

    interpolate(shifted, weights, slopes, nx, ny, emit)
    write_tables(cells, fracs, 1, 0, weights)
    deposit(grad, weights, scaled, piles)
    settle(piles, piled, piled_early)
    outs = (to_y, to_l, to_r, to_ly, to_ry, own)
    for c in range(4):
        source = piled_adjoint.at[0] if c == 0 else piled.at[c - 1]
        at = (c * (nx + 1), c * (LO + 1), c * (HI + 1), c * (nx + 1))
        split_deposits(source, outs, at, nx, ny)


def last_join_kernel(nx, ny, from_y, from_r, from_l, from_ry, from_ly, own, part, rims):
    ins = (from_y, from_r, from_l, from_ry, from_ly, own)
    for c in range(4):

        def put(x, plane, c=c):
            part[c, x] = plane

        at = (c * (nx + 1), c * (LO + 1), c * (HI + 1), c * (nx + 1))
        rims[c * ny : (c + 1) * ny] = join_deposits(ins, at, nx, ny, put)


def last_kernel(nx, ny, part, rims_l, rims_r, intensity_adjoint, velocity_adjoint):
    low = low_lanes(ny)
    for c in range(4):
        rows = slice(c * ny, (c + 1) * ny)
        back = jnp.where(low, rims_l[rows], rims_r[rows])
        for x in range(nx):
            plane = part[c, x] + unpack_rim(back, LO + x)
            if c == 0:
                intensity_adjoint[x] = plane
            else:
                velocity_adjoint[c - 1, x] = plane


def call(kernel, args, outs, scratch, flops):
    def struct(shape):
        return jax.ShapeDtypeStruct(shape, F32)

    in_vmem = pl.BlockSpec(memory_space=pltpu.VMEM)
    moved = 4 * sum(a.size for a in args)
    return pl.pallas_call(
        kernel,
        out_shape=[struct(s) for s in outs],
        in_specs=[in_vmem] * len(args),
        out_specs=[in_vmem] * len(outs),
        scratch_shapes=[pltpu.VMEM(s, F32) for s in scratch],
        compiler_params=pltpu.CompilerParams(vmem_limit_bytes=24 * 1024 * 1024),
        cost_estimate=pl.CostEstimate(flops=flops, bytes_accessed=moved, transcendentals=0),
    )(*args)


def send(message, moves):
    axes = tuple(axis for axis, _ in moves)
    sizes = [lax.axis_size(axis) for axis in axes]
    if len(axes) == 1:
        pairs = [(i, (i + moves[0][1]) % sizes[0]) for i in range(sizes[0])]
        return lax.ppermute(message, axes[0], pairs)
    pairs = [
        (i * sizes[1] + j, (i + moves[0][1]) % sizes[0] * sizes[1] + (j + moves[1][1]) % sizes[1])
        for i in range(sizes[0])
        for j in range(sizes[1])
    ]
    return lax.ppermute(message, axes, pairs)


def send_y(message, *moves):
    if lax.axis_size("gy") == 2:
        return send(message, moves + (("gy", 1),))
    down = send(message[:, :ROWS], moves + (("gy", -1),))
    up = send(message[:, ROWS:], moves + (("gy", 1),))
    return jnp.concatenate([down, up], axis=1)


def send_sides(to_y, to_l, to_r, to_ly, to_ry):
    left, right = ("gx", -1), ("gx", 1)
    return (
        send_y(to_y),
        send(to_l, (left,)),
        send(to_r, (right,)),
        send_y(to_ly, left),
        send_y(to_ry, right),
    )


def send_z(rims):
    return send(rims, (("gz", 1),)), send(rims, (("gz", -1),))


def body(intensity, cotangent, cells, fracs):
    nx, ny, nz = intensity.shape
    rows = ny + 2 * ROWS
    planes = nx + LO + HI
    table = (3, SHIFTS, nx, ny, nz)
    bound = functools.partial
    ring = 2 * ROWS

    def pile(channels):
        return [(channels, nx, ny, nz), (channels, SHIFTS, planes, rows, nz)]

    def piled(channels):
        return (channels, planes + 1, rows, nz)

    cotangent = cotangent[None]
    unit = nx * ny * nz * 512

    y_planes, l_planes, r_planes = nx, HI, LO
    *outs, own = call(
        bound(first_kernel, nx, ny),
        (intensity, cotangent, cells, fracs),
        [
            (2 * nx + 1, ring, nz),
            (HI + LO + 1, ny, nz),
            (LO + HI + 1, ny, nz),
            (HI + LO + 1, ring, nz),
            (LO + HI + 1, ring, nz),
            (nx + 1, ny, nz),
        ],
        [table] + pile(1) + [piled(1)],
        2 * unit,
    )
    sides = send_sides(*outs)
    extended, part, rims = call(
        bound(first_join_kernel, nx, ny),
        (intensity,) + sides + (own,),
        [(planes, rows, nz), (nx, ny, nz), (rows + ny, nz)],
        [],
        unit // 16,
    )
    rims_l, rims_r = send_z(rims)
    image, *outs, shifted, adjoint = call(
        bound(middle_kernel, nx, ny),
        (extended, rims_l, rims_r, part, cells, fracs),
        [
            (nx, ny, nz),
            (nx, ring, nz),
            (HI, ny, nz),
            (LO, ny, nz),
            (HI, ring, nz),
            (LO, ring, nz),
            (SHIFTS, planes, rows, nz),
            (1, nx, ny, nz),
        ],
        [table],
        2 * unit,
    )
    sides = send_sides(*outs)
    grad, piled_adjoint = call(
        bound(early_kernel, nx, ny),
        (shifted, adjoint, cells, fracs),
        [(3, nx, ny, nz), piled(1)],
        [table, table] + pile(1),
        7 * unit,
    )
    extended, rims = call(
        bound(second_join_kernel, nx, ny),
        (image,) + sides,
        [(planes, rows, nz), (rows, nz)],
        [],
        unit // 16,
    )
    rims_l, rims_r = send_z(rims)
    (piled_early,) = call(
        bound(early_spread_kernel, nx, ny),
        (grad, cells, fracs),
        [piled(3)],
        [table] + pile(3),
        6 * unit,
    )
    *outs, own = call(
        bound(late_kernel, nx, ny),
        (extended, rims_l, rims_r, cotangent, cells, fracs, piled_adjoint, piled_early),
        [
            (4 * (nx + 1), ring, nz),
            (4 * (LO + 1), ny, nz),
            (4 * (HI + 1), ny, nz),
            (4 * (LO + 1), ring, nz),
            (4 * (HI + 1), ring, nz),
            (4 * (nx + 1), ny, nz),
        ],
        [(SHIFTS, planes, rows, nz), table, table, (3, nx, ny, nz)] + pile(3) + [piled(3)],
        11 * unit,
    )
    sides = send_sides(*outs)
    part, rims = call(
        bound(last_join_kernel, nx, ny),
        sides + (own,),
        [(4, nx, ny, nz), (4 * ny, nz)],
        [],
        unit // 16,
    )
    rims_l, rims_r = send_z(rims)
    return tuple(
        call(
            bound(last_kernel, nx, ny),
            (part, rims_l, rims_r),
            [(nx, ny, nz), (3, nx, ny, nz)],
            [],
            unit // 16,
        )
    )


def solution(mesh):
    in_specs = (
        P("gx", "gy", "gz"),
        P("gx", "gy", "gz"),
        P(None, None, None, "gx", "gy", "gz"),
        P(None, None, None, "gx", "gy", "gz"),
    )
    out_specs = (P("gx", "gy", "gz"), P(None, "gx", "gy", "gz"))
    return jax.shard_map(body, mesh=mesh, in_specs=in_specs, out_specs=out_specs, check_vma=False)
```

```python
import functools

import jax
import jax.numpy as jnp
from jax import lax
from jax.experimental import pallas as pl
from jax.experimental.pallas import tpu as pltpu
from jax.sharding import PartitionSpec as P

LO = 3
HI = 4
ROWS = 4
SHIFTS = 8
LANES = 128
PILES = 4
F32 = jnp.float32


def lane_of(rows):
    return lax.broadcasted_iota(jnp.int32, (rows, LANES), 1)


def group_of(rows):
    return ((lane_of(rows) + LO) & (LANES - 1)) >> 3


def low_lanes(rows):
    return (lane_of(rows) & 7) < HI


def cubic_weights(t):
    t2 = t * t
    t3 = t2 * t
    return (
        0.5 * (2.0 * t2 - t3 - t),
        0.5 * (3.0 * t3 - 5.0 * t2 + 2.0),
        0.5 * (4.0 * t2 - 3.0 * t3 + t),
        0.5 * (t3 - t2),
    )


def cubic_slopes(t):
    t2 = t * t
    return (
        0.5 * (4.0 * t - 3.0 * t2 - 1.0),
        0.5 * (9.0 * t2 - 10.0 * t),
        0.5 * (8.0 * t - 9.0 * t2 + 1.0),
        0.5 * (3.0 * t2 - 2.0 * t),
    )


def write_tables(cells, fracs, weights, slopes=None):
    def plane(x, carry):
        for c in range(3):
            k = cells[c, x]
            t = fracs[c, x]
            hits = {s: k == s for s in range(-2, 3)}
            for ref, taps in ((weights, cubic_weights), (slopes, cubic_slopes)):
                if ref is None:
                    continue
                values = taps(t)
                for j in range(SHIFTS):
                    entry = jnp.zeros_like(t)
                    for a in range(4):
                        s = j - 3 - (a - 1)
                        if -2 <= s <= 2:
                            entry = jnp.where(hits[s], values[a], entry)
                    ref[c, j, x] = entry
        return carry

    lax.fori_loop(0, cells.shape[1], plane, 0)


def shift_planes(extended, rim, shifted):
    planes, rows, _ = extended.shape
    lane = lane_of(rows)
    for X in range(planes):
        core = extended[X]
        ends = pltpu.roll(rim, (-8 * X) % LANES, 1)
        for j in range(SHIFTS):
            d = j - LO
            if d == 0:
                shifted[j, X] = core
            else:
                wraps = lane >= LANES + d if d < 0 else lane < d
                shifted[j, X] = pltpu.roll(jnp.where(wraps, ends, core), (-d) % LANES, 1)


def interpolate(shifted, weights, slopes, nx, ny, emit):
    def plane(x, carry):
        tz = [weights[2, j, x] for j in range(SHIFTS)]
        sz = None if slopes is None else [slopes[2, j, x] for j in range(SHIFTS)]

        def row(sy, sums):
            ty = weights[1, sy, x]
            a = b = c = None
            for sx in range(SHIFTS):
                window = [shifted[j, x + sx, pl.ds(sy + 1, ny), :] for j in range(SHIFTS)]
                column = total([tz[j] * window[j] for j in range(SHIFTS)])
                tx = weights[0, sx, x]
                a = plus(a, tx * column)
                if slopes is not None:
                    b = plus(b, slopes[0, sx, x] * column)
                    c = plus(c, tx * total([sz[j] * window[j] for j in range(SHIFTS)]))
            if slopes is None:
                return (sums[0] + ty * a,)
            return (sums[0] + ty * b, sums[1] + slopes[1, sy, x] * a, sums[2] + ty * c)

        zero = jnp.zeros((ny, LANES), F32)
        sums = lax.fori_loop(0, SHIFTS, row, (zero,) * (1 if slopes is None else 3))
        emit(x, sums)
        return carry

    lax.fori_loop(0, nx, plane, 0)


def total(terms):
    while len(terms) > 1:
        terms = [terms[i] + terms[i + 1] for i in range(0, len(terms), 2)]
    return terms[0]


def plus(a, b):
    return b if a is None else a + b


def deposit(sources, weights, scaled, piles):
    channels, nx, ny, _ = sources.shape
    planes = nx + LO + HI
    for pile in piles:
        pile[...] = jnp.zeros(pile.shape, F32)

    def scale(sy, carry):
        for x in range(nx):
            ty = weights[1, sy, x]
            for c in range(channels):
                scaled[c, sy, x] = sources[c, x] * ty
        return carry

    lax.fori_loop(0, SHIFTS, scale, 0)

    def row(sy, carry):
        for X in range(planes):
            sums = [[None] * SHIFTS for _ in range(channels)]
            for x in range(max(0, X - SHIFTS + 1), min(nx - 1, X) + 1):
                tx = weights[0, X - x, x]
                parts = [scaled[c, sy, x] * tx for c in range(channels)]
                for j in range(SHIFTS):
                    tz = weights[2, j, x]
                    for c in range(channels):
                        sums[c][j] = plus(sums[c][j], parts[c] * tz)
            for c in range(channels):
                for j in range(SHIFTS):
                    piles[X % PILES][c, j, X // PILES, pl.ds(sy + 1, ny), :] += sums[c][j]
        return carry

    lax.fori_loop(0, SHIFTS, row, 0)


def settle(piles, out, rims, base=None, base_rims=None):
    channels, planes, rows, _ = out.shape
    lane = lane_of(rows)
    group = group_of(rows)
    for c in range(channels):
        rim = jnp.zeros((rows, LANES), F32)
        for X in range(planes):
            pile = piles[X % PILES]
            core = pile[c, LO, X // PILES]
            ends = jnp.zeros((rows, LANES), F32)
            for j in range(SHIFTS):
                d = j - LO
                if d == 0:
                    continue
                moved = pltpu.roll(pile[c, j, X // PILES], d % LANES, 1)
                wraps = lane >= LANES + d if d < 0 else lane < d
                core = core + jnp.where(wraps, 0.0, moved)
                ends = ends + jnp.where(wraps, moved, 0.0)
            out[c, X] = core if base is None else core + base[c, X]
            rim = jnp.where(group == X, pltpu.roll(ends, (8 * X) % LANES, 1), rim)
        rims[c] = rim if base_rims is None else rim + base_rims[c]


def pack_rim(extended):
    planes, rows, _ = extended.shape
    group = group_of(rows)
    rim = jnp.zeros((rows, LANES), F32)
    for X in range(planes):
        rim = jnp.where(group == X, pltpu.roll(extended[X], (8 * X) % LANES, 1), rim)
    return rim


def unpack_rim(rim, X):
    lane = lane_of(rim.shape[0])
    return jnp.where((lane < HI) | (lane >= LANES - LO), pltpu.roll(rim, (-8 * X) % LANES, 1), 0.0)


def fold_rows(message, ny):
    if ny == 2 * ROWS:
        return pltpu.roll(message, ROWS, 0)
    below, above = message[:ROWS], message[ROWS:]
    if ny == ROWS:
        return below + above
    return jnp.concatenate([above, jnp.zeros((ny - 2 * ROWS, LANES), F32), below], axis=0)


def put_edges(out, at, plane, ny):
    if ny == 2 * ROWS:
        out[at] = plane
    else:
        out[at, 0:ROWS] = plane[0:ROWS]
        out[at, ROWS : 2 * ROWS] = plane[ny - ROWS : ny]


def put_rims(out, at, plane, ny):
    out[at, 0:ROWS] = plane[0:ROWS]
    out[at, ROWS : 2 * ROWS] = plane[ROWS + ny : 2 * ROWS + ny]


def place_edges(extended, X, core, edges, ny):
    extended[X, 0:ROWS] = edges[ROWS : 2 * ROWS]
    extended[X, ROWS : ROWS + ny] = core
    extended[X, ROWS + ny : 2 * ROWS + ny] = edges[0:ROWS]


def fill_planes(extended, middle, from_right, from_left, nx):
    rows = middle.shape[1]
    for x in range(nx):
        extended[LO + x] = middle[x]
    for i in range(HI):
        extended[LO + nx + i] = from_right[i * rows : (i + 1) * rows]
    for i in range(LO):
        extended[i] = from_left[i * rows : (i + 1) * rows]


def edge_planes(middle, to_left, to_right, nx):
    rows = middle.shape[1]
    for i in range(HI):
        to_left[i * rows : (i + 1) * rows] = middle[i]
    for i in range(LO):
        to_right[i * rows : (i + 1) * rows] = middle[nx - LO + i]


def first_kernel(
    nx, ny, intensity, cotangent, cells, fracs,
    image, to_y, own,
    cells_here, fracs_here, cotangent_here, sems, weights, scaled, piled, rims, *piles,
):
    copies = [
        pltpu.make_async_copy(source, target, sems.at[i])
        for i, (source, target) in enumerate(
            (
                (cells.at[1, 1], cells_here),
                (fracs.at[1, 1], fracs_here),
                (cotangent, cotangent_here),
                (intensity, image),
            )
        )
    ]
    for copy in copies:
        copy.start()
    for copy in copies:
        copy.wait()
    write_tables(cells_here, fracs_here, weights)
    deposit(cotangent_here, weights, scaled, piles)
    settle(piles, piled, rims)
    planes = nx + LO + HI
    for x in range(nx):
        put_edges(to_y, x, image[x], ny)
    for X in range(planes + 1):
        plane = piled[0, X] if X < planes else rims[0]
        put_rims(to_y, nx + X, plane, ny)
        own[X] = plane[ROWS : ROWS + ny]


def first_y_kernel(nx, ny, image, own, from_y, middle, part, to_left, to_right):
    planes = nx + LO + HI
    rows = ny + 2 * ROWS
    for x in range(nx):
        place_edges(middle, x, image[x], from_y[x], ny)
    for X in range(planes + 1):
        part[X] = own[X] + fold_rows(from_y[nx + X], ny)
    edge_planes(middle, to_left, to_right, nx)
    for i, X in enumerate(list(range(LO)) + [planes]):
        to_left[HI * rows + i * ny : HI * rows + (i + 1) * ny] = part[X]
    for i, X in enumerate(list(range(LO + nx, planes)) + [planes]):
        to_right[LO * rows + i * ny : LO * rows + (i + 1) * ny] = part[X]


def first_x_kernel(nx, ny, middle, part, from_right, from_left, extended, folded, rims):
    rows = ny + 2 * ROWS
    fill_planes(extended, middle, from_right, from_left, nx)
    rims[0:rows] = pack_rim(extended)

    def right(i):
        return from_right[HI * rows + i * ny : HI * rows + (i + 1) * ny]

    def left(i):
        return from_left[LO * rows + i * ny : LO * rows + (i + 1) * ny]

    for x in range(nx):
        plane = part[LO + x]
        if x >= nx - LO:
            plane = plane + right(x - (nx - LO))
        if x < HI:
            plane = plane + left(x)
        folded[x] = plane
    group = group_of(ny)
    turn = 8 * nx
    high = pltpu.roll(right(LO), turn % LANES, 1)
    low = pltpu.roll(left(HI), (-turn) % LANES, 1)
    rim = part[nx + LO + HI]
    rim = rim + jnp.where((group >= nx) & (group < nx + LO), high, 0.0)
    rims[rows : rows + ny] = rim + jnp.where((group >= LO) & (group < LO + HI), low, 0.0)


def middle_kernel(nx, ny, extended, rims_l, rims_r, folded, cells, fracs, image, to_y, shifted, adjoint, weights):
    rows = ny + 2 * ROWS
    rim = jnp.where(low_lanes(rows), rims_r[0:rows], rims_l[0:rows])
    shift_planes(extended, rim, shifted)
    write_tables(cells.at[0, 1], fracs.at[0, 1], weights)

    def emit(x, sums):
        image[x] = sums[0]

    interpolate(shifted, weights, None, nx, ny, emit)
    for x in range(nx):
        put_edges(to_y, x, image[x], ny)
    back = jnp.where(low_lanes(ny), rims_l[rows : rows + ny], rims_r[rows : rows + ny])
    for x in range(nx):
        adjoint[0, x] = folded[x] + unpack_rim(back, LO + x)


def adjoint_kernel(nx, ny, adjoint, cells, fracs, piled, rims, weights, scaled, *piles):
    write_tables(cells.at[0, 1], fracs.at[0, 1], weights)
    deposit(adjoint, weights, scaled, piles)
    settle(piles, piled, rims)


def early_grad_kernel(nx, ny, shifted, adjoint, cells, fracs, grad, weights, slopes):
    write_tables(cells.at[0, 1], fracs.at[0, 1], weights, slopes)

    def emit(x, sums):
        for c in range(3):
            grad[c, x] = adjoint[0, x] * sums[c]

    interpolate(shifted, weights, slopes, nx, ny, emit)


def early_spread_kernel(nx, ny, grad, cells, fracs, piled, rims, weights, scaled, *piles):
    write_tables(cells.at[0, 0], fracs.at[0, 0], weights)
    deposit(grad, weights, scaled, piles)
    settle(piles, piled, rims)


def second_y_kernel(nx, ny, image, from_y, earlier, middle, to_left, to_right):
    for x in range(nx):
        place_edges(middle, x, image[x], from_y[x], ny)
    edge_planes(middle, to_left, to_right, nx)


def second_x_kernel(nx, ny, middle, from_right, from_left, earlier, extended, rims):
    fill_planes(extended, middle, from_right, from_left, nx)
    rims[...] = pack_rim(extended)


def late_kernel(
    nx, ny, extended, rims_l, rims_r, cotangent, cells, fracs, early, early_rims, adjoint_rims,
    piled, rims,
    shifted, weights, slopes, grad, scaled, rims_here, *piles,
):
    rows = ny + 2 * ROWS
    shift_planes(extended, jnp.where(low_lanes(rows), rims_r[...], rims_l[...]), shifted)
    write_tables(cells.at[1, 1], fracs.at[1, 1], weights, slopes)

    def emit(x, sums):
        for c in range(3):
            grad[c, x] = cotangent[0, x] * sums[c]

    interpolate(shifted, weights, slopes, nx, ny, emit)
    write_tables(cells.at[1, 0], fracs.at[1, 0], weights)
    deposit(grad, weights, scaled, piles)
    settle(piles, piled, rims_here, early, early_rims)
    for c in range(3):
        rims[c * rows : (c + 1) * rows] = rims_here[c]
    rims[3 * rows : 4 * rows] = adjoint_rims[0]


def last_z_kernel(nx, ny, velocity, adjoint, rims_l, rims_r, to_left, to_right, own):
    rows = ny + 2 * ROWS
    low = low_lanes(rows)
    for c in range(4):
        back = jnp.where(low, rims_l[c * rows : (c + 1) * rows], rims_r[c * rows : (c + 1) * rows])
        for X in range(nx + LO + HI):
            plane = (velocity[c, X] if c < 3 else adjoint[0, X]) + unpack_rim(back, X)
            if X < LO:
                i = c * LO + X
                to_left[i * rows : (i + 1) * rows] = plane
            elif X < LO + nx:
                own[c * nx + X - LO] = plane
            else:
                i = c * HI + X - LO - nx
                to_right[i * rows : (i + 1) * rows] = plane


def last_x_kernel(nx, ny, own, from_right, from_left, to_y, part):
    rows = ny + 2 * ROWS
    for c in range(4):
        for x in range(nx):
            plane = own[c * nx + x]
            if x >= nx - LO:
                i = c * LO + x - (nx - LO)
                plane = plane + from_right[i * rows : (i + 1) * rows]
            if x < HI:
                i = c * HI + x
                plane = plane + from_left[i * rows : (i + 1) * rows]
            put_rims(to_y, c * nx + x, plane, ny)
            part[c * nx + x] = plane[ROWS : ROWS + ny]


def last_y_kernel(nx, ny, part, from_y, intensity_adjoint, velocity_adjoint):
    for c in range(4):
        for x in range(nx):
            plane = part[c * nx + x] + fold_rows(from_y[c * nx + x], ny)
            if c == 3:
                intensity_adjoint[x] = plane
            else:
                velocity_adjoint[c, x] = plane


def call(kernel, args, outs, scratch, flops, spaces=None):
    def struct(shape):
        return jax.ShapeDtypeStruct(shape, F32)

    in_vmem = pl.BlockSpec(memory_space=pltpu.VMEM)
    in_specs = [in_vmem] * len(args)
    for i, space in (spaces or {}).items():
        in_specs[i] = pl.BlockSpec(memory_space=space)
    moved = 4 * sum(a.size for a in args)
    return pl.pallas_call(
        kernel,
        out_shape=[struct(s) for s in outs],
        in_specs=in_specs,
        out_specs=[in_vmem] * len(outs),
        scratch_shapes=[pltpu.VMEM(s, F32) if isinstance(s, tuple) else s for s in scratch],
        compiler_params=pltpu.CompilerParams(vmem_limit_bytes=24 * 1024 * 1024),
        cost_estimate=pl.CostEstimate(flops=flops, bytes_accessed=moved, transcendentals=0),
    )(*args)


def send(message, axis, move):
    size = lax.axis_size(axis)
    return lax.ppermute(message, axis, [(i, (i + move) % size) for i in range(size)])


def send_y(message):
    if lax.axis_size("gy") == 2:
        return send(message, "gy", 1)
    down = send(message[:, :ROWS], "gy", -1)
    up = send(message[:, ROWS:], "gy", 1)
    return jnp.concatenate([down, up], axis=1)


def send_x(to_left, to_right):
    return send(to_left, "gx", -1), send(to_right, "gx", 1)


def send_z(rims):
    return send(rims, "gz", 1), send(rims, "gz", -1)


def body(intensity, cotangent, cells, fracs):
    nx, ny, nz = intensity.shape
    rows = ny + 2 * ROWS
    planes = nx + LO + HI
    ring = 2 * ROWS
    table = (3, SHIFTS, nx, ny, nz)
    cotangent = cotangent[None]
    unit = nx * ny * nz * 512

    def run(kernel, *rest, **more):
        return call(functools.partial(kernel, nx, ny), *rest, **more)

    def piles(channels):
        return [(channels, SHIFTS, -(-planes // PILES), rows, nz)] * PILES

    def scaled(channels):
        return (channels, SHIFTS, nx, ny, nz)

    def piled(channels):
        return [(channels, planes, rows, nz), (channels, rows, nz)]

    part = (3, nx, ny, nz)
    image, to_y, own = run(
        first_kernel,
        (intensity, cotangent, cells, fracs),
        [(nx, ny, nz), (nx + planes + 1, ring, nz), (planes + 1, ny, nz)],
        [
            pltpu.VMEM(part, jnp.int32),
            part,
            (1, nx, ny, nz),
            pltpu.SemaphoreType.DMA((4,)),
            table,
            scaled(1),
        ]
        + piled(1)
        + piles(1),
        2 * unit,
        spaces=dict.fromkeys(range(4), pltpu.HBM),
    )
    middle, part, *to_x = run(
        first_y_kernel,
        (image, own, send_y(to_y)),
        [
            (nx, rows, nz),
            (planes + 1, ny, nz),
            (HI * rows + (LO + 1) * ny, nz),
            (LO * rows + (HI + 1) * ny, nz),
        ],
        [],
        unit // 32,
    )
    extended, folded, rims = run(
        first_x_kernel,
        (middle, part) + send_x(*to_x),
        [(planes, rows, nz), (nx, ny, nz), (rows + ny, nz)],
        [],
        unit // 32,
    )
    image, to_y, shifted, adjoint = run(
        middle_kernel,
        (extended,) + send_z(rims) + (folded, cells, fracs),
        [(nx, ny, nz), (nx, ring, nz), (SHIFTS, planes, rows, nz), (1, nx, ny, nz)],
        [table],
        2 * unit,
    )

    from_y = send_y(to_y)
    piled_adjoint, adjoint_rims = run(
        adjoint_kernel,
        (adjoint, cells, fracs),
        piled(1),
        [table, scaled(1)] + piles(1),
        2 * unit,
    )
    middle, *to_x = run(
        second_y_kernel,
        (image, from_y, piled_adjoint),
        [(nx, rows, nz), (HI * rows, nz), (LO * rows, nz)],
        [],
        unit // 32,
        spaces={2: pl.ANY},
    )
    from_right, from_left = send_x(*to_x)
    (grad,) = run(
        early_grad_kernel,
        (shifted, adjoint, cells, fracs),
        [(3, nx, ny, nz)],
        [table, table],
        5 * unit,
    )
    extended, rims = run(
        second_x_kernel,
        (middle, from_right, from_left, grad),
        [(planes, rows, nz), (rows, nz)],
        [],
        unit // 32,
        spaces={3: pl.ANY},
    )
    rims_l, rims_r = send_z(rims)
    early, early_rims = run(
        early_spread_kernel,
        (grad, cells, fracs),
        piled(3),
        [table, scaled(3)] + piles(3),
        6 * unit,
    )

    velocity, rims = run(
        late_kernel,
        (extended, rims_l, rims_r, cotangent, cells, fracs, early, early_rims, adjoint_rims),
        [(3, planes, rows, nz), (4 * rows, nz)],
        [(SHIFTS, planes, rows, nz), table, table, (3, nx, ny, nz), scaled(3), (3, rows, nz)] + piles(3),
        11 * unit,
    )
    *to_x, own = run(
        last_z_kernel,
        (velocity, piled_adjoint) + send_z(rims),
        [(4 * LO * rows, nz), (4 * HI * rows, nz), (4 * nx, rows, nz)],
        [],
        unit // 32,
    )
    to_y, part = run(
        last_x_kernel,
        (own,) + send_x(*to_x),
        [(4 * nx, ring, nz), (4 * nx, ny, nz)],
        [],
        unit // 32,
    )
    return tuple(
        run(
            last_y_kernel,
            (part, send_y(to_y)),
            [(nx, ny, nz), (3, nx, ny, nz)],
            [],
            unit // 32,
        )
    )


def solution(mesh):
    in_specs = (
        P("gx", "gy", "gz"),
        P("gx", "gy", "gz"),
        P(None, None, None, "gx", "gy", "gz"),
        P(None, None, None, "gx", "gy", "gz"),
    )
    out_specs = (P("gx", "gy", "gz"), P(None, "gx", "gy", "gz"))
    return jax.shard_map(body, mesh=mesh, in_specs=in_specs, out_specs=out_specs, check_vma=False)
```

```python
import functools

import jax
import jax.numpy as jnp
from jax import lax
from jax.experimental import pallas as pl
from jax.experimental.pallas import tpu as pltpu
from jax.sharding import PartitionSpec as P

LO = 3
HI = 4
ROWS = 4
SHIFTS = 8
LANES = 128
PILES = 1
F32 = jnp.float32


def lane_of(rows):
    return lax.broadcasted_iota(jnp.int32, (rows, LANES), 1)


def group_of(rows):
    return ((lane_of(rows) + LO) & (LANES - 1)) >> 3


def low_lanes(rows):
    return (lane_of(rows) & 7) < HI


def cubic_weights(t):
    t2 = t * t
    t3 = t2 * t
    return (
        0.5 * (2.0 * t2 - t3 - t),
        0.5 * (3.0 * t3 - 5.0 * t2 + 2.0),
        0.5 * (4.0 * t2 - 3.0 * t3 + t),
        0.5 * (t3 - t2),
    )


def cubic_slopes(t):
    t2 = t * t
    return (
        0.5 * (4.0 * t - 3.0 * t2 - 1.0),
        0.5 * (9.0 * t2 - 10.0 * t),
        0.5 * (8.0 * t - 9.0 * t2 + 1.0),
        0.5 * (3.0 * t2 - 2.0 * t),
    )


def write_tables(cells, fracs, weights, slopes=None):
    def plane(x, carry):
        for c in range(3):
            k = cells[c, x]
            t = fracs[c, x]
            hits = {s: k == s for s in range(-2, 3)}
            for ref, taps in ((weights, cubic_weights), (slopes, cubic_slopes)):
                if ref is None:
                    continue
                values = taps(t)
                for j in range(SHIFTS):
                    entry = jnp.zeros_like(t)
                    for a in range(4):
                        s = j - 3 - (a - 1)
                        if -2 <= s <= 2:
                            entry = jnp.where(hits[s], values[a], entry)
                    ref[c, j, x] = entry
        return carry

    lax.fori_loop(0, cells.shape[1], plane, 0)


def gather_planes(blocks, rims, extended, shifted):
    planes, rows, _ = extended.shape
    ny, nx = rows - 2 * ROWS, planes - LO - HI
    lane = lane_of(rows)
    gx, gy, gz = [lax.axis_index(axis) for axis in ("gx", "gy", "gz")]
    sx, sy, sz = [lax.axis_size(axis) for axis in ("gx", "gy", "gz")]
    below, above = lax.rem(gy + sy - 1, sy), lax.rem(gy + 1, sy)
    before, after = lax.rem(gz + sz - 1, sz), lax.rem(gz + 1, sz)
    low = low_lanes(ny)
    for column, first, count, start in ((sx - 1, nx - LO, LO, 0), (0, 0, nx, LO), (1, 0, HI, LO + nx)):
        row = lax.rem(gx + column, sx) * sy
        ends = []
        for y in (below, gy, above):
            at = (row + y) * sz
            ends.append(jnp.where(low, rims[at + after], rims[at + before]))
        ends = jnp.concatenate([ends[0][ny - ROWS :], ends[1], ends[2][:ROWS]], axis=0)
        for i in range(count):
            x, X = first + i, start + i
            extended[X, 0:ROWS] = blocks[row + below, x, ny - ROWS : ny]
            extended[X, ROWS : ROWS + ny] = blocks[row + gy, x]
            extended[X, ROWS + ny : rows] = blocks[row + above, x, 0:ROWS]
            shift_plane(extended[X], pltpu.roll(ends, (-8 * x) % LANES, 1), shifted, X, lane)


def shift_plane(core, ends, shifted, X, lane):
    for j in range(SHIFTS):
        d = j - LO
        if d == 0:
            shifted[j, X] = core
        else:
            wraps = lane >= LANES + d if d < 0 else lane < d
            shifted[j, X] = pltpu.roll(jnp.where(wraps, ends, core), (-d) % LANES, 1)


def interpolate(shifted, weights, slopes, nx, ny, emit):
    def plane(x, carry):
        tz = [weights[2, j, x] for j in range(SHIFTS)]
        sz = None if slopes is None else [slopes[2, j, x] for j in range(SHIFTS)]

        def row(sy, sums):
            ty = weights[1, sy, x]
            a = b = c = None
            for sx in range(SHIFTS):
                window = [shifted[j, x + sx, pl.ds(sy + 1, ny), :] for j in range(SHIFTS)]
                column = total([tz[j] * window[j] for j in range(SHIFTS)])
                tx = weights[0, sx, x]
                a = plus(a, tx * column)
                if slopes is not None:
                    b = plus(b, slopes[0, sx, x] * column)
                    c = plus(c, tx * total([sz[j] * window[j] for j in range(SHIFTS)]))
            if slopes is None:
                return (sums[0] + ty * a,)
            return (sums[0] + ty * b, sums[1] + slopes[1, sy, x] * a, sums[2] + ty * c)

        zero = jnp.zeros((ny, LANES), F32)
        sums = lax.fori_loop(0, SHIFTS, row, (zero,) * (1 if slopes is None else 3))
        emit(x, sums)
        return carry

    lax.fori_loop(0, nx, plane, 0)


def total(terms):
    while len(terms) > 1:
        terms = [terms[i] + terms[i + 1] for i in range(0, len(terms), 2)]
    return terms[0]


def plus(a, b):
    return b if a is None else a + b


def deposit(sources, weights, scaled, piles):
    channels, nx, ny, _ = sources.shape
    planes = nx + LO + HI
    for pile in piles:
        pile[...] = jnp.zeros(pile.shape, F32)

    def scale(sy, carry):
        for x in range(nx):
            ty = weights[1, sy, x]
            for c in range(channels):
                scaled[c, sy, x] = sources[c, x] * ty
        return carry

    lax.fori_loop(0, SHIFTS, scale, 0)

    def row(sy, carry):
        for X in range(planes):
            sums = [[None] * SHIFTS for _ in range(channels)]
            for x in range(max(0, X - SHIFTS + 1), min(nx - 1, X) + 1):
                tx = weights[0, X - x, x]
                parts = [scaled[c, sy, x] * tx for c in range(channels)]
                for j in range(SHIFTS):
                    tz = weights[2, j, x]
                    for c in range(channels):
                        sums[c][j] = plus(sums[c][j], parts[c] * tz)
            for c in range(channels):
                for j in range(SHIFTS):
                    piles[X % PILES][c, j, X // PILES, pl.ds(sy + 1, ny), :] += sums[c][j]
        return carry

    lax.fori_loop(0, SHIFTS, row, 0)


def settle(piles, out, rims, base=None, base_rims=None):
    channels, planes, rows, _ = out.shape
    lane = lane_of(rows)
    group = group_of(rows)
    for c in range(channels):
        rim = jnp.zeros((rows, LANES), F32)
        for X in range(planes):
            pile = piles[X % PILES]
            core = pile[c, LO, X // PILES]
            ends = jnp.zeros((rows, LANES), F32)
            for j in range(SHIFTS):
                d = j - LO
                if d == 0:
                    continue
                moved = pltpu.roll(pile[c, j, X // PILES], d % LANES, 1)
                wraps = lane >= LANES + d if d < 0 else lane < d
                core = core + jnp.where(wraps, 0.0, moved)
                ends = ends + jnp.where(wraps, moved, 0.0)
            out[c, X] = core if base is None else core + base[c, X]
            rim = jnp.where(group == X, pltpu.roll(ends, (8 * X) % LANES, 1), rim)
        rims[c] = rim if base_rims is None else rim + base_rims[c]


def pack_rim(extended):
    planes, rows, _ = extended.shape
    group = group_of(rows)
    rim = jnp.zeros((rows, LANES), F32)
    for X in range(planes):
        rim = jnp.where(group == X, pltpu.roll(extended[X], (8 * X) % LANES, 1), rim)
    return rim


def unpack_rim(rim, X):
    lane = lane_of(rim.shape[0])
    return jnp.where((lane < HI) | (lane >= LANES - LO), pltpu.roll(rim, (-8 * X) % LANES, 1), 0.0)


def fold_rows(message, ny):
    if ny == 2 * ROWS:
        return pltpu.roll(message, ROWS, 0)
    below, above = message[:ROWS], message[ROWS:]
    if ny == ROWS:
        return below + above
    return jnp.concatenate([above, jnp.zeros((ny - 2 * ROWS, LANES), F32), below], axis=0)


def put_rims(out, at, plane, ny):
    out[at, 0:ROWS] = plane[0:ROWS]
    out[at, ROWS : 2 * ROWS] = plane[ROWS + ny : 2 * ROWS + ny]


def start_kernel(nx, ny, intensity, rim):
    rim[...] = pack_rim(intensity)


def first_kernel(
    nx, ny, cotangent, cells, fracs,
    to_y, own,
    cells_here, fracs_here, cotangent_here, sems, weights, scaled, piled, rims, *piles,
):
    copies = [
        pltpu.make_async_copy(source, target, sems.at[i])
        for i, (source, target) in enumerate(
            (
                (cells.at[1, 1], cells_here),
                (fracs.at[1, 1], fracs_here),
                (cotangent, cotangent_here),
            )
        )
    ]
    for copy in copies:
        copy.start()
    for copy in copies:
        copy.wait()
    write_tables(cells_here, fracs_here, weights)
    deposit(cotangent_here, weights, scaled, piles)
    settle(piles, piled, rims)
    planes = nx + LO + HI
    for X in range(planes + 1):
        plane = piled[0, X] if X < planes else rims[0]
        put_rims(to_y, X, plane, ny)
        own[X] = plane[ROWS : ROWS + ny]


def first_y_kernel(nx, ny, own, from_y, part, to_left, to_right):
    planes = nx + LO + HI
    for X in range(planes + 1):
        part[X] = own[X] + fold_rows(from_y[X], ny)
    for i, X in enumerate(list(range(LO)) + [planes]):
        to_left[i] = part[X]
    for i, X in enumerate(list(range(LO + nx, planes)) + [planes]):
        to_right[i] = part[X]


def first_x_kernel(nx, ny, part, from_right, from_left, folded, rim_out):
    for x in range(nx):
        plane = part[LO + x]
        if x >= nx - LO:
            plane = plane + from_right[x - (nx - LO)]
        if x < HI:
            plane = plane + from_left[x]
        folded[x] = plane
    group = group_of(ny)
    turn = 8 * nx
    high = pltpu.roll(from_right[LO], turn % LANES, 1)
    low = pltpu.roll(from_left[HI], (-turn) % LANES, 1)
    rim = part[nx + LO + HI]
    rim = rim + jnp.where((group >= nx) & (group < nx + LO), high, 0.0)
    rim_out[...] = rim + jnp.where((group >= LO) & (group < LO + HI), low, 0.0)


def middle_kernel(nx, ny, blocks, gathered, cells, fracs, image, rim, shifted, extended, weights):
    gather_planes(blocks, gathered, extended, shifted)
    write_tables(cells.at[0, 1], fracs.at[0, 1], weights)

    def emit(x, sums):
        image[x] = sums[0]

    interpolate(shifted, weights, None, nx, ny, emit)
    rim[...] = pack_rim(image)


def early_kernel(
    nx, ny, shifted, folded, gathered, cells, fracs,
    piled_adjoint, adjoint_rims, piled, rims,
    adjoint, grad, weights, slopes, scaled, scaled_one, *piles,
):
    size = lax.axis_size("gz")
    gz = lax.axis_index("gz")
    before, after = lax.rem(gz + size - 1, size), lax.rem(gz + 1, size)
    back = jnp.where(low_lanes(ny), gathered[before], gathered[after])
    for x in range(nx):
        adjoint[0, x] = folded[x] + unpack_rim(back, LO + x)
    write_tables(cells.at[0, 1], fracs.at[0, 1], weights, slopes)

    def emit(x, sums):
        for c in range(3):
            grad[c, x] = adjoint[0, x] * sums[c]

    interpolate(shifted, weights, slopes, nx, ny, emit)
    ones = [pile.at[0:1] for pile in piles]
    deposit(adjoint, weights, scaled_one, ones)
    settle(ones, piled_adjoint, adjoint_rims)
    write_tables(cells.at[0, 0], fracs.at[0, 0], weights)
    deposit(grad, weights, scaled, piles)
    settle(piles, piled, rims)


def late_kernel(
    nx, ny, blocks, gathered, cotangent, cells, fracs, early, early_rims, adjoint_rims,
    piled, rims,
    shifted, extended, weights, slopes, grad, scaled, rims_here, *piles,
):
    rows = ny + 2 * ROWS
    gather_planes(blocks, gathered, extended, shifted)
    write_tables(cells.at[1, 1], fracs.at[1, 1], weights, slopes)

    def emit(x, sums):
        for c in range(3):
            grad[c, x] = cotangent[0, x] * sums[c]

    interpolate(shifted, weights, slopes, nx, ny, emit)
    write_tables(cells.at[1, 0], fracs.at[1, 0], weights)
    deposit(grad, weights, scaled, piles)
    settle(piles, piled, rims_here, early, early_rims)
    for c in range(3):
        rims[c * rows : (c + 1) * rows] = rims_here[c]
    rims[3 * rows : 4 * rows] = adjoint_rims[0]


def last_z_kernel(nx, ny, velocity, adjoint, rims_l, rims_r, to_left, to_right, own):
    rows = ny + 2 * ROWS
    low = low_lanes(rows)
    for c in range(4):
        back = jnp.where(low, rims_l[c * rows : (c + 1) * rows], rims_r[c * rows : (c + 1) * rows])
        for X in range(nx + LO + HI):
            plane = (velocity[c, X] if c < 3 else adjoint[0, X]) + unpack_rim(back, X)
            if X < LO:
                i = c * LO + X
                to_left[i * rows : (i + 1) * rows] = plane
            elif X < LO + nx:
                own[c * nx + X - LO] = plane
            else:
                i = c * HI + X - LO - nx
                to_right[i * rows : (i + 1) * rows] = plane


def last_x_kernel(nx, ny, own, from_right, from_left, to_y, part):
    rows = ny + 2 * ROWS
    for c in range(4):
        for x in range(nx):
            plane = own[c * nx + x]
            if x >= nx - LO:
                i = c * LO + x - (nx - LO)
                plane = plane + from_right[i * rows : (i + 1) * rows]
            if x < HI:
                i = c * HI + x
                plane = plane + from_left[i * rows : (i + 1) * rows]
            put_rims(to_y, c * nx + x, plane, ny)
            part[c * nx + x] = plane[ROWS : ROWS + ny]


def last_y_kernel(nx, ny, part, from_y, intensity_adjoint, velocity_adjoint):
    for c in range(4):
        for x in range(nx):
            plane = part[c * nx + x] + fold_rows(from_y[c * nx + x], ny)
            if c == 3:
                intensity_adjoint[x] = plane
            else:
                velocity_adjoint[c, x] = plane


def call(kernel, args, outs, scratch, flops, spaces=None, limit=24):
    def struct(shape):
        return jax.ShapeDtypeStruct(shape, F32)

    in_vmem = pl.BlockSpec(memory_space=pltpu.VMEM)
    in_specs = [in_vmem] * len(args)
    for i, space in (spaces or {}).items():
        in_specs[i] = pl.BlockSpec(memory_space=space)
    moved = 4 * sum(a.size for a in args)
    return pl.pallas_call(
        kernel,
        out_shape=[struct(s) for s in outs],
        in_specs=in_specs,
        out_specs=[in_vmem] * len(outs),
        scratch_shapes=[pltpu.VMEM(s, F32) if isinstance(s, tuple) else s for s in scratch],
        compiler_params=pltpu.CompilerParams(vmem_limit_bytes=limit * 1024 * 1024),
        cost_estimate=pl.CostEstimate(flops=flops, bytes_accessed=moved, transcendentals=0),
    )(*args)


def send(message, axis, move):
    size = lax.axis_size(axis)
    return lax.ppermute(message, axis, [(i, (i + move) % size) for i in range(size)])


def send_y(message):
    if lax.axis_size("gy") == 2:
        return send(message, "gy", 1)
    down = send(message[:, :ROWS], "gy", -1)
    up = send(message[:, ROWS:], "gy", 1)
    return jnp.concatenate([down, up], axis=1)


def send_x(to_left, to_right):
    return send(to_left, "gx", -1), send(to_right, "gx", 1)


def send_z(rims):
    return send(rims, "gz", 1), send(rims, "gz", -1)


def body(intensity, cotangent, cells, fracs):
    nx, ny, nz = intensity.shape
    rows = ny + 2 * ROWS
    planes = nx + LO + HI
    ring = 2 * ROWS
    table = (3, SHIFTS, nx, ny, nz)
    cotangent = cotangent[None]
    unit = nx * ny * nz * 512

    def run(kernel, *rest, **more):
        return call(functools.partial(kernel, nx, ny), *rest, **more)

    def piles(channels):
        return [(channels, SHIFTS, -(-planes // PILES), rows, nz)] * PILES

    def scaled(channels):
        return (channels, SHIFTS, nx, ny, nz)

    def piled(channels):
        return [(channels, planes, rows, nz), (channels, rows, nz)]

    def gather(block, rim):
        return (
            lax.all_gather(block, ("gx", "gy")),
            lax.all_gather(rim, ("gx", "gy", "gz")),
        )

    field = (nx, ny, nz)
    (rim,) = run(start_kernel, (intensity,), [(ny, nz)], [], unit // 64)
    blocks, rims = gather(intensity, rim)

    part = (3, nx, ny, nz)
    to_y, own = run(
        first_kernel,
        (cotangent, cells, fracs),
        [(planes + 1, ring, nz), (planes + 1, ny, nz)],
        [
            pltpu.VMEM(part, jnp.int32),
            part,
            (1, nx, ny, nz),
            pltpu.SemaphoreType.DMA((3,)),
            table,
            scaled(1),
        ]
        + piled(1)
        + piles(1),
        2 * unit,
        spaces=dict.fromkeys(range(3), pltpu.HBM),
        limit=61,
    )
    part, *to_x = run(
        first_y_kernel,
        (own, send_y(to_y)),
        [(planes + 1, ny, nz), (LO + 1, ny, nz), (HI + 1, ny, nz)],
        [],
        unit // 32,
    )
    folded, adjoint_rim = run(
        first_x_kernel,
        (part,) + send_x(*to_x),
        [field, (ny, nz)],
        [],
        unit // 32,
    )
    adjoint_rims = lax.all_gather(adjoint_rim, "gz")

    image, rim, shifted = run(
        middle_kernel,
        (blocks, rims, cells, fracs),
        [field, (ny, nz), (SHIFTS, planes, rows, nz)],
        [(planes, rows, nz), table],
        2 * unit,
    )
    blocks, rims = gather(image, rim)

    piled_adjoint, adjoint_rims, early, early_rims = run(
        early_kernel,
        (shifted, folded, adjoint_rims, cells, fracs),
        piled(1) + piled(3),
        [(1,) + field, (3,) + field, table, table, scaled(3), scaled(1)] + piles(3),
        13 * unit,
    )

    velocity, rims = run(
        late_kernel,
        (blocks, rims, cotangent, cells, fracs, early, early_rims, adjoint_rims),
        [(3, planes, rows, nz), (4 * rows, nz)],
        [(SHIFTS, planes, rows, nz), (planes, rows, nz), table, table, (3, nx, ny, nz), scaled(3), (3, rows, nz)]
        + piles(3),
        11 * unit,
    )
    *to_x, own = run(
        last_z_kernel,
        (velocity, piled_adjoint) + send_z(rims),
        [(4 * LO * rows, nz), (4 * HI * rows, nz), (4 * nx, rows, nz)],
        [],
        unit // 32,
    )
    to_y, part = run(
        last_x_kernel,
        (own,) + send_x(*to_x),
        [(4 * nx, ring, nz), (4 * nx, ny, nz)],
        [],
        unit // 32,
    )
    return tuple(
        run(
            last_y_kernel,
            (part, send_y(to_y)),
            [(nx, ny, nz), (3, nx, ny, nz)],
            [],
            unit // 32,
        )
    )


def solution(mesh):
    in_specs = (
        P("gx", "gy", "gz"),
        P("gx", "gy", "gz"),
        P(None, None, None, "gx", "gy", "gz"),
        P(None, None, None, "gx", "gy", "gz"),
    )
    out_specs = (P("gx", "gy", "gz"), P(None, "gx", "gy", "gz"))
    return jax.shard_map(body, mesh=mesh, in_specs=in_specs, out_specs=out_specs, check_vma=False)
```

```python
import functools

import jax
import jax.numpy as jnp
from jax import lax
from jax.experimental import pallas as pl
from jax.experimental.pallas import tpu as pltpu
from jax.sharding import PartitionSpec as P

LO = 3
HI = 4
ROWS = 4
SHIFTS = 8
LANES = 128
PILES = 1
F32 = jnp.float32


def lane_of(rows):
    return lax.broadcasted_iota(jnp.int32, (rows, LANES), 1)


def group_of(rows):
    return ((lane_of(rows) + LO) & (LANES - 1)) >> 3


def low_lanes(rows):
    return (lane_of(rows) & 7) < HI


def cubic_weights(t):
    t2 = t * t
    t3 = t2 * t
    return (
        0.5 * (2.0 * t2 - t3 - t),
        0.5 * (3.0 * t3 - 5.0 * t2 + 2.0),
        0.5 * (4.0 * t2 - 3.0 * t3 + t),
        0.5 * (t3 - t2),
    )


def cubic_slopes(t):
    t2 = t * t
    return (
        0.5 * (4.0 * t - 3.0 * t2 - 1.0),
        0.5 * (9.0 * t2 - 10.0 * t),
        0.5 * (8.0 * t - 9.0 * t2 + 1.0),
        0.5 * (3.0 * t2 - 2.0 * t),
    )


def write_tables(cells, fracs, weights, slopes=None):
    def plane(x, carry):
        for c in range(3):
            k = cells[c, x]
            t = fracs[c, x]
            hits = {s: k == s for s in range(-2, 3)}
            for ref, taps in ((weights, cubic_weights), (slopes, cubic_slopes)):
                if ref is None:
                    continue
                values = taps(t)
                for j in range(SHIFTS):
                    entry = jnp.zeros_like(t)
                    for a in range(4):
                        s = j - 3 - (a - 1)
                        if -2 <= s <= 2:
                            entry = jnp.where(hits[s], values[a], entry)
                    ref[c, j, x] = entry
        return carry

    lax.fori_loop(0, cells.shape[1], plane, 0)


def gather_planes(blocks, rims, extended, shifted):
    planes, rows, _ = extended.shape
    ny, nx = rows - 2 * ROWS, planes - LO - HI
    lane = lane_of(rows)
    gx, gy, gz = [lax.axis_index(axis) for axis in ("gx", "gy", "gz")]
    sx, sy, sz = [lax.axis_size(axis) for axis in ("gx", "gy", "gz")]
    below, above = lax.rem(gy + sy - 1, sy), lax.rem(gy + 1, sy)
    before, after = lax.rem(gz + sz - 1, sz), lax.rem(gz + 1, sz)
    low = low_lanes(ny)
    for column, first, count, start in ((sx - 1, nx - LO, LO, 0), (0, 0, nx, LO), (1, 0, HI, LO + nx)):
        row = lax.rem(gx + column, sx) * sy
        ends = []
        for y in (below, gy, above):
            at = (row + y) * sz
            ends.append(jnp.where(low, rims[at + after], rims[at + before]))
        ends = jnp.concatenate([ends[0][ny - ROWS :], ends[1], ends[2][:ROWS]], axis=0)
        for i in range(count):
            x, X = first + i, start + i
            extended[X, 0:ROWS] = blocks[row + below, x, ny - ROWS : ny]
            extended[X, ROWS : ROWS + ny] = blocks[row + gy, x]
            extended[X, ROWS + ny : rows] = blocks[row + above, x, 0:ROWS]
            shift_plane(extended[X], pltpu.roll(ends, (-8 * x) % LANES, 1), shifted, X, lane)


def shift_plane(core, ends, shifted, X, lane):
    for j in range(SHIFTS):
        d = j - LO
        if d == 0:
            shifted[j, X] = core
        else:
            wraps = lane >= LANES + d if d < 0 else lane < d
            shifted[j, X] = pltpu.roll(jnp.where(wraps, ends, core), (-d) % LANES, 1)


def interpolate(shifted, weights, slopes, nx, ny, emit):
    def plane(x, carry):
        tz = [weights[2, j, x] for j in range(SHIFTS)]
        sz = None if slopes is None else [slopes[2, j, x] for j in range(SHIFTS)]

        def row(sy, sums):
            ty = weights[1, sy, x]
            a = b = c = None
            for sx in range(SHIFTS):
                window = [shifted[j, x + sx, pl.ds(sy + 1, ny), :] for j in range(SHIFTS)]
                column = total([tz[j] * window[j] for j in range(SHIFTS)])
                tx = weights[0, sx, x]
                a = plus(a, tx * column)
                if slopes is not None:
                    b = plus(b, slopes[0, sx, x] * column)
                    c = plus(c, tx * total([sz[j] * window[j] for j in range(SHIFTS)]))
            if slopes is None:
                return (sums[0] + ty * a,)
            return (sums[0] + ty * b, sums[1] + slopes[1, sy, x] * a, sums[2] + ty * c)

        zero = jnp.zeros((ny, LANES), F32)
        sums = lax.fori_loop(0, SHIFTS, row, (zero,) * (1 if slopes is None else 3))
        emit(x, sums)
        return carry

    lax.fori_loop(0, nx, plane, 0)


def total(terms):
    while len(terms) > 1:
        terms = [terms[i] + terms[i + 1] for i in range(0, len(terms), 2)]
    return terms[0]


def plus(a, b):
    return b if a is None else a + b


def deposit(sources, weights, scaled, piles):
    channels, nx, ny, _ = sources.shape
    planes = nx + LO + HI
    for pile in piles:
        pile[...] = jnp.zeros(pile.shape, F32)

    def scale(sy, carry):
        for x in range(nx):
            ty = weights[1, sy, x]
            for c in range(channels):
                scaled[c, sy, x] = sources[c, x] * ty
        return carry

    lax.fori_loop(0, SHIFTS, scale, 0)

    def row(sy, carry):
        for X in range(planes):
            sums = [[None] * SHIFTS for _ in range(channels)]
            for x in range(max(0, X - SHIFTS + 1), min(nx - 1, X) + 1):
                tx = weights[0, X - x, x]
                parts = [scaled[c, sy, x] * tx for c in range(channels)]
                for j in range(SHIFTS):
                    tz = weights[2, j, x]
                    for c in range(channels):
                        sums[c][j] = plus(sums[c][j], parts[c] * tz)
            for c in range(channels):
                for j in range(SHIFTS):
                    piles[X % PILES][c, j, X // PILES, pl.ds(sy + 1, ny), :] += sums[c][j]
        return carry

    lax.fori_loop(0, SHIFTS, row, 0)


def settle(piles, out, rims, base=None, base_rims=None):
    channels, planes, rows, _ = out.shape
    lane = lane_of(rows)
    group = group_of(rows)
    for c in range(channels):
        rim = jnp.zeros((rows, LANES), F32)
        for X in range(planes):
            pile = piles[X % PILES]
            core = pile[c, LO, X // PILES]
            ends = jnp.zeros((rows, LANES), F32)
            for j in range(SHIFTS):
                d = j - LO
                if d == 0:
                    continue
                moved = pltpu.roll(pile[c, j, X // PILES], d % LANES, 1)
                wraps = lane >= LANES + d if d < 0 else lane < d
                core = core + jnp.where(wraps, 0.0, moved)
                ends = ends + jnp.where(wraps, moved, 0.0)
            out[c, X] = core if base is None else core + base[c, X]
            rim = jnp.where(group == X, pltpu.roll(ends, (8 * X) % LANES, 1), rim)
        rims[c] = rim if base_rims is None else rim + base_rims[c]


def pack_rim(extended):
    planes, rows, _ = extended.shape
    group = group_of(rows)
    rim = jnp.zeros((rows, LANES), F32)
    for X in range(planes):
        rim = jnp.where(group == X, pltpu.roll(extended[X], (8 * X) % LANES, 1), rim)
    return rim


def unpack_rim(rim, X):
    lane = lane_of(rim.shape[0])
    return jnp.where((lane < HI) | (lane >= LANES - LO), pltpu.roll(rim, (-8 * X) % LANES, 1), 0.0)


def fold_rows(message, ny):
    if ny == 2 * ROWS:
        return pltpu.roll(message, ROWS, 0)
    below, above = message[:ROWS], message[ROWS:]
    if ny == ROWS:
        return below + above
    return jnp.concatenate([above, jnp.zeros((ny - 2 * ROWS, LANES), F32), below], axis=0)


def put_rims(out, at, plane, ny):
    out[at, 0:ROWS] = plane[0:ROWS]
    out[at, ROWS : 2 * ROWS] = plane[ROWS + ny : 2 * ROWS + ny]


def start_kernel(nx, ny, intensity, rim):
    rim[...] = pack_rim(intensity)


def first_kernel(
    nx, ny, cotangent, cells, fracs,
    to_y, own,
    cells_here, fracs_here, cotangent_here, sems, weights, scaled, piled, rims, *piles,
):
    copies = [
        pltpu.make_async_copy(source, target, sems.at[i])
        for i, (source, target) in enumerate(
            (
                (cells.at[1, 1], cells_here),
                (fracs.at[1, 1], fracs_here),
                (cotangent, cotangent_here),
            )
        )
    ]
    for copy in copies:
        copy.start()
    for copy in copies:
        copy.wait()
    write_tables(cells_here, fracs_here, weights)
    deposit(cotangent_here, weights, scaled, piles)
    settle(piles, piled, rims)
    planes = nx + LO + HI
    for X in range(planes + 1):
        plane = piled[0, X] if X < planes else rims[0]
        put_rims(to_y, X, plane, ny)
        own[X] = plane[ROWS : ROWS + ny]


def first_y_kernel(nx, ny, own, from_y, part, to_left, to_right):
    planes = nx + LO + HI
    for X in range(planes + 1):
        part[X] = own[X] + fold_rows(from_y[X], ny)
    for i, X in enumerate(list(range(LO)) + [planes]):
        to_left[i] = part[X]
    for i, X in enumerate(list(range(LO + nx, planes)) + [planes]):
        to_right[i] = part[X]


def first_x_kernel(nx, ny, part, from_right, from_left, folded, rim_out):
    for x in range(nx):
        plane = part[LO + x]
        if x >= nx - LO:
            plane = plane + from_right[x - (nx - LO)]
        if x < HI:
            plane = plane + from_left[x]
        folded[x] = plane
    group = group_of(ny)
    turn = 8 * nx
    high = pltpu.roll(from_right[LO], turn % LANES, 1)
    low = pltpu.roll(from_left[HI], (-turn) % LANES, 1)
    rim = part[nx + LO + HI]
    rim = rim + jnp.where((group >= nx) & (group < nx + LO), high, 0.0)
    rim_out[...] = rim + jnp.where((group >= LO) & (group < LO + HI), low, 0.0)


def middle_kernel(nx, ny, blocks, gathered, cells, fracs, image, rim, shifted, extended, weights):
    gather_planes(blocks, gathered, extended, shifted)
    write_tables(cells.at[0, 1], fracs.at[0, 1], weights)

    def emit(x, sums):
        image[x] = sums[0]

    interpolate(shifted, weights, None, nx, ny, emit)
    rim[...] = pack_rim(image)


def early_kernel(
    nx, ny, shifted, folded, gathered, cells, fracs,
    piled_adjoint, adjoint_rims, piled, rims,
    adjoint, grad, weights, slopes, scaled, scaled_one, *piles,
):
    size = lax.axis_size("gz")
    gz = lax.axis_index("gz")
    before, after = lax.rem(gz + size - 1, size), lax.rem(gz + 1, size)
    back = jnp.where(low_lanes(ny), gathered[before], gathered[after])
    for x in range(nx):
        adjoint[0, x] = folded[x] + unpack_rim(back, LO + x)
    write_tables(cells.at[0, 1], fracs.at[0, 1], weights, slopes)

    def emit(x, sums):
        for c in range(3):
            grad[c, x] = adjoint[0, x] * sums[c]

    interpolate(shifted, weights, slopes, nx, ny, emit)
    ones = [pile.at[0:1] for pile in piles]
    deposit(adjoint, weights, scaled_one, ones)
    settle(ones, piled_adjoint, adjoint_rims)
    write_tables(cells.at[0, 0], fracs.at[0, 0], weights)
    deposit(grad, weights, scaled, piles)
    settle(piles, piled, rims)


def late_kernel(
    nx, ny, blocks, gathered, cotangent, cells, fracs, early, early_rims, adjoint_rims,
    piled, rims,
    shifted, extended, weights, slopes, grad, scaled, rims_here, *piles,
):
    rows = ny + 2 * ROWS
    gather_planes(blocks, gathered, extended, shifted)
    write_tables(cells.at[1, 1], fracs.at[1, 1], weights, slopes)

    def emit(x, sums):
        for c in range(3):
            grad[c, x] = cotangent[0, x] * sums[c]

    interpolate(shifted, weights, slopes, nx, ny, emit)
    write_tables(cells.at[1, 0], fracs.at[1, 0], weights)
    deposit(grad, weights, scaled, piles)
    settle(piles, piled, rims_here, early, early_rims)
    for c in range(3):
        rims[c * rows : (c + 1) * rows] = rims_here[c]
    rims[3 * rows : 4 * rows] = adjoint_rims[0]


def last_z_kernel(nx, ny, velocity, adjoint, rims_l, rims_r, to_left, to_right, own):
    rows = ny + 2 * ROWS
    low = low_lanes(rows)
    for c in range(4):
        back = jnp.where(low, rims_l[c * rows : (c + 1) * rows], rims_r[c * rows : (c + 1) * rows])
        for X in range(nx + LO + HI):
            plane = (velocity[c, X] if c < 3 else adjoint[0, X]) + unpack_rim(back, X)
            if X < LO:
                i = c * LO + X
                to_left[i * rows : (i + 1) * rows] = plane
            elif X < LO + nx:
                own[c * nx + X - LO] = plane
            else:
                i = c * HI + X - LO - nx
                to_right[i * rows : (i + 1) * rows] = plane


def last_x_kernel(nx, ny, own, from_right, from_left, to_y, part):
    rows = ny + 2 * ROWS
    for c in range(4):
        for x in range(nx):
            plane = own[c * nx + x]
            if x >= nx - LO:
                i = c * LO + x - (nx - LO)
                plane = plane + from_right[i * rows : (i + 1) * rows]
            if x < HI:
                i = c * HI + x
                plane = plane + from_left[i * rows : (i + 1) * rows]
            put_rims(to_y, c * nx + x, plane, ny)
            part[c * nx + x] = plane[ROWS : ROWS + ny]


def last_y_kernel(nx, ny, part, from_y, intensity_adjoint, velocity_adjoint):
    for c in range(4):
        for x in range(nx):
            plane = part[c * nx + x] + fold_rows(from_y[c * nx + x], ny)
            if c == 3:
                intensity_adjoint[x] = plane
            else:
                velocity_adjoint[c, x] = plane


def call(kernel, args, outs, scratch, flops, spaces=None, limit=24):
    def struct(shape):
        return jax.ShapeDtypeStruct(shape, F32)

    in_vmem = pl.BlockSpec(memory_space=pltpu.VMEM)
    in_specs = [in_vmem] * len(args)
    for i, space in (spaces or {}).items():
        in_specs[i] = pl.BlockSpec(memory_space=space)
    moved = 4 * sum(a.size for a in args)
    return pl.pallas_call(
        kernel,
        out_shape=[struct(s) for s in outs],
        in_specs=in_specs,
        out_specs=[in_vmem] * len(outs),
        scratch_shapes=[pltpu.VMEM(s, F32) if isinstance(s, tuple) else s for s in scratch],
        compiler_params=pltpu.CompilerParams(vmem_limit_bytes=limit * 1024 * 1024),
        cost_estimate=pl.CostEstimate(flops=flops, bytes_accessed=moved, transcendentals=0),
    )(*args)


def send(message, axis, move):
    size = lax.axis_size(axis)
    return lax.ppermute(message, axis, [(i, (i + move) % size) for i in range(size)])


def send_y(message):
    if lax.axis_size("gy") == 2:
        return send(message, "gy", 1)
    down = send(message[:, :ROWS], "gy", -1)
    up = send(message[:, ROWS:], "gy", 1)
    return jnp.concatenate([down, up], axis=1)


def send_x(to_left, to_right):
    return send(to_left, "gx", -1), send(to_right, "gx", 1)


def send_z(rims):
    return send(rims, "gz", 1), send(rims, "gz", -1)


def spread(block, axes):
    size = 1
    for axis in axes:
        size *= lax.axis_size(axis)
    slots = jnp.broadcast_to(block, (size,) + block.shape)
    return lax.all_to_all(slots, axes, 0, 0)


def body(intensity, cotangent, cells, fracs):
    nx, ny, nz = intensity.shape
    rows = ny + 2 * ROWS
    planes = nx + LO + HI
    ring = 2 * ROWS
    table = (3, SHIFTS, nx, ny, nz)
    cotangent = cotangent[None]
    unit = nx * ny * nz * 512

    def run(kernel, *rest, **more):
        return call(functools.partial(kernel, nx, ny), *rest, **more)

    def piles(channels):
        return [(channels, SHIFTS, -(-planes // PILES), rows, nz)] * PILES

    def scaled(channels):
        return (channels, SHIFTS, nx, ny, nz)

    def piled(channels):
        return [(channels, planes, rows, nz), (channels, rows, nz)]

    def gather(block, rim):
        return (
            spread(block, ("gx", "gy")),
            spread(rim, ("gx", "gy", "gz")),
        )

    field = (nx, ny, nz)
    (rim,) = run(start_kernel, (intensity,), [(ny, nz)], [], unit // 64)
    blocks, rims = gather(intensity, rim)

    part = (3, nx, ny, nz)
    to_y, own = run(
        first_kernel,
        (cotangent, cells, fracs),
        [(planes + 1, ring, nz), (planes + 1, ny, nz)],
        [
            pltpu.VMEM(part, jnp.int32),
            part,
            (1, nx, ny, nz),
            pltpu.SemaphoreType.DMA((3,)),
            table,
            scaled(1),
        ]
        + piled(1)
        + piles(1),
        2 * unit,
        spaces=dict.fromkeys(range(3), pltpu.HBM),
        limit=61,
    )
    part, *to_x = run(
        first_y_kernel,
        (own, send_y(to_y)),
        [(planes + 1, ny, nz), (LO + 1, ny, nz), (HI + 1, ny, nz)],
        [],
        unit // 32,
    )
    folded, adjoint_rim = run(
        first_x_kernel,
        (part,) + send_x(*to_x),
        [field, (ny, nz)],
        [],
        unit // 32,
    )
    adjoint_rims = spread(adjoint_rim, ("gz",))

    image, rim, shifted = run(
        middle_kernel,
        (blocks, rims, cells, fracs),
        [field, (ny, nz), (SHIFTS, planes, rows, nz)],
        [(planes, rows, nz), table],
        2 * unit,
    )
    blocks, rims = gather(image, rim)

    piled_adjoint, adjoint_rims, early, early_rims = run(
        early_kernel,
        (shifted, folded, adjoint_rims, cells, fracs),
        piled(1) + piled(3),
        [(1,) + field, (3,) + field, table, table, scaled(3), scaled(1)] + piles(3),
        13 * unit,
    )

    velocity, rims = run(
        late_kernel,
        (blocks, rims, cotangent, cells, fracs, early, early_rims, adjoint_rims),
        [(3, planes, rows, nz), (4 * rows, nz)],
        [(SHIFTS, planes, rows, nz), (planes, rows, nz), table, table, (3, nx, ny, nz), scaled(3), (3, rows, nz)]
        + piles(3),
        11 * unit,
    )
    *to_x, own = run(
        last_z_kernel,
        (velocity, piled_adjoint) + send_z(rims),
        [(4 * LO * rows, nz), (4 * HI * rows, nz), (4 * nx, rows, nz)],
        [],
        unit // 32,
    )
    to_y, part = run(
        last_x_kernel,
        (own,) + send_x(*to_x),
        [(4 * nx, ring, nz), (4 * nx, ny, nz)],
        [],
        unit // 32,
    )
    return tuple(
        run(
            last_y_kernel,
            (part, send_y(to_y)),
            [(nx, ny, nz), (3, nx, ny, nz)],
            [],
            unit // 32,
        )
    )


def solution(mesh):
    in_specs = (
        P("gx", "gy", "gz"),
        P("gx", "gy", "gz"),
        P(None, None, None, "gx", "gy", "gz"),
        P(None, None, None, "gx", "gy", "gz"),
    )
    out_specs = (P("gx", "gy", "gz"), P(None, "gx", "gy", "gz"))
    return jax.shard_map(body, mesh=mesh, in_specs=in_specs, out_specs=out_specs, check_vma=False)
```

```python
import functools

import jax
import jax.numpy as jnp
from jax import lax
from jax.experimental import pallas as pl
from jax.experimental.pallas import tpu as pltpu
from jax.sharding import PartitionSpec as P

LO = 3
HI = 4
ROWS = 4
SHIFTS = 8
LANES = 128
F32 = jnp.float32


def lane_of(rows):
    return lax.broadcasted_iota(jnp.int32, (rows, LANES), 1)


def group_of(rows):
    return ((lane_of(rows) + LO) & (LANES - 1)) >> 3


def low_lanes(rows):
    return (lane_of(rows) & 7) < HI


def cubic_weights(t):
    t2 = t * t
    t3 = t2 * t
    return (
        0.5 * (2.0 * t2 - t3 - t),
        0.5 * (3.0 * t3 - 5.0 * t2 + 2.0),
        0.5 * (4.0 * t2 - 3.0 * t3 + t),
        0.5 * (t3 - t2),
    )


def cubic_slopes(t):
    t2 = t * t
    return (
        0.5 * (4.0 * t - 3.0 * t2 - 1.0),
        0.5 * (9.0 * t2 - 10.0 * t),
        0.5 * (8.0 * t - 9.0 * t2 + 1.0),
        0.5 * (3.0 * t2 - 2.0 * t),
    )


def write_tables(cells, fracs, weights, slopes=None):
    def plane(x, carry):
        for c in range(3):
            k = cells[c, x]
            t = fracs[c, x]
            hits = {s: k == s for s in range(-2, 3)}
            for ref, taps in ((weights, cubic_weights), (slopes, cubic_slopes)):
                if ref is None:
                    continue
                values = taps(t)
                for j in range(SHIFTS):
                    entry = jnp.zeros_like(t)
                    for a in range(4):
                        s = j - 3 - (a - 1)
                        if -2 <= s <= 2:
                            entry = jnp.where(hits[s], values[a], entry)
                    ref[c, j, x] = entry
        return carry

    lax.fori_loop(0, cells.shape[1], plane, 0)


def shift_planes(extended, rim, shifted):
    planes, rows, _ = extended.shape
    lane = lane_of(rows)
    for X in range(planes):
        core = extended[X]
        ends = pltpu.roll(rim, (-8 * X) % LANES, 1)
        for j in range(SHIFTS):
            d = j - LO
            if d == 0:
                shifted[j, X] = core
            else:
                wraps = lane >= LANES + d if d < 0 else lane < d
                shifted[j, X] = pltpu.roll(jnp.where(wraps, ends, core), (-d) % LANES, 1)


def interpolate(shifted, weights, slopes, nx, ny, emit):
    pair = 2 if nx % 2 == 0 else 1

    def plane(step, carry):
        x0 = step * pair
        tz = [[weights[2, j, x0 + p] for j in range(SHIFTS)] for p in range(pair)]
        if slopes is not None:
            sz = [[slopes[2, j, x0 + p] for j in range(SHIFTS)] for p in range(pair)]

        def row(sy, sums):
            a, b, c = [None] * pair, [None] * pair, [None] * pair
            for q in range(SHIFTS + pair - 1):
                window = [shifted[j, x0 + q, pl.ds(sy + 1, ny), :] for j in range(SHIFTS)]
                for p in range(pair):
                    sx = q - p
                    if not 0 <= sx < SHIFTS:
                        continue
                    x = x0 + p
                    column = total([tz[p][j] * window[j] for j in range(SHIFTS)])
                    tx = weights[0, sx, x]
                    a[p] = plus(a[p], tx * column)
                    if slopes is not None:
                        b[p] = plus(b[p], slopes[0, sx, x] * column)
                        c[p] = plus(c[p], tx * total([sz[p][j] * window[j] for j in range(SHIFTS)]))
            out = []
            for p in range(pair):
                ty = weights[1, sy, x0 + p]
                if slopes is None:
                    out.append((sums[p][0] + ty * a[p],))
                else:
                    steep = slopes[1, sy, x0 + p] * a[p]
                    out.append((sums[p][0] + ty * b[p], sums[p][1] + steep, sums[p][2] + ty * c[p]))
            return tuple(out)

        zero = jnp.zeros((ny, LANES), F32)
        sums = lax.fori_loop(0, SHIFTS, row, ((zero,) * (1 if slopes is None else 3),) * pair)
        for p in range(pair):
            emit(x0 + p, sums[p])
        return carry

    lax.fori_loop(0, nx // pair, plane, 0)


def total(terms):
    while len(terms) > 1:
        terms = [terms[i] + terms[i + 1] for i in range(0, len(terms), 2)]
    return terms[0]


def plus(a, b):
    return b if a is None else a + b


def deposit(sources, weights, scaled, piles, ys, js):
    channels, nx, ny, _ = sources.shape
    planes = nx + LO + HI
    piles[...] = jnp.zeros(piles.shape, F32)

    def scale(sy, carry):
        for x in range(nx):
            ty = weights[1, sy, x]
            for c in range(channels):
                scaled[c, sy, x] = sources[c, x] * ty
        return carry

    lax.fori_loop(0, SHIFTS, scale, 0)

    def row(step, carry):
        first = step * ys
        pending = []

        def flush(count):
            for _ in range(min(count, len(pending))):
                c, y, j, X, value = pending.pop(0)
                piles[c, j, X, pl.ds(first + y + 1, ny), :] += value

        for X in range(planes):
            xs = range(max(0, X - SHIFTS + 1), min(nx - 1, X) + 1)
            for j0 in range(0, SHIFTS, js):
                pace = -(-len(pending) // len(xs))
                sums = {}
                for x in xs:
                    tx = weights[0, X - x, x]
                    parts = {(c, y): scaled[c, first + y, x] * tx for c in range(channels) for y in range(ys)}
                    for j in range(j0, j0 + js):
                        tz = weights[2, j, x]
                        for at, part in parts.items():
                            sums[at + (j,)] = plus(sums.get(at + (j,)), part * tz)
                    flush(pace)
                flush(len(pending))
                pending.extend(at + (X, value) for at, value in sums.items())
        flush(len(pending))
        return carry

    lax.fori_loop(0, SHIFTS // ys, row, 0)


def settle(piles, out, rims, base=None, base_rims=None):
    channels, planes, rows, _ = out.shape
    lane = lane_of(rows)
    group = group_of(rows)
    for c in range(channels):
        rim = jnp.zeros((rows, LANES), F32)
        for X in range(planes):
            core = piles[c, LO, X]
            ends = jnp.zeros((rows, LANES), F32)
            for j in range(SHIFTS):
                d = j - LO
                if d == 0:
                    continue
                moved = pltpu.roll(piles[c, j, X], d % LANES, 1)
                wraps = lane >= LANES + d if d < 0 else lane < d
                core = core + jnp.where(wraps, 0.0, moved)
                ends = ends + jnp.where(wraps, moved, 0.0)
            out[c, X] = core if base is None else core + base[c, X]
            rim = jnp.where(group == X, pltpu.roll(ends, (8 * X) % LANES, 1), rim)
        rims[c] = rim if base_rims is None else rim + base_rims[c]


def pack_rim(extended):
    planes, rows, _ = extended.shape
    group = group_of(rows)
    rim = jnp.zeros((rows, LANES), F32)
    for X in range(planes):
        rim = jnp.where(group == X, pltpu.roll(extended[X], (8 * X) % LANES, 1), rim)
    return rim


def unpack_rim(rim, X):
    lane = lane_of(rim.shape[0])
    return jnp.where((lane < HI) | (lane >= LANES - LO), pltpu.roll(rim, (-8 * X) % LANES, 1), 0.0)


def fold_rows(message, ny):
    if ny == 2 * ROWS:
        return pltpu.roll(message, ROWS, 0)
    below, above = message[:ROWS], message[ROWS:]
    if ny == ROWS:
        return below + above
    return jnp.concatenate([above, jnp.zeros((ny - 2 * ROWS, LANES), F32), below], axis=0)


def put_edges(out, at, plane, ny):
    if ny == 2 * ROWS:
        out[at] = plane
    else:
        out[at, 0:ROWS] = plane[0:ROWS]
        out[at, ROWS : 2 * ROWS] = plane[ny - ROWS : ny]


def put_rims(out, at, plane, ny):
    out[at, 0:ROWS] = plane[0:ROWS]
    out[at, ROWS : 2 * ROWS] = plane[ROWS + ny : 2 * ROWS + ny]


def split_deposits(piled, outs, at, nx, ny):
    to_y, to_left, to_right, to_left_y, to_right_y, own = outs
    at_y, at_left, at_right, at_own = at
    planes = nx + LO + HI
    core = slice(ROWS, ROWS + ny)
    for i, X in enumerate(list(range(LO, LO + nx)) + [planes]):
        own[at_own + i] = piled[X, core]
        put_rims(to_y, at_y + i, piled[X], ny)
    for i, X in enumerate(list(range(LO)) + [planes]):
        to_left[at_left + i] = piled[X, core]
        put_rims(to_left_y, at_left + i, piled[X], ny)
    for i, X in enumerate(list(range(LO + nx, planes)) + [planes]):
        to_right[at_right + i] = piled[X, core]
        put_rims(to_right_y, at_right + i, piled[X], ny)


def join_deposits(ins, at, nx, ny, put):
    from_y, from_right, from_left, from_right_y, from_left_y, own = ins
    at_y, at_left, at_right, at_own = at

    def right(i):
        return from_right[at_left + i] + fold_rows(from_right_y[at_left + i], ny)

    def left(i):
        return from_left[at_right + i] + fold_rows(from_left_y[at_right + i], ny)

    for x in range(nx):
        plane = own[at_own + x] + fold_rows(from_y[at_y + x], ny)
        if x >= nx - LO:
            plane = plane + right(x - (nx - LO))
        if x < HI:
            plane = plane + left(x)
        put(x, plane)
    group = group_of(ny)
    rim = own[at_own + nx] + fold_rows(from_y[at_y + nx], ny)
    turn = 8 * nx
    high = pltpu.roll(right(LO), turn % LANES, 1)
    low = pltpu.roll(left(HI), (-turn) % LANES, 1)
    rim = rim + jnp.where((group >= nx) & (group < nx + LO), high, 0.0)
    return rim + jnp.where((group >= LO) & (group < LO + HI), low, 0.0)


def join_halo(field, ins, extended, nx, ny):
    from_y, from_right, from_left, from_right_y, from_left_y = ins

    def place(X, core, edges):
        extended[X, 0:ROWS] = edges[ROWS : 2 * ROWS]
        extended[X, ROWS : ROWS + ny] = core
        extended[X, ROWS + ny : 2 * ROWS + ny] = edges[0:ROWS]

    for x in range(nx):
        place(LO + x, field[x], from_y[x])
    for i in range(HI):
        place(LO + nx + i, from_right[i], from_right_y[i])
    for i in range(LO):
        place(i, from_left[i], from_left_y[i])


def split_halo(field, outs, nx, ny):
    to_y, to_left, to_right, to_left_y, to_right_y = outs
    for x in range(nx):
        put_edges(to_y, x, field[x], ny)
    for i in range(HI):
        to_left[i] = field[i]
        put_edges(to_left_y, i, field[i], ny)
    for i in range(LO):
        to_right[i] = field[nx - LO + i]
        put_edges(to_right_y, i, field[nx - LO + i], ny)


def first_kernel(
    nx, ny, intensity, cotangent, cells, fracs,
    to_y, to_l, to_r, to_ly, to_ry, own,
    cells_here, fracs_here, cotangent_here, image, sems, weights, scaled, piles, piled, rims,
):
    copies = [
        pltpu.make_async_copy(source, target, sems.at[i])
        for i, (source, target) in enumerate(
            (
                (cells.at[1, 1], cells_here),
                (fracs.at[1, 1], fracs_here),
                (cotangent, cotangent_here),
                (intensity, image),
            )
        )
    ]
    for copy in copies:
        copy.start()
    for copy in copies:
        copy.wait()
    write_tables(cells_here, fracs_here, weights)
    deposit(cotangent_here, weights, scaled, piles, 2, SHIFTS)
    settle(piles, piled.at[:, 0 : nx + LO + HI], rims)
    piled[0, nx + LO + HI] = rims[0]
    split_halo(image, (to_y, to_l, to_r, to_ly, to_ry), nx, ny)
    split_deposits(piled.at[0], (to_y, to_l, to_r, to_ly, to_ry, own), (nx, HI, LO, 0), nx, ny)


def first_join_kernel(nx, ny, intensity, from_y, from_r, from_l, from_ry, from_ly, own, extended, part, rims):
    rows = ny + 2 * ROWS
    join_halo(intensity, (from_y, from_r, from_l, from_ry, from_ly), extended, nx, ny)
    rims[0:rows] = pack_rim(extended)

    def put(x, plane):
        part[x] = plane

    rims[rows : rows + ny] = join_deposits((from_y, from_r, from_l, from_ry, from_ly, own), (nx, HI, LO, 0), nx, ny, put)


def middle_kernel(nx, ny, extended, rims_l, rims_r, part, cells, fracs, image, to_y, to_l, to_r, to_ly, to_ry, shifted, adjoint, weights):
    rows = ny + 2 * ROWS
    rim = jnp.where(low_lanes(rows), rims_r[0:rows], rims_l[0:rows])
    shift_planes(extended, rim, shifted)
    write_tables(cells.at[0, 1], fracs.at[0, 1], weights)

    def emit(x, sums):
        image[x] = sums[0]

    interpolate(shifted, weights, None, nx, ny, emit)
    split_halo(image, (to_y, to_l, to_r, to_ly, to_ry), nx, ny)
    back = jnp.where(low_lanes(ny), rims_l[rows : rows + ny], rims_r[rows : rows + ny])
    for x in range(nx):
        adjoint[0, x] = part[x] + unpack_rim(back, LO + x)


def early_kernel(nx, ny, shifted, adjoint, cells, fracs, grad, piled, rims, weights, slopes, scaled, piles):
    write_tables(cells.at[0, 1], fracs.at[0, 1], weights, slopes)

    def emit(x, sums):
        for c in range(3):
            grad[c, x] = adjoint[0, x] * sums[c]

    interpolate(shifted, weights, slopes, nx, ny, emit)
    deposit(adjoint, weights, scaled, piles, 2, SHIFTS)
    settle(piles, piled, rims)


def early_spread_kernel(nx, ny, grad, cells, fracs, piled, rims, weights, scaled, piles):
    write_tables(cells.at[0, 0], fracs.at[0, 0], weights)
    deposit(grad, weights, scaled, piles, 1, SHIFTS // 2)
    settle(piles, piled, rims)


def second_join_kernel(nx, ny, image, from_y, from_r, from_l, from_ry, from_ly, earlier, extended, rims):
    join_halo(image, (from_y, from_r, from_l, from_ry, from_ly), extended, nx, ny)
    rims[...] = pack_rim(extended)


def late_kernel(
    nx, ny, extended, rims_l, rims_r, cotangent, cells, fracs, early, early_rims, adjoint_rims,
    piled, rims,
    shifted, weights, slopes, grad, scaled, rims_here, piles,
):
    rows = ny + 2 * ROWS
    shift_planes(extended, jnp.where(low_lanes(rows), rims_r[...], rims_l[...]), shifted)
    write_tables(cells.at[1, 1], fracs.at[1, 1], weights, slopes)

    def emit(x, sums):
        for c in range(3):
            grad[c, x] = cotangent[0, x] * sums[c]

    interpolate(shifted, weights, slopes, nx, ny, emit)
    write_tables(cells.at[1, 0], fracs.at[1, 0], weights)
    deposit(grad, weights, scaled, piles, 1, SHIFTS // 2)
    settle(piles, piled, rims_here, early, early_rims)
    for c in range(3):
        rims[c * rows : (c + 1) * rows] = rims_here[c]
    rims[3 * rows : 4 * rows] = adjoint_rims[0]


def last_z_kernel(nx, ny, velocity, adjoint, rims_l, rims_r, to_y, to_l, to_r, to_ly, to_ry, own):
    rows = ny + 2 * ROWS
    low = low_lanes(rows)
    core = slice(ROWS, ROWS + ny)
    for c in range(4):
        here = slice(c * rows, (c + 1) * rows)
        back = jnp.where(low, rims_l[here], rims_r[here])
        for X in range(nx + LO + HI):
            plane = (velocity[c, X] if c < 3 else adjoint[0, X]) + unpack_rim(back, X)
            if X < LO:
                straight, corner, at = to_l, to_ly, c * LO + X
            elif X < LO + nx:
                straight, corner, at = own, to_y, c * nx + X - LO
            else:
                straight, corner, at = to_r, to_ry, c * HI + X - LO - nx
            straight[at] = plane[core]
            put_rims(corner, at, plane, ny)


def last_kernel(nx, ny, own, from_y, from_r, from_l, from_ry, from_ly, intensity_adjoint, velocity_adjoint):
    for c in range(4):
        for x in range(nx):
            at = c * nx + x
            plane = own[at] + fold_rows(from_y[at], ny)
            if x >= nx - LO:
                at = c * LO + x - (nx - LO)
                plane = plane + from_r[at] + fold_rows(from_ry[at], ny)
            if x < HI:
                at = c * HI + x
                plane = plane + from_l[at] + fold_rows(from_ly[at], ny)
            if c == 3:
                intensity_adjoint[x] = plane
            else:
                velocity_adjoint[c, x] = plane


def call(kernel, args, outs, scratch, flops, spaces=None, limit=24):
    def struct(shape):
        return jax.ShapeDtypeStruct(shape, F32)

    in_vmem = pl.BlockSpec(memory_space=pltpu.VMEM)
    in_specs = [in_vmem] * len(args)
    for i, space in (spaces or {}).items():
        in_specs[i] = pl.BlockSpec(memory_space=space)
    moved = 4 * sum(a.size for a in args)
    return pl.pallas_call(
        kernel,
        out_shape=[struct(s) for s in outs],
        in_specs=in_specs,
        out_specs=[in_vmem] * len(outs),
        scratch_shapes=[pltpu.VMEM(s, F32) if isinstance(s, tuple) else s for s in scratch],
        compiler_params=pltpu.CompilerParams(vmem_limit_bytes=limit * 1024 * 1024),
        cost_estimate=pl.CostEstimate(flops=flops, bytes_accessed=moved, transcendentals=0),
    )(*args)


def send(message, moves):
    axes = tuple(axis for axis, _ in moves)
    sizes = [lax.axis_size(axis) for axis in axes]
    if len(axes) == 1:
        pairs = [(i, (i + moves[0][1]) % sizes[0]) for i in range(sizes[0])]
        return lax.ppermute(message, axes[0], pairs)
    pairs = [
        (i * sizes[1] + j, (i + moves[0][1]) % sizes[0] * sizes[1] + (j + moves[1][1]) % sizes[1])
        for i in range(sizes[0])
        for j in range(sizes[1])
    ]
    return lax.ppermute(message, axes, pairs)


def send_y(message, *moves):
    if lax.axis_size("gy") == 2:
        return send(message, moves + (("gy", 1),))
    down = send(message[:, :ROWS], moves + (("gy", -1),))
    up = send(message[:, ROWS:], moves + (("gy", 1),))
    return jnp.concatenate([down, up], axis=1)


def send_sides(to_y, to_l, to_r, to_ly, to_ry):
    left, right = ("gx", -1), ("gx", 1)
    return (
        send_y(to_y),
        send(to_l, (left,)),
        send(to_r, (right,)),
        send_y(to_ly, left),
        send_y(to_ry, right),
    )


def send_z(rims):
    return send(rims, (("gz", 1),)), send(rims, (("gz", -1),))


FIRST_LIMIT = 56


def body(intensity, cotangent, cells, fracs):
    nx, ny, nz = intensity.shape
    rows = ny + 2 * ROWS
    planes = nx + LO + HI
    ring = 2 * ROWS
    field = (nx, ny, nz)
    table = (3, SHIFTS) + field
    cotangent = cotangent[None]
    unit = nx * ny * nz * 512

    def run(kernel, *rest, **more):
        return call(functools.partial(kernel, nx, ny), *rest, **more)

    def pile(channels):
        return [(channels, SHIFTS) + field, (channels, SHIFTS, planes, rows, nz)]

    def piled(channels):
        return [(channels, planes, rows, nz), (channels, rows, nz)]

    def messages(y, l, r):
        return [(y, ring, nz), (l, ny, nz), (r, ny, nz), (l, ring, nz), (r, ring, nz)]

    part = (3,) + field
    *outs, own = run(
        first_kernel,
        (intensity, cotangent, cells, fracs),
        messages(2 * nx + 1, HI + LO + 1, LO + HI + 1) + [(nx + 1, ny, nz)],
        [pltpu.VMEM(part, jnp.int32), part, (1,) + field, field, pltpu.SemaphoreType.DMA((4,)), table]
        + pile(1)
        + [(1, planes + 1, rows, nz), (1, rows, nz)],
        2 * unit,
        spaces=dict.fromkeys(range(4), pltpu.HBM),
        limit=FIRST_LIMIT,
    )
    extended, folded, rims = run(
        first_join_kernel,
        (intensity,) + send_sides(*outs) + (own,),
        [(planes, rows, nz), field, (rows + ny, nz)],
        [],
        unit // 16,
    )
    image, *outs, shifted, adjoint = run(
        middle_kernel,
        (extended,) + send_z(rims) + (folded, cells, fracs),
        [field] + messages(nx, HI, LO) + [(SHIFTS, planes, rows, nz), (1,) + field],
        [table],
        2 * unit,
    )

    sides = send_sides(*outs)
    grad, piled_adjoint, adjoint_rims = run(
        early_kernel,
        (shifted, adjoint, cells, fracs),
        [(3,) + field] + piled(1),
        [table, table] + pile(1),
        7 * unit,
    )
    extended, rims = run(
        second_join_kernel,
        (image,) + sides + (grad,),
        [(planes, rows, nz), (rows, nz)],
        [],
        unit // 16,
        spaces={6: pl.ANY},
    )
    rims_l, rims_r = send_z(rims)
    early, early_rims = run(
        early_spread_kernel,
        (grad, cells, fracs),
        piled(3),
        [table] + pile(3),
        6 * unit,
    )

    velocity, rims = run(
        late_kernel,
        (extended, rims_l, rims_r, cotangent, cells, fracs, early, early_rims, adjoint_rims),
        [(3, planes, rows, nz), (4 * rows, nz)],
        [(SHIFTS, planes, rows, nz), table, table, (3,) + field, pile(3)[0], (3, rows, nz), pile(3)[1]],
        11 * unit,
    )
    *outs, own = run(
        last_z_kernel,
        (velocity, piled_adjoint) + send_z(rims),
        messages(4 * nx, 4 * LO, 4 * HI) + [(4 * nx, ny, nz)],
        [],
        unit // 16,
    )
    return tuple(
        run(
            last_kernel,
            (own,) + send_sides(*outs),
            [field, (3,) + field],
            [],
            unit // 16,
        )
    )


def solution(mesh):
    in_specs = (
        P("gx", "gy", "gz"),
        P("gx", "gy", "gz"),
        P(None, None, None, "gx", "gy", "gz"),
        P(None, None, None, "gx", "gy", "gz"),
    )
    out_specs = (P("gx", "gy", "gz"), P(None, "gx", "gy", "gz"))
    return jax.shard_map(body, mesh=mesh, in_specs=in_specs, out_specs=out_specs, check_vma=False)
```

```python
import functools

import jax
import jax.numpy as jnp
from jax import lax
from jax.experimental import pallas as pl
from jax.experimental.pallas import tpu as pltpu
from jax.sharding import PartitionSpec as P

LO = 3
HI = 4
ROWS = 4
SHIFTS = 8
LANES = 128
F32 = jnp.float32


def lane_of(rows):
    return lax.broadcasted_iota(jnp.int32, (rows, LANES), 1)


def group_of(rows):
    return ((lane_of(rows) + LO) & (LANES - 1)) >> 3


def low_lanes(rows):
    return (lane_of(rows) & 7) < HI


def cubic_weights(t):
    t2 = t * t
    t3 = t2 * t
    return (
        0.5 * (2.0 * t2 - t3 - t),
        0.5 * (3.0 * t3 - 5.0 * t2 + 2.0),
        0.5 * (4.0 * t2 - 3.0 * t3 + t),
        0.5 * (t3 - t2),
    )


def cubic_slopes(t):
    t2 = t * t
    return (
        0.5 * (4.0 * t - 3.0 * t2 - 1.0),
        0.5 * (9.0 * t2 - 10.0 * t),
        0.5 * (8.0 * t - 9.0 * t2 + 1.0),
        0.5 * (3.0 * t2 - 2.0 * t),
    )


def write_tables(cells, fracs, weights, slopes=None):
    def plane(x, carry):
        for c in range(3):
            k = cells[c, x]
            t = fracs[c, x]
            hits = {s: k == s for s in range(-2, 3)}
            for ref, taps in ((weights, cubic_weights), (slopes, cubic_slopes)):
                if ref is None:
                    continue
                values = taps(t)
                for j in range(SHIFTS):
                    entry = jnp.zeros_like(t)
                    for a in range(4):
                        s = j - 3 - (a - 1)
                        if -2 <= s <= 2:
                            entry = jnp.where(hits[s], values[a], entry)
                    ref[c, j, x] = entry
        return carry

    lax.fori_loop(0, cells.shape[1], plane, 0)


def shift_planes(extended, rim, shifted):
    planes, rows, _ = extended.shape
    lane = lane_of(rows)
    for X in range(planes):
        core = extended[X]
        ends = pltpu.roll(rim, (-8 * X) % LANES, 1)
        for j in range(SHIFTS):
            d = j - LO
            if d == 0:
                shifted[j, X] = core
            else:
                wraps = lane >= LANES + d if d < 0 else lane < d
                shifted[j, X] = pltpu.roll(jnp.where(wraps, ends, core), (-d) % LANES, 1)


def interpolate(shifted, weights, slopes, nx, ny, emit, with_value):
    pair = 2 if nx % 2 == 0 else 1

    def plane(step, carry):
        x0 = step * pair
        tz = [[weights[2, j, x0 + p] for j in range(SHIFTS)] for p in range(pair)]
        sz = [[slopes[2, j, x0 + p] for j in range(SHIFTS)] for p in range(pair)]

        def row(sy, sums):
            a, b, c = [None] * pair, [None] * pair, [None] * pair
            for q in range(SHIFTS + pair - 1):
                window = [shifted[j, x0 + q, pl.ds(sy + 1, ny), :] for j in range(SHIFTS)]
                for p in range(pair):
                    sx = q - p
                    if not 0 <= sx < SHIFTS:
                        continue
                    x = x0 + p
                    column = total([tz[p][j] * window[j] for j in range(SHIFTS)])
                    tx = weights[0, sx, x]
                    a[p] = plus(a[p], tx * column)
                    b[p] = plus(b[p], slopes[0, sx, x] * column)
                    c[p] = plus(c[p], tx * total([sz[p][j] * window[j] for j in range(SHIFTS)]))
            out = []
            for p in range(pair):
                ty = weights[1, sy, x0 + p]
                terms = [ty * b[p], slopes[1, sy, x0 + p] * a[p], ty * c[p]]
                if with_value:
                    terms.append(ty * a[p])
                out.append(tuple(old + new for old, new in zip(sums[p], terms)))
            return tuple(out)

        zero = jnp.zeros((ny, LANES), F32)
        sums = lax.fori_loop(0, SHIFTS, row, ((zero,) * (4 if with_value else 3),) * pair)
        for p in range(pair):
            emit(x0 + p, sums[p])
        return carry

    lax.fori_loop(0, nx // pair, plane, 0)


def total(terms):
    while len(terms) > 1:
        terms = [terms[i] + terms[i + 1] for i in range(0, len(terms), 2)]
    return terms[0]


def plus(a, b):
    return b if a is None else a + b


def deposit(sources, weights, scaled, piles, ys, js, fresh=True):
    channels, nx, ny, _ = sources.shape
    planes = nx + LO + HI
    if fresh:
        piles[...] = jnp.zeros(piles.shape, F32)

    def scale(sy, carry):
        for x in range(nx):
            ty = weights[1, sy, x]
            for c in range(channels):
                scaled[c, sy, x] = sources[c, x] * ty
        return carry

    lax.fori_loop(0, SHIFTS, scale, 0)

    def row(step, carry):
        first = step * ys
        pending = []

        def flush(count):
            for _ in range(min(count, len(pending))):
                c, y, j, X, value = pending.pop(0)
                piles[c, j, X, pl.ds(first + y + 1, ny), :] += value

        for X in range(planes):
            xs = range(max(0, X - SHIFTS + 1), min(nx - 1, X) + 1)
            for j0 in range(0, SHIFTS, js):
                pace = -(-len(pending) // len(xs))
                sums = {}
                for x in xs:
                    tx = weights[0, X - x, x]
                    parts = {(c, y): scaled[c, first + y, x] * tx for c in range(channels) for y in range(ys)}
                    for j in range(j0, j0 + js):
                        tz = weights[2, j, x]
                        for at, part in parts.items():
                            sums[at + (j,)] = plus(sums.get(at + (j,)), part * tz)
                    flush(pace)
                flush(len(pending))
                pending.extend(at + (X, value) for at, value in sums.items())
        flush(len(pending))
        return carry

    lax.fori_loop(0, SHIFTS // ys, row, 0)


def settle(piles, out, rims):
    channels, planes, rows, _ = out.shape
    lane = lane_of(rows)
    group = group_of(rows)
    for c in range(channels):
        rim = jnp.zeros((rows, LANES), F32)
        for X in range(planes):
            core = piles[c, LO, X]
            ends = jnp.zeros((rows, LANES), F32)
            for j in range(SHIFTS):
                d = j - LO
                if d == 0:
                    continue
                moved = pltpu.roll(piles[c, j, X], d % LANES, 1)
                wraps = lane >= LANES + d if d < 0 else lane < d
                core = core + jnp.where(wraps, 0.0, moved)
                ends = ends + jnp.where(wraps, moved, 0.0)
            out[c, X] = core
            rim = jnp.where(group == X, pltpu.roll(ends, (8 * X) % LANES, 1), rim)
        rims[c] = rim


def pack_rim(extended):
    planes, rows, _ = extended.shape
    group = group_of(rows)
    rim = jnp.zeros((rows, LANES), F32)
    for X in range(planes):
        rim = jnp.where(group == X, pltpu.roll(extended[X], (8 * X) % LANES, 1), rim)
    return rim


def unpack_rim(rim, X):
    lane = lane_of(rim.shape[0])
    return jnp.where((lane < HI) | (lane >= LANES - LO), pltpu.roll(rim, (-8 * X) % LANES, 1), 0.0)


def fold_rows(message, ny):
    if ny == 2 * ROWS:
        return pltpu.roll(message, ROWS, 0)
    below, above = message[:ROWS], message[ROWS:]
    if ny == ROWS:
        return below + above
    return jnp.concatenate([above, jnp.zeros((ny - 2 * ROWS, LANES), F32), below], axis=0)


def put_edges(out, at, plane, ny):
    if ny == 2 * ROWS:
        out[at] = plane
    else:
        out[at, 0:ROWS] = plane[0:ROWS]
        out[at, ROWS : 2 * ROWS] = plane[ny - ROWS : ny]


def put_rims(out, at, plane, ny):
    out[at, 0:ROWS] = plane[0:ROWS]
    out[at, ROWS : 2 * ROWS] = plane[ROWS + ny : 2 * ROWS + ny]


def split_deposits(piled, outs, at, nx, ny):
    to_y, to_left, to_right, to_left_y, to_right_y, own = outs
    at_y, at_left, at_right, at_own = at
    planes = nx + LO + HI
    core = slice(ROWS, ROWS + ny)
    for i, X in enumerate(list(range(LO, LO + nx)) + [planes]):
        own[at_own + i] = piled[X, core]
        put_rims(to_y, at_y + i, piled[X], ny)
    for i, X in enumerate(list(range(LO)) + [planes]):
        to_left[at_left + i] = piled[X, core]
        put_rims(to_left_y, at_left + i, piled[X], ny)
    for i, X in enumerate(list(range(LO + nx, planes)) + [planes]):
        to_right[at_right + i] = piled[X, core]
        put_rims(to_right_y, at_right + i, piled[X], ny)


def join_deposits(ins, at, nx, ny, put):
    from_y, from_right, from_left, from_right_y, from_left_y, own = ins
    at_y, at_left, at_right, at_own = at

    def right(i):
        return from_right[at_left + i] + fold_rows(from_right_y[at_left + i], ny)

    def left(i):
        return from_left[at_right + i] + fold_rows(from_left_y[at_right + i], ny)

    for x in range(nx):
        plane = own[at_own + x] + fold_rows(from_y[at_y + x], ny)
        if x >= nx - LO:
            plane = plane + right(x - (nx - LO))
        if x < HI:
            plane = plane + left(x)
        put(x, plane)
    group = group_of(ny)
    rim = own[at_own + nx] + fold_rows(from_y[at_y + nx], ny)
    turn = 8 * nx
    high = pltpu.roll(right(LO), turn % LANES, 1)
    low = pltpu.roll(left(HI), (-turn) % LANES, 1)
    rim = rim + jnp.where((group >= nx) & (group < nx + LO), high, 0.0)
    return rim + jnp.where((group >= LO) & (group < LO + HI), low, 0.0)


def join_halo(field, ins, extended, nx, ny):
    from_y, from_right, from_left, from_right_y, from_left_y = ins

    def place(X, core, edges):
        extended[X, 0:ROWS] = edges[ROWS : 2 * ROWS]
        extended[X, ROWS : ROWS + ny] = core
        extended[X, ROWS + ny : 2 * ROWS + ny] = edges[0:ROWS]

    for x in range(nx):
        place(LO + x, field[x], from_y[x])
    for i in range(HI):
        place(LO + nx + i, from_right[i], from_right_y[i])
    for i in range(LO):
        place(i, from_left[i], from_left_y[i])


def split_halo(field, outs, nx, ny):
    to_y, to_left, to_right, to_left_y, to_right_y = outs
    for x in range(nx):
        put_edges(to_y, x, field[x], ny)
    for i in range(HI):
        to_left[i] = field[i]
        put_edges(to_left_y, i, field[i], ny)
    for i in range(LO):
        to_right[i] = field[nx - LO + i]
        put_edges(to_right_y, i, field[nx - LO + i], ny)


def first_kernel(
    nx, ny, intensity, cotangent, cells, fracs,
    to_y, to_l, to_r, to_ly, to_ry, own, image,
    cells_here, fracs_here, cotangent_here, sems, weights, scaled, piles, piled, rims,
):
    copies = [
        pltpu.make_async_copy(source, target, sems.at[i])
        for i, (source, target) in enumerate(
            (
                (cells.at[1, 1], cells_here),
                (fracs.at[1, 1], fracs_here),
                (cotangent, cotangent_here),
                (intensity, image),
            )
        )
    ]
    for copy in copies:
        copy.start()
    for copy in copies:
        copy.wait()
    write_tables(cells_here, fracs_here, weights)
    deposit(cotangent_here, weights, scaled, piles, 2, SHIFTS)
    settle(piles, piled.at[:, 0 : nx + LO + HI], rims)
    piled[0, nx + LO + HI] = rims[0]
    split_halo(image, (to_y, to_l, to_r, to_ly, to_ry), nx, ny)
    split_deposits(piled.at[0], (to_y, to_l, to_r, to_ly, to_ry, own), (nx, HI, LO, 0), nx, ny)


def first_join_kernel(nx, ny, intensity, from_y, from_r, from_l, from_ry, from_ly, own, extended, part, rims):
    rows = ny + 2 * ROWS
    join_halo(intensity, (from_y, from_r, from_l, from_ry, from_ly), extended, nx, ny)
    rims[0:rows] = pack_rim(extended)

    def put(x, plane):
        part[x] = plane

    rims[rows : rows + ny] = join_deposits((from_y, from_r, from_l, from_ry, from_ly, own), (nx, HI, LO, 0), nx, ny, put)


def middle_kernel(
    nx, ny, extended, rims_l, rims_r, part, cells, fracs,
    image, to_y, to_l, to_r, to_ly, to_ry, adjoint, gradient, weights,
    shifted, slopes,
):
    rows = ny + 2 * ROWS
    rim = jnp.where(low_lanes(rows), rims_r[0:rows], rims_l[0:rows])
    shift_planes(extended, rim, shifted)
    write_tables(cells.at[0, 1], fracs.at[0, 1], weights, slopes)

    def emit(x, sums):
        image[x] = sums[3]
        for c in range(3):
            gradient[c, x] = sums[c]

    interpolate(shifted, weights, slopes, nx, ny, emit, True)
    split_halo(image, (to_y, to_l, to_r, to_ly, to_ry), nx, ny)
    back = jnp.where(low_lanes(ny), rims_l[rows : rows + ny], rims_r[rows : rows + ny])
    for x in range(nx):
        adjoint[0, x] = part[x] + unpack_rim(back, LO + x)


def adjoint_kernel(nx, ny, adjoint, weights, piled, rims, scaled, piles):
    deposit(adjoint, weights, scaled, piles, 2, SHIFTS)
    settle(piles, piled, rims)


def early_kernel(nx, ny, gradient, adjoint, cells, fracs, piles, product, weights, scaled):
    write_tables(cells.at[0, 0], fracs.at[0, 0], weights)
    for c in range(3):
        for x in range(nx):
            product[c, x] = adjoint[0, x] * gradient[c, x]
    deposit(product, weights, scaled, piles, 1, SHIFTS // 2)


def second_join_kernel(nx, ny, image, from_y, from_r, from_l, from_ry, from_ly, earlier, extended, rims):
    join_halo(image, (from_y, from_r, from_l, from_ry, from_ly), extended, nx, ny)
    rims[...] = pack_rim(extended)


def late_kernel(
    nx, ny, extended, rims_l, rims_r, cotangent, cells, fracs, adjoint_rims, early_piles,
    piled, rims, piles,
    shifted, weights, slopes, product, scaled, rims_here,
):
    rows = ny + 2 * ROWS
    shift_planes(extended, jnp.where(low_lanes(rows), rims_r[...], rims_l[...]), shifted)
    write_tables(cells.at[1, 1], fracs.at[1, 1], weights, slopes)

    def emit(x, sums):
        for c in range(3):
            product[c, x] = cotangent[0, x] * sums[c]

    interpolate(shifted, weights, slopes, nx, ny, emit, False)
    write_tables(cells.at[1, 0], fracs.at[1, 0], weights)
    deposit(product, weights, scaled, piles, 1, SHIFTS // 2, fresh=False)
    settle(piles, piled, rims_here)
    for c in range(3):
        rims[c * rows : (c + 1) * rows] = rims_here[c]
    rims[3 * rows : 4 * rows] = adjoint_rims[0]


def last_z_kernel(nx, ny, velocity, adjoint, rims_l, rims_r, to_y, to_l, to_r, to_ly, to_ry, own):
    rows = ny + 2 * ROWS
    low = low_lanes(rows)
    core = slice(ROWS, ROWS + ny)
    for c in range(4):
        here = slice(c * rows, (c + 1) * rows)
        back = jnp.where(low, rims_l[here], rims_r[here])
        for X in range(nx + LO + HI):
            plane = (velocity[c, X] if c < 3 else adjoint[0, X]) + unpack_rim(back, X)
            if X < LO:
                straight, corner, at = to_l, to_ly, c * LO + X
            elif X < LO + nx:
                straight, corner, at = own, to_y, c * nx + X - LO
            else:
                straight, corner, at = to_r, to_ry, c * HI + X - LO - nx
            straight[at] = plane[core]
            put_rims(corner, at, plane, ny)


def last_kernel(nx, ny, own, from_y, from_r, from_l, from_ry, from_ly, intensity_adjoint, velocity_adjoint):
    for c in range(4):
        for x in range(nx):
            at = c * nx + x
            plane = own[at] + fold_rows(from_y[at], ny)
            if x >= nx - LO:
                at = c * LO + x - (nx - LO)
                plane = plane + from_r[at] + fold_rows(from_ry[at], ny)
            if x < HI:
                at = c * HI + x
                plane = plane + from_l[at] + fold_rows(from_ly[at], ny)
            if c == 3:
                intensity_adjoint[x] = plane
            else:
                velocity_adjoint[c, x] = plane


def call(kernel, args, outs, scratch, flops, spaces=None, limit=24 * 1024, aliases=None):
    def struct(shape):
        return jax.ShapeDtypeStruct(shape, F32)

    in_vmem = pl.BlockSpec(memory_space=pltpu.VMEM)
    in_specs = [in_vmem] * len(args)
    for i, space in (spaces or {}).items():
        in_specs[i] = pl.BlockSpec(memory_space=space)
    moved = 4 * sum(a.size for a in args)
    return pl.pallas_call(
        kernel,
        out_shape=[struct(s) for s in outs],
        in_specs=in_specs,
        out_specs=[in_vmem] * len(outs),
        scratch_shapes=[pltpu.VMEM(s, F32) if isinstance(s, tuple) else s for s in scratch],
        input_output_aliases=aliases or {},
        compiler_params=pltpu.CompilerParams(vmem_limit_bytes=limit * 1024),
        cost_estimate=pl.CostEstimate(flops=flops, bytes_accessed=moved, transcendentals=0),
    )(*args)


def send(message, moves):
    axes = tuple(axis for axis, _ in moves)
    sizes = [lax.axis_size(axis) for axis in axes]
    if len(axes) == 1:
        pairs = [(i, (i + moves[0][1]) % sizes[0]) for i in range(sizes[0])]
        return lax.ppermute(message, axes[0], pairs)
    pairs = [
        (i * sizes[1] + j, (i + moves[0][1]) % sizes[0] * sizes[1] + (j + moves[1][1]) % sizes[1])
        for i in range(sizes[0])
        for j in range(sizes[1])
    ]
    return lax.ppermute(message, axes, pairs)


def send_y(message, *moves):
    if lax.axis_size("gy") == 2:
        return send(message, moves + (("gy", 1),))
    down = send(message[:, :ROWS], moves + (("gy", -1),))
    up = send(message[:, ROWS:], moves + (("gy", 1),))
    return jnp.concatenate([down, up], axis=1)


def send_sides(to_y, to_l, to_r, to_ly, to_ry):
    left, right = ("gx", -1), ("gx", 1)
    return (
        send_y(to_y),
        send(to_l, (left,)),
        send(to_r, (right,)),
        send_y(to_ly, left),
        send_y(to_ry, right),
    )


def send_z(rims):
    return send(rims, (("gz", 1),)), send(rims, (("gz", -1),))


FIRST_LIMIT = 55150


def body(intensity, cotangent, cells, fracs):
    nx, ny, nz = intensity.shape
    rows = ny + 2 * ROWS
    planes = nx + LO + HI
    ring = 2 * ROWS
    field = (nx, ny, nz)
    table = (3, SHIFTS) + field
    cotangent = cotangent[None]
    unit = nx * ny * nz * 512

    def run(kernel, *rest, **more):
        return call(functools.partial(kernel, nx, ny), *rest, **more)

    def pile(channels):
        return [(channels, SHIFTS) + field, (channels, SHIFTS, planes, rows, nz)]

    def piled(channels):
        return [(channels, planes, rows, nz), (channels, rows, nz)]

    def messages(y, l, r):
        return [(y, ring, nz), (l, ny, nz), (r, ny, nz), (l, ring, nz), (r, ring, nz)]

    part = (3,) + field
    *outs, own, image = run(
        first_kernel,
        (intensity, cotangent, cells, fracs),
        messages(2 * nx + 1, HI + LO + 1, LO + HI + 1) + [(nx + 1, ny, nz), field],
        [pltpu.VMEM(part, jnp.int32), part, (1,) + field, pltpu.SemaphoreType.DMA((4,)), table]
        + pile(1)
        + [(1, planes + 1, rows, nz), (1, rows, nz)],
        2 * unit,
        spaces=dict.fromkeys(range(4), pltpu.HBM),
        limit=FIRST_LIMIT,
    )
    extended, folded, rims = run(
        first_join_kernel,
        (image,) + send_sides(*outs) + (own,),
        [(planes, rows, nz), field, (rows + ny, nz)],
        [],
        unit // 16,
    )
    image, *outs, adjoint, gradient, weights = run(
        middle_kernel,
        (extended,) + send_z(rims) + (folded, cells, fracs),
        [field] + messages(nx, HI, LO) + [(1,) + field, (3,) + field, table],
        [(SHIFTS, planes, rows, nz), table],
        5 * unit,
    )

    sides = send_sides(*outs)
    piled_adjoint, adjoint_rims = run(
        adjoint_kernel,
        (adjoint, weights),
        piled(1),
        pile(1),
        2 * unit,
    )
    extended, rims = run(
        second_join_kernel,
        (image,) + sides + (piled_adjoint,),
        [(planes, rows, nz), (rows, nz)],
        [],
        unit // 16,
        spaces={6: pl.ANY},
    )
    rims_l, rims_r = send_z(rims)
    scaled_3, piles_3 = pile(3)
    (piles,) = run(
        early_kernel,
        (gradient, adjoint, cells, fracs),
        [piles_3],
        [(3,) + field, table, scaled_3],
        6 * unit,
    )

    velocity, rims, _ = run(
        late_kernel,
        (extended, rims_l, rims_r, cotangent, cells, fracs, adjoint_rims, piles),
        [(3, planes, rows, nz), (4 * rows, nz), piles_3],
        [(SHIFTS, planes, rows, nz), table, table, (3,) + field, scaled_3, (3, rows, nz)],
        11 * unit,
        aliases={7: 2},
    )
    *outs, own = run(
        last_z_kernel,
        (velocity, piled_adjoint) + send_z(rims),
        messages(4 * nx, 4 * LO, 4 * HI) + [(4 * nx, ny, nz)],
        [],
        unit // 16,
    )
    return tuple(
        run(
            last_kernel,
            (own,) + send_sides(*outs),
            [field, (3,) + field],
            [],
            unit // 16,
        )
    )


def solution(mesh):
    in_specs = (
        P("gx", "gy", "gz"),
        P("gx", "gy", "gz"),
        P(None, None, None, "gx", "gy", "gz"),
        P(None, None, None, "gx", "gy", "gz"),
    )
    out_specs = (P("gx", "gy", "gz"), P(None, "gx", "gy", "gz"))
    return jax.shard_map(body, mesh=mesh, in_specs=in_specs, out_specs=out_specs, check_vma=False)
```

```python
import functools

import jax
import jax.numpy as jnp
from jax import lax
from jax.experimental import pallas as pl
from jax.experimental.pallas import tpu as pltpu
from jax.sharding import PartitionSpec as P

LO = 3
HI = 4
ROWS = 4
SHIFTS = 8
LANES = 128
BATCH = 5
F32 = jnp.float32


def lane_of(rows):
    return lax.broadcasted_iota(jnp.int32, (rows, LANES), 1)


def group_of(rows):
    return ((lane_of(rows) + LO) & (LANES - 1)) >> 3


def low_lanes(rows):
    return (lane_of(rows) & 7) < HI


def cubic_weights(t):
    t2 = t * t
    t3 = t2 * t
    return (
        0.5 * (2.0 * t2 - t3 - t),
        0.5 * (3.0 * t3 - 5.0 * t2 + 2.0),
        0.5 * (4.0 * t2 - 3.0 * t3 + t),
        0.5 * (t3 - t2),
    )


def cubic_slopes(t):
    t2 = t * t
    return (
        0.5 * (4.0 * t - 3.0 * t2 - 1.0),
        0.5 * (9.0 * t2 - 10.0 * t),
        0.5 * (8.0 * t - 9.0 * t2 + 1.0),
        0.5 * (3.0 * t2 - 2.0 * t),
    )


def write_tables(cells, fracs, weights, slopes=None):
    def plane(x, carry):
        entries = []
        for c in range(3):
            k = cells[c, x]
            t = fracs[c, x]
            hits = {s: k == s for s in range(-2, 3)}
            for ref, taps in ((weights, cubic_weights), (slopes, cubic_slopes)):
                if ref is None:
                    continue
                values = taps(t)
                for j in range(SHIFTS):
                    entry = jnp.zeros_like(t)
                    for a in range(4):
                        s = j - 3 - (a - 1)
                        if -2 <= s <= 2:
                            entry = jnp.where(hits[s], values[a], entry)
                    entries.append((ref, c, j, entry))
        for ref, c, j, entry in entries:
            ref[c, j, x] = entry
        return carry

    lax.fori_loop(0, cells.shape[1], plane, 0)


def shift_planes(extended, rim, shifted):
    planes, rows, _ = extended.shape
    lane = lane_of(rows)
    for first in range(0, planes, BATCH):
        batch = range(first, min(first + BATCH, planes))
        cores = {X: extended[X] for X in batch}
        moved = []
        for X in batch:
            ends = pltpu.roll(rim, (-8 * X) % LANES, 1)
            for j in range(SHIFTS):
                d = j - LO
                if d == 0:
                    moved.append((j, X, cores[X]))
                else:
                    wraps = lane >= LANES + d if d < 0 else lane < d
                    moved.append((j, X, pltpu.roll(jnp.where(wraps, ends, cores[X]), (-d) % LANES, 1)))
        for j, X, value in moved:
            shifted[j, X] = value


def interpolate(shifted, weights, slopes, nx, ny, emit, with_value):
    pair = 2 if nx % 2 == 0 else 1

    def plane(step, carry):
        x0 = step * pair
        tz = [[weights[2, j, x0 + p] for j in range(SHIFTS)] for p in range(pair)]
        sz = [[slopes[2, j, x0 + p] for j in range(SHIFTS)] for p in range(pair)]

        def row(sy, sums):
            a, b, c = [None] * pair, [None] * pair, [None] * pair
            for q in range(SHIFTS + pair - 1):
                window = [shifted[j, x0 + q, pl.ds(sy + 1, ny), :] for j in range(SHIFTS)]
                for p in range(pair):
                    sx = q - p
                    if not 0 <= sx < SHIFTS:
                        continue
                    x = x0 + p
                    column = total([tz[p][j] * window[j] for j in range(SHIFTS)])
                    tx = weights[0, sx, x]
                    a[p] = plus(a[p], tx * column)
                    b[p] = plus(b[p], slopes[0, sx, x] * column)
                    c[p] = plus(c[p], tx * total([sz[p][j] * window[j] for j in range(SHIFTS)]))
            out = []
            for p in range(pair):
                ty = weights[1, sy, x0 + p]
                terms = [ty * b[p], slopes[1, sy, x0 + p] * a[p], ty * c[p]]
                if with_value:
                    terms.append(ty * a[p])
                out.append(tuple(old + new for old, new in zip(sums[p], terms)))
            return tuple(out)

        zero = jnp.zeros((ny, LANES), F32)
        sums = lax.fori_loop(0, SHIFTS, row, ((zero,) * (4 if with_value else 3),) * pair)
        for p in range(pair):
            emit(x0 + p, sums[p])
        return carry

    lax.fori_loop(0, nx // pair, plane, 0)


def total(terms):
    while len(terms) > 1:
        odd = terms[len(terms) & ~1 :]
        terms = [terms[i] + terms[i + 1] for i in range(0, len(terms) - 1, 2)] + odd
    return terms[0]


def plus(a, b):
    return b if a is None else a + b


def deposit(sources, weights, scaled, piles, ys, js, fresh=True):
    channels, nx, ny, _ = sources.shape
    planes = nx + LO + HI
    if fresh:
        piles[...] = jnp.zeros(piles.shape, F32)

    def scale(sy, carry):
        tys = [weights[1, sy, x] for x in range(nx)]
        products = [(c, x, sources[c, x] * tys[x]) for c in range(channels) for x in range(nx)]
        for c, x, product in products:
            scaled[c, sy, x] = product
        return carry

    lax.fori_loop(0, SHIFTS, scale, 0)

    def row(step, carry):
        first = step * ys
        pending = []

        def flush(count):
            for _ in range(min(count, len(pending))):
                c, y, j, X, value = pending.pop(0)
                piles[c, j, X, pl.ds(first + y + 1, ny), :] += value

        for X in range(planes):
            xs = range(max(0, X - SHIFTS + 1), min(nx - 1, X) + 1)
            for j0 in range(0, SHIFTS, js):
                pace = -(-len(pending) // len(xs))
                sums = {}
                for x in xs:
                    tx = weights[0, X - x, x]
                    parts = {(c, y): scaled[c, first + y, x] * tx for c in range(channels) for y in range(ys)}
                    for j in range(j0, j0 + js):
                        tz = weights[2, j, x]
                        for at, part in parts.items():
                            sums[at + (j,)] = plus(sums.get(at + (j,)), part * tz)
                    flush(pace)
                flush(len(pending))
                pending.extend(at + (X, value) for at, value in sums.items())
        flush(len(pending))
        return carry

    lax.fori_loop(0, SHIFTS // ys, row, 0)


def settle(piles, out, rims):
    channels, planes, rows, _ = out.shape
    lane = lane_of(rows)
    group = group_of(rows)
    for c in range(channels):
        rim = jnp.zeros((rows, LANES), F32)
        for first in range(0, planes, BATCH):
            cores = []
            for X in range(first, min(first + BATCH, planes)):
                inside, ends = [piles[c, LO, X]], []
                for j in range(SHIFTS):
                    d = j - LO
                    if d == 0:
                        continue
                    moved = pltpu.roll(piles[c, j, X], d % LANES, 1)
                    wraps = lane >= LANES + d if d < 0 else lane < d
                    inside.append(jnp.where(wraps, 0.0, moved))
                    ends.append(jnp.where(wraps, moved, 0.0))
                cores.append((X, total(inside)))
                rim = jnp.where(group == X, pltpu.roll(total(ends), (8 * X) % LANES, 1), rim)
            for X, core in cores:
                out[c, X] = core
        rims[c] = rim


def pack_rim(extended):
    planes, rows, _ = extended.shape
    group = group_of(rows)
    rim = jnp.zeros((rows, LANES), F32)
    for X in range(planes):
        rim = jnp.where(group == X, pltpu.roll(extended[X], (8 * X) % LANES, 1), rim)
    return rim


def unpack_rim(rim, X):
    lane = lane_of(rim.shape[0])
    return jnp.where((lane < HI) | (lane >= LANES - LO), pltpu.roll(rim, (-8 * X) % LANES, 1), 0.0)


def fold_rows(message, ny):
    if ny == 2 * ROWS:
        return pltpu.roll(message, ROWS, 0)
    below, above = message[:ROWS], message[ROWS:]
    if ny == ROWS:
        return below + above
    return jnp.concatenate([above, jnp.zeros((ny - 2 * ROWS, LANES), F32), below], axis=0)


def put_edges(out, at, plane, ny):
    if ny == 2 * ROWS:
        out[at] = plane
    else:
        out[at, 0:ROWS] = plane[0:ROWS]
        out[at, ROWS : 2 * ROWS] = plane[ny - ROWS : ny]


def put_rims(out, at, plane, ny):
    out[at, 0:ROWS] = plane[0:ROWS]
    out[at, ROWS : 2 * ROWS] = plane[ROWS + ny : 2 * ROWS + ny]


def split_deposits(piled, outs, at, nx, ny):
    to_y, to_left, to_right, to_left_y, to_right_y, own = outs
    at_y, at_left, at_right, at_own = at
    planes = nx + LO + HI
    core = slice(ROWS, ROWS + ny)
    for i, X in enumerate(list(range(LO, LO + nx)) + [planes]):
        own[at_own + i] = piled[X, core]
        put_rims(to_y, at_y + i, piled[X], ny)
    for i, X in enumerate(list(range(LO)) + [planes]):
        to_left[at_left + i] = piled[X, core]
        put_rims(to_left_y, at_left + i, piled[X], ny)
    for i, X in enumerate(list(range(LO + nx, planes)) + [planes]):
        to_right[at_right + i] = piled[X, core]
        put_rims(to_right_y, at_right + i, piled[X], ny)


def join_deposits(ins, at, nx, ny, put):
    from_y, from_right, from_left, from_right_y, from_left_y, own = ins
    at_y, at_left, at_right, at_own = at

    def right(i):
        return from_right[at_left + i] + fold_rows(from_right_y[at_left + i], ny)

    def left(i):
        return from_left[at_right + i] + fold_rows(from_left_y[at_right + i], ny)

    for x in range(nx):
        plane = own[at_own + x] + fold_rows(from_y[at_y + x], ny)
        if x >= nx - LO:
            plane = plane + right(x - (nx - LO))
        if x < HI:
            plane = plane + left(x)
        put(x, plane)
    group = group_of(ny)
    rim = own[at_own + nx] + fold_rows(from_y[at_y + nx], ny)
    turn = 8 * nx
    high = pltpu.roll(right(LO), turn % LANES, 1)
    low = pltpu.roll(left(HI), (-turn) % LANES, 1)
    rim = rim + jnp.where((group >= nx) & (group < nx + LO), high, 0.0)
    return rim + jnp.where((group >= LO) & (group < LO + HI), low, 0.0)


def join_halo(field, ins, extended, nx, ny):
    from_y, from_right, from_left, from_right_y, from_left_y = ins

    def place(X, core, edges):
        extended[X, 0:ROWS] = edges[ROWS : 2 * ROWS]
        extended[X, ROWS : ROWS + ny] = core
        extended[X, ROWS + ny : 2 * ROWS + ny] = edges[0:ROWS]

    for x in range(nx):
        place(LO + x, field[x], from_y[x])
    for i in range(HI):
        place(LO + nx + i, from_right[i], from_right_y[i])
    for i in range(LO):
        place(i, from_left[i], from_left_y[i])


def split_halo(field, outs, nx, ny):
    to_y, to_left, to_right, to_left_y, to_right_y = outs
    for x in range(nx):
        put_edges(to_y, x, field[x], ny)
    for i in range(HI):
        to_left[i] = field[i]
        put_edges(to_left_y, i, field[i], ny)
    for i in range(LO):
        to_right[i] = field[nx - LO + i]
        put_edges(to_right_y, i, field[nx - LO + i], ny)


def first_kernel(
    nx, ny, intensity, cotangent, cells, fracs,
    to_y, to_l, to_r, to_ly, to_ry, own,
    cells_here, fracs_here, cotangent_here, image, sems, weights, scaled, piles, piled, rims,
):
    copies = [
        pltpu.make_async_copy(source, target, sems.at[i])
        for i, (source, target) in enumerate(
            (
                (cells.at[1, 1], cells_here),
                (fracs.at[1, 1], fracs_here),
                (cotangent, cotangent_here),
                (intensity, image),
            )
        )
    ]
    for copy in copies:
        copy.start()
    for copy in copies:
        copy.wait()
    write_tables(cells_here, fracs_here, weights)
    deposit(cotangent_here, weights, scaled, piles, 2, SHIFTS)
    settle(piles, piled.at[:, 0 : nx + LO + HI], rims)
    piled[0, nx + LO + HI] = rims[0]
    split_halo(image, (to_y, to_l, to_r, to_ly, to_ry), nx, ny)
    split_deposits(piled.at[0], (to_y, to_l, to_r, to_ly, to_ry, own), (nx, HI, LO, 0), nx, ny)


def first_join_kernel(nx, ny, intensity, from_y, from_r, from_l, from_ry, from_ly, own, extended, part, rims):
    rows = ny + 2 * ROWS
    join_halo(intensity, (from_y, from_r, from_l, from_ry, from_ly), extended, nx, ny)
    rims[0:rows] = pack_rim(extended)

    def put(x, plane):
        part[x] = plane

    rims[rows : rows + ny] = join_deposits((from_y, from_r, from_l, from_ry, from_ly, own), (nx, HI, LO, 0), nx, ny, put)


def middle_kernel(
    nx, ny, extended, rims_l, rims_r, part, cells, fracs,
    image, to_y, to_l, to_r, to_ly, to_ry, adjoint, gradient, weights,
    shifted, slopes,
):
    rows = ny + 2 * ROWS
    rim = jnp.where(low_lanes(rows), rims_r[0:rows], rims_l[0:rows])
    shift_planes(extended, rim, shifted)
    write_tables(cells.at[0, 1], fracs.at[0, 1], weights, slopes)

    def emit(x, sums):
        image[x] = sums[3]
        for c in range(3):
            gradient[c, x] = sums[c]

    interpolate(shifted, weights, slopes, nx, ny, emit, True)
    split_halo(image, (to_y, to_l, to_r, to_ly, to_ry), nx, ny)
    back = jnp.where(low_lanes(ny), rims_l[rows : rows + ny], rims_r[rows : rows + ny])
    for x in range(nx):
        adjoint[0, x] = part[x] + unpack_rim(back, LO + x)


def adjoint_kernel(nx, ny, adjoint, weights, piled, rims, scaled, piles):
    deposit(adjoint, weights, scaled, piles, 2, SHIFTS)
    settle(piles, piled, rims)


def early_kernel(nx, ny, gradient, adjoint, cells, fracs, piles, product, weights, scaled):
    write_tables(cells.at[0, 0], fracs.at[0, 0], weights)
    for c in range(3):
        for x in range(nx):
            product[c, x] = adjoint[0, x] * gradient[c, x]
    deposit(product, weights, scaled, piles, 1, SHIFTS // 2)


def second_join_kernel(nx, ny, image, from_y, from_r, from_l, from_ry, from_ly, earlier, extended, rims):
    join_halo(image, (from_y, from_r, from_l, from_ry, from_ly), extended, nx, ny)
    rims[...] = pack_rim(extended)


def late_kernel(
    nx, ny, extended, rims_l, rims_r, cotangent, cells, fracs, adjoint_rims, early_piles,
    piled, rims, piles,
    shifted, weights, slopes, product, scaled, rims_here,
):
    rows = ny + 2 * ROWS
    shift_planes(extended, jnp.where(low_lanes(rows), rims_r[...], rims_l[...]), shifted)
    write_tables(cells.at[1, 1], fracs.at[1, 1], weights, slopes)

    def emit(x, sums):
        for c in range(3):
            product[c, x] = cotangent[0, x] * sums[c]

    interpolate(shifted, weights, slopes, nx, ny, emit, False)
    write_tables(cells.at[1, 0], fracs.at[1, 0], weights)
    deposit(product, weights, scaled, piles, 1, SHIFTS // 2, fresh=False)
    settle(piles, piled, rims_here)
    for c in range(3):
        rims[c * rows : (c + 1) * rows] = rims_here[c]
    rims[3 * rows : 4 * rows] = adjoint_rims[0]


def last_z_kernel(nx, ny, velocity, adjoint, rims_l, rims_r, to_y, to_l, to_r, to_ly, to_ry, own):
    rows = ny + 2 * ROWS
    low = low_lanes(rows)
    core = slice(ROWS, ROWS + ny)
    for c in range(4):
        here = slice(c * rows, (c + 1) * rows)
        back = jnp.where(low, rims_l[here], rims_r[here])
        for X in range(nx + LO + HI):
            plane = (velocity[c, X] if c < 3 else adjoint[0, X]) + unpack_rim(back, X)
            if X < LO:
                straight, corner, at = to_l, to_ly, c * LO + X
            elif X < LO + nx:
                straight, corner, at = own, to_y, c * nx + X - LO
            else:
                straight, corner, at = to_r, to_ry, c * HI + X - LO - nx
            straight[at] = plane[core]
            put_rims(corner, at, plane, ny)


def last_kernel(nx, ny, own, from_y, from_r, from_l, from_ry, from_ly, intensity_adjoint, velocity_adjoint):
    for c in range(4):
        for x in range(nx):
            at = c * nx + x
            plane = own[at] + fold_rows(from_y[at], ny)
            if x >= nx - LO:
                at = c * LO + x - (nx - LO)
                plane = plane + from_r[at] + fold_rows(from_ry[at], ny)
            if x < HI:
                at = c * HI + x
                plane = plane + from_l[at] + fold_rows(from_ly[at], ny)
            if c == 3:
                intensity_adjoint[x] = plane
            else:
                velocity_adjoint[c, x] = plane


def call(kernel, args, outs, scratch, flops, spaces=None, limit=24 * 1024, aliases=None):
    def struct(shape):
        return jax.ShapeDtypeStruct(shape, F32)

    in_vmem = pl.BlockSpec(memory_space=pltpu.VMEM)
    in_specs = [in_vmem] * len(args)
    for i, space in (spaces or {}).items():
        in_specs[i] = pl.BlockSpec(memory_space=space)
    moved = 4 * sum(a.size for a in args)
    return pl.pallas_call(
        kernel,
        out_shape=[struct(s) for s in outs],
        in_specs=in_specs,
        out_specs=[in_vmem] * len(outs),
        scratch_shapes=[pltpu.VMEM(s, F32) if isinstance(s, tuple) else s for s in scratch],
        input_output_aliases=aliases or {},
        compiler_params=pltpu.CompilerParams(vmem_limit_bytes=limit * 1024),
        cost_estimate=pl.CostEstimate(flops=flops, bytes_accessed=moved, transcendentals=0),
    )(*args)


def send(message, moves):
    axes = tuple(axis for axis, _ in moves)
    sizes = [lax.axis_size(axis) for axis in axes]
    if len(axes) == 1:
        pairs = [(i, (i + moves[0][1]) % sizes[0]) for i in range(sizes[0])]
        return lax.ppermute(message, axes[0], pairs)
    pairs = [
        (i * sizes[1] + j, (i + moves[0][1]) % sizes[0] * sizes[1] + (j + moves[1][1]) % sizes[1])
        for i in range(sizes[0])
        for j in range(sizes[1])
    ]
    return lax.ppermute(message, axes, pairs)


def send_y(message, *moves):
    if lax.axis_size("gy") == 2:
        return send(message, moves + (("gy", 1),))
    down = send(message[:, :ROWS], moves + (("gy", -1),))
    up = send(message[:, ROWS:], moves + (("gy", 1),))
    return jnp.concatenate([down, up], axis=1)


def send_sides(to_y, to_l, to_r, to_ly, to_ry):
    left, right = ("gx", -1), ("gx", 1)
    return (
        send_y(to_y),
        send(to_l, (left,)),
        send(to_r, (right,)),
        send_y(to_ly, left),
        send_y(to_ry, right),
    )


def send_z(rims):
    return send(rims, (("gz", 1),)), send(rims, (("gz", -1),))


FIRST_LIMIT = 56 * 1024


def body(intensity, cotangent, cells, fracs):
    nx, ny, nz = intensity.shape
    rows = ny + 2 * ROWS
    planes = nx + LO + HI
    ring = 2 * ROWS
    field = (nx, ny, nz)
    table = (3, SHIFTS) + field
    cotangent = cotangent[None]
    unit = nx * ny * nz * 512

    def run(kernel, *rest, **more):
        return call(functools.partial(kernel, nx, ny), *rest, **more)

    def pile(channels):
        return [(channels, SHIFTS) + field, (channels, SHIFTS, planes, rows, nz)]

    def piled(channels):
        return [(channels, planes, rows, nz), (channels, rows, nz)]

    def messages(y, l, r):
        return [(y, ring, nz), (l, ny, nz), (r, ny, nz), (l, ring, nz), (r, ring, nz)]

    part = (3,) + field
    *outs, own = run(
        first_kernel,
        (intensity, cotangent, cells, fracs),
        messages(2 * nx + 1, HI + LO + 1, LO + HI + 1) + [(nx + 1, ny, nz)],
        [pltpu.VMEM(part, jnp.int32), part, (1,) + field, field, pltpu.SemaphoreType.DMA((4,)), table]
        + pile(1)
        + [(1, planes + 1, rows, nz), (1, rows, nz)],
        2 * unit,
        spaces=dict.fromkeys(range(4), pltpu.HBM),
        limit=FIRST_LIMIT,
    )
    extended, folded, rims = run(
        first_join_kernel,
        (intensity,) + send_sides(*outs) + (own,),
        [(planes, rows, nz), field, (rows + ny, nz)],
        [],
        unit // 16,
    )
    image, *outs, adjoint, gradient, weights = run(
        middle_kernel,
        (extended,) + send_z(rims) + (folded, cells, fracs),
        [field] + messages(nx, HI, LO) + [(1,) + field, (3,) + field, table],
        [(SHIFTS, planes, rows, nz), table],
        5 * unit,
    )

    sides = send_sides(*outs)
    piled_adjoint, adjoint_rims = run(
        adjoint_kernel,
        (adjoint, weights),
        piled(1),
        pile(1),
        2 * unit,
    )
    extended, rims = run(
        second_join_kernel,
        (image,) + sides + (piled_adjoint,),
        [(planes, rows, nz), (rows, nz)],
        [],
        unit // 16,
        spaces={6: pl.ANY},
    )
    rims_l, rims_r = send_z(rims)
    scaled_3, piles_3 = pile(3)
    (piles,) = run(
        early_kernel,
        (gradient, adjoint, cells, fracs),
        [piles_3],
        [(3,) + field, table, scaled_3],
        6 * unit,
    )

    velocity, rims, _ = run(
        late_kernel,
        (extended, rims_l, rims_r, cotangent, cells, fracs, adjoint_rims, piles),
        [(3, planes, rows, nz), (4 * rows, nz), piles_3],
        [(SHIFTS, planes, rows, nz), table, table, (3,) + field, scaled_3, (3, rows, nz)],
        11 * unit,
        aliases={7: 2},
    )
    *outs, own = run(
        last_z_kernel,
        (velocity, piled_adjoint) + send_z(rims),
        messages(4 * nx, 4 * LO, 4 * HI) + [(4 * nx, ny, nz)],
        [],
        unit // 16,
    )
    return tuple(
        run(
            last_kernel,
            (own,) + send_sides(*outs),
            [field, (3,) + field],
            [],
            unit // 16,
        )
    )


def solution(mesh):
    in_specs = (
        P("gx", "gy", "gz"),
        P("gx", "gy", "gz"),
        P(None, None, None, "gx", "gy", "gz"),
        P(None, None, None, "gx", "gy", "gz"),
    )
    out_specs = (P("gx", "gy", "gz"), P(None, "gx", "gy", "gz"))
    return jax.shard_map(body, mesh=mesh, in_specs=in_specs, out_specs=out_specs, check_vma=False)
```

```python
import functools

import jax
import jax.numpy as jnp
from jax import lax
from jax.experimental import pallas as pl
from jax.experimental.pallas import tpu as pltpu
from jax.sharding import PartitionSpec as P

LO = 3
HI = 4
ROWS = 4
SHIFTS = 8
LANES = 128
F32 = jnp.float32


def lane_of(rows):
    return lax.broadcasted_iota(jnp.int32, (rows, LANES), 1)


def group_of(rows):
    return ((lane_of(rows) + LO) & (LANES - 1)) >> 3


def low_lanes(rows):
    return (lane_of(rows) & 7) < HI


def cubic_weights(t):
    t2 = t * t
    t3 = t2 * t
    return (
        0.5 * (2.0 * t2 - t3 - t),
        0.5 * (3.0 * t3 - 5.0 * t2 + 2.0),
        0.5 * (4.0 * t2 - 3.0 * t3 + t),
        0.5 * (t3 - t2),
    )


def cubic_slopes(t):
    t2 = t * t
    return (
        0.5 * (4.0 * t - 3.0 * t2 - 1.0),
        0.5 * (9.0 * t2 - 10.0 * t),
        0.5 * (8.0 * t - 9.0 * t2 + 1.0),
        0.5 * (3.0 * t2 - 2.0 * t),
    )


def write_tables(cells, fracs, weights, slopes=None):
    def plane(x, carry):
        entries = []
        for c in range(3):
            k = cells[c, x]
            t = fracs[c, x]
            hits = {s: k == s for s in range(-2, 3)}
            for ref, taps in ((weights, cubic_weights), (slopes, cubic_slopes)):
                if ref is None:
                    continue
                values = taps(t)
                for j in range(SHIFTS):
                    entry = jnp.zeros_like(t)
                    for a in range(4):
                        s = j - 3 - (a - 1)
                        if -2 <= s <= 2:
                            entry = jnp.where(hits[s], values[a], entry)
                    entries.append((ref, c, j, entry))
        for ref, c, j, entry in entries:
            ref[c, j, x] = entry
        return carry

    lax.fori_loop(0, cells.shape[1], plane, 0)


def shift_planes(extended, rim, ends, shifted):
    planes, rows, _ = extended.shape
    lane = lane_of(rows)
    for X in range(planes):
        ends[X] = pltpu.roll(rim, (-8 * X) % LANES, 1)
    for X in range(planes):
        core, end = extended[X], ends[X]
        for j in range(SHIFTS):
            d = j - LO
            if d == 0:
                shifted[j, X] = core
            else:
                wraps = lane >= LANES + d if d < 0 else lane < d
                shifted[j, X] = pltpu.roll(jnp.where(wraps, end, core), (-d) % LANES, 1)


def interpolate(shifted, weights, slopes, nx, ny, emit, with_value):
    pair = 2 if nx % 2 == 0 else 1

    def plane(step, carry):
        x0 = step * pair
        tz = [[weights[2, j, x0 + p] for j in range(SHIFTS)] for p in range(pair)]
        sz = [[slopes[2, j, x0 + p] for j in range(SHIFTS)] for p in range(pair)]

        def row(sy, sums):
            a, b, c = [None] * pair, [None] * pair, [None] * pair
            for q in range(SHIFTS + pair - 1):
                window = [shifted[j, x0 + q, pl.ds(sy + 1, ny), :] for j in range(SHIFTS)]
                for p in range(pair):
                    sx = q - p
                    if not 0 <= sx < SHIFTS:
                        continue
                    x = x0 + p
                    column = total([tz[p][j] * window[j] for j in range(SHIFTS)])
                    tx = weights[0, sx, x]
                    a[p] = plus(a[p], tx * column)
                    b[p] = plus(b[p], slopes[0, sx, x] * column)
                    c[p] = plus(c[p], tx * total([sz[p][j] * window[j] for j in range(SHIFTS)]))
            out = []
            for p in range(pair):
                ty = weights[1, sy, x0 + p]
                terms = [ty * b[p], slopes[1, sy, x0 + p] * a[p], ty * c[p]]
                if with_value:
                    terms.append(ty * a[p])
                out.append(tuple(old + new for old, new in zip(sums[p], terms)))
            return tuple(out)

        zero = jnp.zeros((ny, LANES), F32)
        sums = lax.fori_loop(0, SHIFTS, row, ((zero,) * (4 if with_value else 3),) * pair)
        for p in range(pair):
            emit(x0 + p, sums[p])
        return carry

    lax.fori_loop(0, nx // pair, plane, 0)


def total(terms):
    while len(terms) > 1:
        odd = terms[len(terms) & ~1 :]
        terms = [terms[i] + terms[i + 1] for i in range(0, len(terms) - 1, 2)] + odd
    return terms[0]


def plus(a, b):
    return b if a is None else a + b


def deposit(sources, weights, scaled, piles, ys, js, fresh=True):
    channels, nx, ny, _ = sources.shape
    planes = nx + LO + HI
    if fresh:
        piles[...] = jnp.zeros(piles.shape, F32)

    def scale(sy, carry):
        tys = [weights[1, sy, x] for x in range(nx)]
        products = [(c, x, sources[c, x] * tys[x]) for c in range(channels) for x in range(nx)]
        for c, x, product in products:
            scaled[c, sy, x] = product
        return carry

    lax.fori_loop(0, SHIFTS, scale, 0)

    def row(step, carry):
        first = step * ys
        pending = []

        def flush(count):
            for _ in range(min(count, len(pending))):
                c, y, j, X, value = pending.pop(0)
                piles[c, j, X, pl.ds(first + y + 1, ny), :] += value

        for X in range(planes):
            xs = range(max(0, X - SHIFTS + 1), min(nx - 1, X) + 1)
            for j0 in range(0, SHIFTS, js):
                pace = -(-len(pending) // len(xs))
                sums = {}
                for x in xs:
                    tx = weights[0, X - x, x]
                    parts = {(c, y): scaled[c, first + y, x] * tx for c in range(channels) for y in range(ys)}
                    for j in range(j0, j0 + js):
                        tz = weights[2, j, x]
                        for at, part in parts.items():
                            sums[at + (j,)] = plus(sums.get(at + (j,)), part * tz)
                    flush(pace)
                flush(len(pending))
                pending.extend(at + (X, value) for at, value in sums.items())
        flush(len(pending))
        return carry

    lax.fori_loop(0, SHIFTS // ys, row, 0)


def settle(piles, ends, out, rims):
    channels, planes, rows, _ = out.shape
    lane = lane_of(rows)
    for c in range(channels):
        for X in range(planes):
            inside, outside = [piles[c, LO, X]], []
            for j in range(SHIFTS):
                d = j - LO
                if d == 0:
                    continue
                moved = pltpu.roll(piles[c, j, X], d % LANES, 1)
                wraps = lane >= LANES + d if d < 0 else lane < d
                inside.append(jnp.where(wraps, 0.0, moved))
                outside.append(jnp.where(wraps, moved, 0.0))
            out[c, X] = total(inside)
            ends[c, X] = total(outside)
    for c in range(channels):
        rims[c] = pack_rim(ends.at[c])


def pack_rim(extended):
    planes, rows, _ = extended.shape
    group = group_of(rows)
    rim = jnp.zeros((rows, LANES), F32)
    for X in range(planes):
        rim = jnp.where(group == X, pltpu.roll(extended[X], (8 * X) % LANES, 1), rim)
    return rim


def unpack_rim(rim, X):
    lane = lane_of(rim.shape[0])
    return jnp.where((lane < HI) | (lane >= LANES - LO), pltpu.roll(rim, (-8 * X) % LANES, 1), 0.0)


def fold_rows(message, ny):
    if ny == 2 * ROWS:
        return pltpu.roll(message, ROWS, 0)
    below, above = message[:ROWS], message[ROWS:]
    if ny == ROWS:
        return below + above
    return jnp.concatenate([above, jnp.zeros((ny - 2 * ROWS, LANES), F32), below], axis=0)


def put_edges(out, at, plane, ny):
    if ny == 2 * ROWS:
        out[at] = plane
    else:
        out[at, 0:ROWS] = plane[0:ROWS]
        out[at, ROWS : 2 * ROWS] = plane[ny - ROWS : ny]


def put_rims(out, at, plane, ny):
    out[at, 0:ROWS] = plane[0:ROWS]
    out[at, ROWS : 2 * ROWS] = plane[ROWS + ny : 2 * ROWS + ny]


def split_deposits(piled, outs, at, nx, ny):
    to_y, to_left, to_right, to_left_y, to_right_y, own = outs
    at_y, at_left, at_right, at_own = at
    planes = nx + LO + HI
    core = slice(ROWS, ROWS + ny)
    for i, X in enumerate(list(range(LO, LO + nx)) + [planes]):
        own[at_own + i] = piled[X, core]
        put_rims(to_y, at_y + i, piled[X], ny)
    for i, X in enumerate(list(range(LO)) + [planes]):
        to_left[at_left + i] = piled[X, core]
        put_rims(to_left_y, at_left + i, piled[X], ny)
    for i, X in enumerate(list(range(LO + nx, planes)) + [planes]):
        to_right[at_right + i] = piled[X, core]
        put_rims(to_right_y, at_right + i, piled[X], ny)


def join_deposits(ins, at, nx, ny, put):
    from_y, from_right, from_left, from_right_y, from_left_y, own = ins
    at_y, at_left, at_right, at_own = at

    def right(i):
        return from_right[at_left + i] + fold_rows(from_right_y[at_left + i], ny)

    def left(i):
        return from_left[at_right + i] + fold_rows(from_left_y[at_right + i], ny)

    for x in range(nx):
        plane = own[at_own + x] + fold_rows(from_y[at_y + x], ny)
        if x >= nx - LO:
            plane = plane + right(x - (nx - LO))
        if x < HI:
            plane = plane + left(x)
        put(x, plane)
    group = group_of(ny)
    rim = own[at_own + nx] + fold_rows(from_y[at_y + nx], ny)
    turn = 8 * nx
    high = pltpu.roll(right(LO), turn % LANES, 1)
    low = pltpu.roll(left(HI), (-turn) % LANES, 1)
    rim = rim + jnp.where((group >= nx) & (group < nx + LO), high, 0.0)
    return rim + jnp.where((group >= LO) & (group < LO + HI), low, 0.0)


def join_halo(field, ins, extended, nx, ny):
    from_y, from_right, from_left, from_right_y, from_left_y = ins

    def place(X, core, edges):
        extended[X, 0:ROWS] = edges[ROWS : 2 * ROWS]
        extended[X, ROWS : ROWS + ny] = core
        extended[X, ROWS + ny : 2 * ROWS + ny] = edges[0:ROWS]

    for x in range(nx):
        place(LO + x, field[x], from_y[x])
    for i in range(HI):
        place(LO + nx + i, from_right[i], from_right_y[i])
    for i in range(LO):
        place(i, from_left[i], from_left_y[i])


def split_halo(field, outs, nx, ny):
    to_y, to_left, to_right, to_left_y, to_right_y = outs
    for x in range(nx):
        put_edges(to_y, x, field[x], ny)
    for i in range(HI):
        to_left[i] = field[i]
        put_edges(to_left_y, i, field[i], ny)
    for i in range(LO):
        to_right[i] = field[nx - LO + i]
        put_edges(to_right_y, i, field[nx - LO + i], ny)


def first_kernel(
    nx, ny, intensity, cotangent, cells, fracs,
    to_y, to_l, to_r, to_ly, to_ry, own,
    weights, scaled, piles, ends, piled, rims,
):
    write_tables(cells.at[1, 1], fracs.at[1, 1], weights)
    deposit(cotangent, weights, scaled, piles, 2, SHIFTS)
    settle(piles, ends, piled.at[:, 0 : nx + LO + HI], rims)
    piled[0, nx + LO + HI] = rims[0]
    split_halo(intensity, (to_y, to_l, to_r, to_ly, to_ry), nx, ny)
    split_deposits(piled.at[0], (to_y, to_l, to_r, to_ly, to_ry, own), (nx, HI, LO, 0), nx, ny)


def first_join_kernel(nx, ny, intensity, from_y, from_r, from_l, from_ry, from_ly, own, extended, part, rims):
    rows = ny + 2 * ROWS
    join_halo(intensity, (from_y, from_r, from_l, from_ry, from_ly), extended, nx, ny)
    rims[0:rows] = pack_rim(extended)

    def put(x, plane):
        part[x] = plane

    rims[rows : rows + ny] = join_deposits((from_y, from_r, from_l, from_ry, from_ly, own), (nx, HI, LO, 0), nx, ny, put)


def middle_kernel(
    nx, ny, extended, rims_l, rims_r, part, cells, fracs,
    image, to_y, to_l, to_r, to_ly, to_ry, adjoint, gradient, weights,
    shifted, ends, slopes,
):
    rows = ny + 2 * ROWS
    rim = jnp.where(low_lanes(rows), rims_r[0:rows], rims_l[0:rows])
    shift_planes(extended, rim, ends, shifted)
    write_tables(cells.at[0, 1], fracs.at[0, 1], weights, slopes)

    def emit(x, sums):
        image[x] = sums[3]
        for c in range(3):
            gradient[c, x] = sums[c]

    interpolate(shifted, weights, slopes, nx, ny, emit, True)
    split_halo(image, (to_y, to_l, to_r, to_ly, to_ry), nx, ny)
    back = jnp.where(low_lanes(ny), rims_l[rows : rows + ny], rims_r[rows : rows + ny])
    for x in range(nx):
        adjoint[0, x] = part[x] + unpack_rim(back, LO + x)


def adjoint_kernel(nx, ny, adjoint, weights, piled, rims, scaled, piles, ends):
    deposit(adjoint, weights, scaled, piles, 2, SHIFTS)
    settle(piles, ends, piled, rims)


def early_kernel(nx, ny, gradient, adjoint, cells, fracs, piles, product, weights, scaled):
    write_tables(cells.at[0, 0], fracs.at[0, 0], weights)
    for c in range(3):
        for x in range(nx):
            product[c, x] = adjoint[0, x] * gradient[c, x]
    deposit(product, weights, scaled, piles, 1, SHIFTS // 2)


def second_join_kernel(nx, ny, image, from_y, from_r, from_l, from_ry, from_ly, earlier, extended, rims):
    join_halo(image, (from_y, from_r, from_l, from_ry, from_ly), extended, nx, ny)
    rims[...] = pack_rim(extended)


def late_kernel(
    nx, ny, extended, rims_l, rims_r, cotangent, cells, fracs, adjoint_rims, early_piles,
    piled, rims, piles,
    shifted, ends, weights, slopes, product, scaled, rims_here,
):
    rows = ny + 2 * ROWS
    shift_planes(extended, jnp.where(low_lanes(rows), rims_r[...], rims_l[...]), ends.at[0], shifted)
    write_tables(cells.at[1, 1], fracs.at[1, 1], weights, slopes)

    def emit(x, sums):
        for c in range(3):
            product[c, x] = cotangent[0, x] * sums[c]

    interpolate(shifted, weights, slopes, nx, ny, emit, False)
    write_tables(cells.at[1, 0], fracs.at[1, 0], weights)
    deposit(product, weights, scaled, piles, 1, SHIFTS // 2, fresh=False)
    settle(piles, ends, piled, rims_here)
    for c in range(3):
        rims[c * rows : (c + 1) * rows] = rims_here[c]
    rims[3 * rows : 4 * rows] = adjoint_rims[0]


def last_z_kernel(nx, ny, velocity, adjoint, rims_l, rims_r, to_y, to_l, to_r, to_ly, to_ry, own):
    rows = ny + 2 * ROWS
    low = low_lanes(rows)
    core = slice(ROWS, ROWS + ny)
    for c in range(4):
        here = slice(c * rows, (c + 1) * rows)
        back = jnp.where(low, rims_l[here], rims_r[here])
        for X in range(nx + LO + HI):
            plane = (velocity[c, X] if c < 3 else adjoint[0, X]) + unpack_rim(back, X)
            if X < LO:
                straight, corner, at = to_l, to_ly, c * LO + X
            elif X < LO + nx:
                straight, corner, at = own, to_y, c * nx + X - LO
            else:
                straight, corner, at = to_r, to_ry, c * HI + X - LO - nx
            straight[at] = plane[core]
            put_rims(corner, at, plane, ny)


def last_kernel(nx, ny, own, from_y, from_r, from_l, from_ry, from_ly, intensity_adjoint, velocity_adjoint):
    for c in range(4):
        for x in range(nx):
            at = c * nx + x
            plane = own[at] + fold_rows(from_y[at], ny)
            if x >= nx - LO:
                at = c * LO + x - (nx - LO)
                plane = plane + from_r[at] + fold_rows(from_ry[at], ny)
            if x < HI:
                at = c * HI + x
                plane = plane + from_l[at] + fold_rows(from_ly[at], ny)
            if c == 3:
                intensity_adjoint[x] = plane
            else:
                velocity_adjoint[c, x] = plane


def call(kernel, args, outs, scratch, flops, spaces=None, aliases=None):
    def struct(shape):
        return jax.ShapeDtypeStruct(shape, F32)

    in_vmem = pl.BlockSpec(memory_space=pltpu.VMEM)
    in_specs = [in_vmem] * len(args)
    for i, space in (spaces or {}).items():
        in_specs[i] = pl.BlockSpec(memory_space=space)
    moved = 4 * sum(a.size for a in args)
    return pl.pallas_call(
        kernel,
        out_shape=[struct(s) for s in outs],
        in_specs=in_specs,
        out_specs=[in_vmem] * len(outs),
        scratch_shapes=[pltpu.VMEM(s, F32) if isinstance(s, tuple) else s for s in scratch],
        input_output_aliases=aliases or {},
        compiler_params=pltpu.CompilerParams(vmem_limit_bytes=24 * 1024 * 1024),
        cost_estimate=pl.CostEstimate(flops=flops, bytes_accessed=moved, transcendentals=0),
    )(*args)


def send(message, moves):
    axes = tuple(axis for axis, _ in moves)
    sizes = [lax.axis_size(axis) for axis in axes]
    if len(axes) == 1:
        pairs = [(i, (i + moves[0][1]) % sizes[0]) for i in range(sizes[0])]
        return lax.ppermute(message, axes[0], pairs)
    pairs = [
        (i * sizes[1] + j, (i + moves[0][1]) % sizes[0] * sizes[1] + (j + moves[1][1]) % sizes[1])
        for i in range(sizes[0])
        for j in range(sizes[1])
    ]
    return lax.ppermute(message, axes, pairs)


def send_y(message, *moves):
    if lax.axis_size("gy") == 2:
        return send(message, moves + (("gy", 1),))
    down = send(message[:, :ROWS], moves + (("gy", -1),))
    up = send(message[:, ROWS:], moves + (("gy", 1),))
    return jnp.concatenate([down, up], axis=1)


def send_sides(to_y, to_l, to_r, to_ly, to_ry):
    left, right = ("gx", -1), ("gx", 1)
    return (
        send_y(to_y),
        send(to_l, (left,)),
        send(to_r, (right,)),
        send_y(to_ly, left),
        send_y(to_ry, right),
    )


def send_z(rims):
    return send(rims, (("gz", 1),)), send(rims, (("gz", -1),))


def body(intensity, cotangent, cells, fracs):
    nx, ny, nz = intensity.shape
    rows = ny + 2 * ROWS
    planes = nx + LO + HI
    ring = 2 * ROWS
    field = (nx, ny, nz)
    table = (3, SHIFTS) + field
    cotangent = cotangent[None]
    unit = nx * ny * nz * 512

    def run(kernel, *rest, **more):
        return call(functools.partial(kernel, nx, ny), *rest, **more)

    def pile(channels):
        return [(channels, SHIFTS) + field, (channels, SHIFTS, planes, rows, nz)]

    def piled(channels):
        return [(channels, planes, rows, nz), (channels, rows, nz)]

    def messages(y, l, r):
        return [(y, ring, nz), (l, ny, nz), (r, ny, nz), (l, ring, nz), (r, ring, nz)]

    *outs, own = run(
        first_kernel,
        (intensity, cotangent, cells, fracs),
        messages(2 * nx + 1, HI + LO + 1, LO + HI + 1) + [(nx + 1, ny, nz)],
        [table] + pile(1) + [(1, planes, rows, nz), (1, planes + 1, rows, nz), (1, rows, nz)],
        2 * unit,
    )
    extended, folded, rims = run(
        first_join_kernel,
        (intensity,) + send_sides(*outs) + (own,),
        [(planes, rows, nz), field, (rows + ny, nz)],
        [],
        unit // 16,
    )
    image, *outs, adjoint, gradient, weights = run(
        middle_kernel,
        (extended,) + send_z(rims) + (folded, cells, fracs),
        [field] + messages(nx, HI, LO) + [(1,) + field, (3,) + field, table],
        [(SHIFTS, planes, rows, nz), (planes, rows, nz), table],
        5 * unit,
    )

    sides = send_sides(*outs)
    piled_adjoint, adjoint_rims = run(
        adjoint_kernel,
        (adjoint, weights),
        piled(1),
        pile(1) + [(1, planes, rows, nz)],
        2 * unit,
    )
    extended, rims = run(
        second_join_kernel,
        (image,) + sides + (piled_adjoint,),
        [(planes, rows, nz), (rows, nz)],
        [],
        unit // 16,
        spaces={6: pl.ANY},
    )
    rims_l, rims_r = send_z(rims)
    scaled_3, piles_3 = pile(3)
    (piles,) = run(
        early_kernel,
        (gradient, adjoint, cells, fracs),
        [piles_3],
        [(3,) + field, table, scaled_3],
        6 * unit,
    )

    velocity, rims, _ = run(
        late_kernel,
        (extended, rims_l, rims_r, cotangent, cells, fracs, adjoint_rims, piles),
        [(3, planes, rows, nz), (4 * rows, nz), piles_3],
        [(SHIFTS, planes, rows, nz), (3, planes, rows, nz), table, table, (3,) + field, scaled_3, (3, rows, nz)],
        11 * unit,
        aliases={7: 2},
    )
    *outs, own = run(
        last_z_kernel,
        (velocity, piled_adjoint) + send_z(rims),
        messages(4 * nx, 4 * LO, 4 * HI) + [(4 * nx, ny, nz)],
        [],
        unit // 16,
    )
    return tuple(
        run(
            last_kernel,
            (own,) + send_sides(*outs),
            [field, (3,) + field],
            [],
            unit // 16,
        )
    )


def solution(mesh):
    in_specs = (
        P("gx", "gy", "gz"),
        P("gx", "gy", "gz"),
        P(None, None, None, "gx", "gy", "gz"),
        P(None, None, None, "gx", "gy", "gz"),
    )
    out_specs = (P("gx", "gy", "gz"), P(None, "gx", "gy", "gz"))
    return jax.shard_map(body, mesh=mesh, in_specs=in_specs, out_specs=out_specs, check_vma=False)
```

```python
import functools

import jax
import jax.numpy as jnp
from jax import lax
from jax.experimental import pallas as pl
from jax.experimental.pallas import tpu as pltpu
from jax.sharding import PartitionSpec as P

LO = 3
HI = 4
ROWS = 4
SHIFTS = 8
LANES = 128
F32 = jnp.float32


def lane_of(rows):
    return lax.broadcasted_iota(jnp.int32, (rows, LANES), 1)


def group_of(rows):
    return ((lane_of(rows) + LO) & (LANES - 1)) >> 3


def low_lanes(rows):
    return (lane_of(rows) & 7) < HI


def cubic_weights(t):
    t2 = t * t
    t3 = t2 * t
    return (
        0.5 * (2.0 * t2 - t3 - t),
        0.5 * (3.0 * t3 - 5.0 * t2 + 2.0),
        0.5 * (4.0 * t2 - 3.0 * t3 + t),
        0.5 * (t3 - t2),
    )


def cubic_slopes(t):
    t2 = t * t
    return (
        0.5 * (4.0 * t - 3.0 * t2 - 1.0),
        0.5 * (9.0 * t2 - 10.0 * t),
        0.5 * (8.0 * t - 9.0 * t2 + 1.0),
        0.5 * (3.0 * t2 - 2.0 * t),
    )


def write_tables(cells, fracs, weights=None, slopes=None):
    def plane(x, carry):
        entries = []
        for c in range(3):
            k = cells[c, x]
            t = fracs[c, x]
            hits = {s: k == s for s in range(-2, 3)}
            for ref, taps in ((weights, cubic_weights), (slopes, cubic_slopes)):
                if ref is None:
                    continue
                values = taps(t)
                for j in range(SHIFTS):
                    entry = jnp.zeros_like(t)
                    for a in range(4):
                        s = j - 3 - (a - 1)
                        if -2 <= s <= 2:
                            entry = jnp.where(hits[s], values[a], entry)
                    entries.append((ref, c, j, entry))
        for ref, c, j, entry in entries:
            ref[c, j, x] = entry
        return carry

    lax.fori_loop(0, cells.shape[1], plane, 0)


def shift_planes(extended, rim, ends, shifted):
    planes, rows, _ = extended.shape
    lane = lane_of(rows)
    for X in range(planes):
        ends[X] = pltpu.roll(rim, (-8 * X) % LANES, 1)
    for X in range(planes):
        core, end = extended[X], ends[X]
        for j in range(SHIFTS):
            d = j - LO
            if d == 0:
                shifted[j, X] = core
            else:
                wraps = lane >= LANES + d if d < 0 else lane < d
                shifted[j, X] = pltpu.roll(jnp.where(wraps, end, core), (-d) % LANES, 1)


def interpolate(shifted, weights, slopes, nx, ny, emit, with_value):
    pair = 2 if nx % 2 == 0 else 1

    def plane(step, carry):
        x0 = step * pair
        tz = [[weights[2, j, x0 + p] for j in range(SHIFTS)] for p in range(pair)]
        sz = [[slopes[2, j, x0 + p] for j in range(SHIFTS)] for p in range(pair)]

        def row(sy, sums):
            a, b, c = [None] * pair, [None] * pair, [None] * pair
            for q in range(SHIFTS + pair - 1):
                window = [shifted[j, x0 + q, pl.ds(sy + 1, ny), :] for j in range(SHIFTS)]
                for p in range(pair):
                    sx = q - p
                    if not 0 <= sx < SHIFTS:
                        continue
                    x = x0 + p
                    column = total([tz[p][j] * window[j] for j in range(SHIFTS)])
                    tx = weights[0, sx, x]
                    a[p] = plus(a[p], tx * column)
                    b[p] = plus(b[p], slopes[0, sx, x] * column)
                    c[p] = plus(c[p], tx * total([sz[p][j] * window[j] for j in range(SHIFTS)]))
            out = []
            for p in range(pair):
                ty = weights[1, sy, x0 + p]
                terms = [ty * b[p], slopes[1, sy, x0 + p] * a[p], ty * c[p]]
                if with_value:
                    terms.append(ty * a[p])
                out.append(tuple(old + new for old, new in zip(sums[p], terms)))
            return tuple(out)

        zero = jnp.zeros((ny, LANES), F32)
        sums = lax.fori_loop(0, SHIFTS, row, ((zero,) * (4 if with_value else 3),) * pair)
        for p in range(pair):
            emit(x0 + p, sums[p])
        return carry

    lax.fori_loop(0, nx // pair, plane, 0)


def total(terms):
    while len(terms) > 1:
        odd = terms[len(terms) & ~1 :]
        terms = [terms[i] + terms[i + 1] for i in range(0, len(terms) - 1, 2)] + odd
    return terms[0]


def plus(a, b):
    return b if a is None else a + b


def deposit(sources, weights, scaled, piles, ys, js, fresh=True):
    channels, nx, ny, _ = sources.shape
    planes = nx + LO + HI
    if fresh:
        piles[...] = jnp.zeros(piles.shape, F32)

    def scale(sy, carry):
        tys = [weights[1, sy, x] for x in range(nx)]
        products = [(c, x, sources[c, x] * tys[x]) for c in range(channels) for x in range(nx)]
        for c, x, product in products:
            scaled[c, sy, x] = product
        return carry

    lax.fori_loop(0, SHIFTS, scale, 0)

    def row(step, carry):
        first = step * ys
        pending = []

        def flush(count):
            for _ in range(min(count, len(pending))):
                c, y, j, X, value = pending.pop(0)
                piles[c, j, X, pl.ds(first + y + 1, ny), :] += value

        for X in range(planes):
            xs = range(max(0, X - SHIFTS + 1), min(nx - 1, X) + 1)
            for j0 in range(0, SHIFTS, js):
                pace = -(-len(pending) // len(xs))
                sums = {}
                for x in xs:
                    tx = weights[0, X - x, x]
                    parts = {(c, y): scaled[c, first + y, x] * tx for c in range(channels) for y in range(ys)}
                    for j in range(j0, j0 + js):
                        tz = weights[2, j, x]
                        for at, part in parts.items():
                            sums[at + (j,)] = plus(sums.get(at + (j,)), part * tz)
                    flush(pace)
                flush(len(pending))
                pending.extend(at + (X, value) for at, value in sums.items())
        flush(len(pending))
        return carry

    lax.fori_loop(0, SHIFTS // ys, row, 0)


def settle(piles, ends, out, rims):
    channels, planes, rows, _ = out.shape
    lane = lane_of(rows)
    for c in range(channels):
        for X in range(planes):
            inside, outside = [piles[c, LO, X]], []
            for j in range(SHIFTS):
                d = j - LO
                if d == 0:
                    continue
                moved = pltpu.roll(piles[c, j, X], d % LANES, 1)
                wraps = lane >= LANES + d if d < 0 else lane < d
                inside.append(jnp.where(wraps, 0.0, moved))
                outside.append(jnp.where(wraps, moved, 0.0))
            out[c, X] = total(inside)
            ends[c, X] = total(outside)
    for c in range(channels):
        rims[c] = pack_rim(ends.at[c])


def pack_rim(extended):
    planes, rows, _ = extended.shape
    group = group_of(rows)
    rim = jnp.zeros((rows, LANES), F32)
    for X in range(planes):
        rim = jnp.where(group == X, pltpu.roll(extended[X], (8 * X) % LANES, 1), rim)
    return rim


def unpack_rim(rim, X):
    lane = lane_of(rim.shape[0])
    return jnp.where((lane < HI) | (lane >= LANES - LO), pltpu.roll(rim, (-8 * X) % LANES, 1), 0.0)


def fold_rows(message, ny):
    if ny == 2 * ROWS:
        return pltpu.roll(message, ROWS, 0)
    below, above = message[:ROWS], message[ROWS:]
    if ny == ROWS:
        return below + above
    return jnp.concatenate([above, jnp.zeros((ny - 2 * ROWS, LANES), F32), below], axis=0)


def put_edges(out, at, plane, ny):
    if ny == 2 * ROWS:
        out[at] = plane
    else:
        out[at, 0:ROWS] = plane[0:ROWS]
        out[at, ROWS : 2 * ROWS] = plane[ny - ROWS : ny]


def put_rims(out, at, plane, ny):
    out[at, 0:ROWS] = plane[0:ROWS]
    out[at, ROWS : 2 * ROWS] = plane[ROWS + ny : 2 * ROWS + ny]


def split_deposits(piled, outs, at, nx, ny):
    to_y, to_left, to_right, to_left_y, to_right_y, own = outs
    at_y, at_left, at_right, at_own = at
    planes = nx + LO + HI
    core = slice(ROWS, ROWS + ny)
    for i, X in enumerate(list(range(LO, LO + nx)) + [planes]):
        own[at_own + i] = piled[X, core]
        put_rims(to_y, at_y + i, piled[X], ny)
    for i, X in enumerate(list(range(LO)) + [planes]):
        to_left[at_left + i] = piled[X, core]
        put_rims(to_left_y, at_left + i, piled[X], ny)
    for i, X in enumerate(list(range(LO + nx, planes)) + [planes]):
        to_right[at_right + i] = piled[X, core]
        put_rims(to_right_y, at_right + i, piled[X], ny)


def join_deposits(ins, at, nx, ny, put):
    from_y, from_right, from_left, from_right_y, from_left_y, own = ins
    at_y, at_left, at_right, at_own = at

    def right(i):
        return from_right[at_left + i] + fold_rows(from_right_y[at_left + i], ny)

    def left(i):
        return from_left[at_right + i] + fold_rows(from_left_y[at_right + i], ny)

    for x in range(nx):
        plane = own[at_own + x] + fold_rows(from_y[at_y + x], ny)
        if x >= nx - LO:
            plane = plane + right(x - (nx - LO))
        if x < HI:
            plane = plane + left(x)
        put(x, plane)
    group = group_of(ny)
    rim = own[at_own + nx] + fold_rows(from_y[at_y + nx], ny)
    turn = 8 * nx
    high = pltpu.roll(right(LO), turn % LANES, 1)
    low = pltpu.roll(left(HI), (-turn) % LANES, 1)
    rim = rim + jnp.where((group >= nx) & (group < nx + LO), high, 0.0)
    return rim + jnp.where((group >= LO) & (group < LO + HI), low, 0.0)


def join_halo(field, ins, extended, nx, ny):
    from_y, from_right, from_left, from_right_y, from_left_y = ins

    def place(X, core, edges):
        extended[X, 0:ROWS] = edges[ROWS : 2 * ROWS]
        extended[X, ROWS : ROWS + ny] = core
        extended[X, ROWS + ny : 2 * ROWS + ny] = edges[0:ROWS]

    for x in range(nx):
        place(LO + x, field[x], from_y[x])
    for i in range(HI):
        place(LO + nx + i, from_right[i], from_right_y[i])
    for i in range(LO):
        place(i, from_left[i], from_left_y[i])


def split_halo(field, outs, nx, ny):
    to_y, to_left, to_right, to_left_y, to_right_y = outs
    for x in range(nx):
        put_edges(to_y, x, field[x], ny)
    for i in range(HI):
        to_left[i] = field[i]
        put_edges(to_left_y, i, field[i], ny)
    for i in range(LO):
        to_right[i] = field[nx - LO + i]
        put_edges(to_right_y, i, field[nx - LO + i], ny)


def table_kernel(nx, ny, cells, fracs, late, early, early_slopes):
    write_tables(cells.at[1, 1], fracs.at[1, 1], late)
    write_tables(cells.at[0, 1], fracs.at[0, 1], early, early_slopes)


def first_kernel(
    nx, ny, intensity, cotangent, weights,
    to_y, to_l, to_r, to_ly, to_ry, own,
    scaled, piles, ends, piled, rims,
):
    deposit(cotangent, weights, scaled, piles, 2, SHIFTS)
    settle(piles, ends, piled.at[:, 0 : nx + LO + HI], rims)
    piled[0, nx + LO + HI] = rims[0]
    split_halo(intensity, (to_y, to_l, to_r, to_ly, to_ry), nx, ny)
    split_deposits(piled.at[0], (to_y, to_l, to_r, to_ly, to_ry, own), (nx, HI, LO, 0), nx, ny)


def first_join_kernel(nx, ny, intensity, from_y, from_r, from_l, from_ry, from_ly, own, extended, part, rims):
    rows = ny + 2 * ROWS
    join_halo(intensity, (from_y, from_r, from_l, from_ry, from_ly), extended, nx, ny)
    rims[0:rows] = pack_rim(extended)

    def put(x, plane):
        part[x] = plane

    rims[rows : rows + ny] = join_deposits((from_y, from_r, from_l, from_ry, from_ly, own), (nx, HI, LO, 0), nx, ny, put)


def middle_kernel(
    nx, ny, extended, rims_l, rims_r, part, weights, slopes,
    image, to_y, to_l, to_r, to_ly, to_ry, adjoint, gradient,
    shifted, ends,
):
    rows = ny + 2 * ROWS
    rim = jnp.where(low_lanes(rows), rims_r[0:rows], rims_l[0:rows])
    shift_planes(extended, rim, ends, shifted)

    def emit(x, sums):
        image[x] = sums[3]
        for c in range(3):
            gradient[c, x] = sums[c]

    interpolate(shifted, weights, slopes, nx, ny, emit, True)
    split_halo(image, (to_y, to_l, to_r, to_ly, to_ry), nx, ny)
    back = jnp.where(low_lanes(ny), rims_l[rows : rows + ny], rims_r[rows : rows + ny])
    for x in range(nx):
        adjoint[0, x] = part[x] + unpack_rim(back, LO + x)


def adjoint_kernel(
    nx, ny, adjoint, weights, cells, fracs,
    piled, rims, early_mid, late_slopes, late_mid,
    scaled, piles, ends,
):
    deposit(adjoint, weights, scaled, piles, 2, SHIFTS)
    settle(piles, ends, piled, rims)
    write_tables(cells.at[0, 0], fracs.at[0, 0], early_mid)
    write_tables(cells.at[1, 1], fracs.at[1, 1], None, late_slopes)
    write_tables(cells.at[1, 0], fracs.at[1, 0], late_mid)


def early_kernel(nx, ny, gradient, adjoint, weights, piles, product, scaled):
    for c in range(3):
        for x in range(nx):
            product[c, x] = adjoint[0, x] * gradient[c, x]
    deposit(product, weights, scaled, piles, 1, SHIFTS // 2)


def second_join_kernel(nx, ny, image, from_y, from_r, from_l, from_ry, from_ly, earlier, extended, rims):
    join_halo(image, (from_y, from_r, from_l, from_ry, from_ly), extended, nx, ny)
    rims[...] = pack_rim(extended)


def late_kernel(
    nx, ny, extended, rims_l, rims_r, cotangent, weights, slopes, mid_weights, adjoint_rims, early_piles,
    piled, rims, piles,
    shifted, ends, product, scaled, rims_here,
):
    rows = ny + 2 * ROWS
    shift_planes(extended, jnp.where(low_lanes(rows), rims_r[...], rims_l[...]), ends.at[0], shifted)

    def emit(x, sums):
        for c in range(3):
            product[c, x] = cotangent[0, x] * sums[c]

    interpolate(shifted, weights, slopes, nx, ny, emit, False)
    deposit(product, mid_weights, scaled, piles, 1, SHIFTS // 2, fresh=False)
    settle(piles, ends, piled, rims_here)
    for c in range(3):
        rims[c * rows : (c + 1) * rows] = rims_here[c]
    rims[3 * rows : 4 * rows] = adjoint_rims[0]


def last_z_kernel(nx, ny, velocity, adjoint, rims_l, rims_r, to_y, to_l, to_r, to_ly, to_ry, own):
    rows = ny + 2 * ROWS
    low = low_lanes(rows)
    core = slice(ROWS, ROWS + ny)
    for c in range(4):
        here = slice(c * rows, (c + 1) * rows)
        back = jnp.where(low, rims_l[here], rims_r[here])
        for X in range(nx + LO + HI):
            plane = (velocity[c, X] if c < 3 else adjoint[0, X]) + unpack_rim(back, X)
            if X < LO:
                straight, corner, at = to_l, to_ly, c * LO + X
            elif X < LO + nx:
                straight, corner, at = own, to_y, c * nx + X - LO
            else:
                straight, corner, at = to_r, to_ry, c * HI + X - LO - nx
            straight[at] = plane[core]
            put_rims(corner, at, plane, ny)


def last_kernel(nx, ny, own, from_y, from_r, from_l, from_ry, from_ly, intensity_adjoint, velocity_adjoint):
    for c in range(4):
        for x in range(nx):
            at = c * nx + x
            plane = own[at] + fold_rows(from_y[at], ny)
            if x >= nx - LO:
                at = c * LO + x - (nx - LO)
                plane = plane + from_r[at] + fold_rows(from_ry[at], ny)
            if x < HI:
                at = c * HI + x
                plane = plane + from_l[at] + fold_rows(from_ly[at], ny)
            if c == 3:
                intensity_adjoint[x] = plane
            else:
                velocity_adjoint[c, x] = plane


def call(kernel, args, outs, scratch, flops, spaces=None, aliases=None):
    def struct(shape):
        return jax.ShapeDtypeStruct(shape, F32)

    in_vmem = pl.BlockSpec(memory_space=pltpu.VMEM)
    in_specs = [in_vmem] * len(args)
    for i, space in (spaces or {}).items():
        in_specs[i] = pl.BlockSpec(memory_space=space)
    moved = 4 * sum(a.size for a in args)
    return pl.pallas_call(
        kernel,
        out_shape=[struct(s) for s in outs],
        in_specs=in_specs,
        out_specs=[in_vmem] * len(outs),
        scratch_shapes=[pltpu.VMEM(s, F32) if isinstance(s, tuple) else s for s in scratch],
        input_output_aliases=aliases or {},
        compiler_params=pltpu.CompilerParams(vmem_limit_bytes=24 * 1024 * 1024),
        cost_estimate=pl.CostEstimate(flops=flops, bytes_accessed=moved, transcendentals=0),
    )(*args)


def send(message, moves):
    axes = tuple(axis for axis, _ in moves)
    sizes = [lax.axis_size(axis) for axis in axes]
    if len(axes) == 1:
        pairs = [(i, (i + moves[0][1]) % sizes[0]) for i in range(sizes[0])]
        return lax.ppermute(message, axes[0], pairs)
    pairs = [
        (i * sizes[1] + j, (i + moves[0][1]) % sizes[0] * sizes[1] + (j + moves[1][1]) % sizes[1])
        for i in range(sizes[0])
        for j in range(sizes[1])
    ]
    return lax.ppermute(message, axes, pairs)


def send_y(message, *moves):
    if lax.axis_size("gy") == 2:
        return send(message, moves + (("gy", 1),))
    down = send(message[:, :ROWS], moves + (("gy", -1),))
    up = send(message[:, ROWS:], moves + (("gy", 1),))
    return jnp.concatenate([down, up], axis=1)


def send_sides(to_y, to_l, to_r, to_ly, to_ry):
    left, right = ("gx", -1), ("gx", 1)
    return (
        send_y(to_y),
        send(to_l, (left,)),
        send(to_r, (right,)),
        send_y(to_ly, left),
        send_y(to_ry, right),
    )


def send_z(rims):
    return send(rims, (("gz", 1),)), send(rims, (("gz", -1),))


def body(intensity, cotangent, cells, fracs):
    nx, ny, nz = intensity.shape
    rows = ny + 2 * ROWS
    planes = nx + LO + HI
    ring = 2 * ROWS
    field = (nx, ny, nz)
    table = (3, SHIFTS) + field
    cotangent = cotangent[None]
    unit = nx * ny * nz * 512

    def run(kernel, *rest, **more):
        return call(functools.partial(kernel, nx, ny), *rest, **more)

    def pile(channels):
        return [(channels, SHIFTS) + field, (channels, SHIFTS, planes, rows, nz)]

    def piled(channels):
        return [(channels, planes, rows, nz), (channels, rows, nz)]

    def messages(y, l, r):
        return [(y, ring, nz), (l, ny, nz), (r, ny, nz), (l, ring, nz), (r, ring, nz)]

    late, early, early_slopes = run(
        table_kernel,
        (cells, fracs),
        [table, table, table],
        [],
        unit // 16,
    )
    *outs, own = run(
        first_kernel,
        (intensity, cotangent, late),
        messages(2 * nx + 1, HI + LO + 1, LO + HI + 1) + [(nx + 1, ny, nz)],
        pile(1) + [(1, planes, rows, nz), (1, planes + 1, rows, nz), (1, rows, nz)],
        2 * unit,
    )
    extended, folded, rims = run(
        first_join_kernel,
        (intensity,) + send_sides(*outs) + (own,),
        [(planes, rows, nz), field, (rows + ny, nz)],
        [],
        unit // 16,
    )
    image, *outs, adjoint, gradient = run(
        middle_kernel,
        (extended,) + send_z(rims) + (folded, early, early_slopes),
        [field] + messages(nx, HI, LO) + [(1,) + field, (3,) + field],
        [(SHIFTS, planes, rows, nz), (planes, rows, nz)],
        5 * unit,
    )

    sides = send_sides(*outs)
    piled_adjoint, adjoint_rims, early_mid, late_slopes, late_mid = run(
        adjoint_kernel,
        (adjoint, early, cells, fracs),
        piled(1) + [table, table, table],
        pile(1) + [(1, planes, rows, nz)],
        2 * unit,
    )
    extended, rims = run(
        second_join_kernel,
        (image,) + sides + (piled_adjoint,),
        [(planes, rows, nz), (rows, nz)],
        [],
        unit // 16,
        spaces={6: pl.ANY},
    )
    rims_l, rims_r = send_z(rims)
    scaled_3, piles_3 = pile(3)
    (piles,) = run(
        early_kernel,
        (gradient, adjoint, early_mid),
        [piles_3],
        [(3,) + field, scaled_3],
        6 * unit,
    )

    velocity, rims, _ = run(
        late_kernel,
        (extended, rims_l, rims_r, cotangent, late, late_slopes, late_mid, adjoint_rims, piles),
        [(3, planes, rows, nz), (4 * rows, nz), piles_3],
        [(SHIFTS, planes, rows, nz), (3, planes, rows, nz), (3,) + field, scaled_3, (3, rows, nz)],
        11 * unit,
        aliases={8: 2},
    )
    *outs, own = run(
        last_z_kernel,
        (velocity, piled_adjoint) + send_z(rims),
        messages(4 * nx, 4 * LO, 4 * HI) + [(4 * nx, ny, nz)],
        [],
        unit // 16,
    )
    return tuple(
        run(
            last_kernel,
            (own,) + send_sides(*outs),
            [field, (3,) + field],
            [],
            unit // 16,
        )
    )


def solution(mesh):
    in_specs = (
        P("gx", "gy", "gz"),
        P("gx", "gy", "gz"),
        P(None, None, None, "gx", "gy", "gz"),
        P(None, None, None, "gx", "gy", "gz"),
    )
    out_specs = (P("gx", "gy", "gz"), P(None, "gx", "gy", "gz"))
    return jax.shard_map(body, mesh=mesh, in_specs=in_specs, out_specs=out_specs, check_vma=False)
```

```python
import functools

import jax
import jax.numpy as jnp
from jax import lax
from jax.experimental import pallas as pl
from jax.experimental.pallas import tpu as pltpu
from jax.sharding import PartitionSpec as P

LO = 3
HI = 4
ROWS = 4
SHIFTS = 8
LANES = 128
F32 = jnp.float32


def lane_of(rows):
    return lax.broadcasted_iota(jnp.int32, (rows, LANES), 1)


def group_of(rows):
    return ((lane_of(rows) + LO) & (LANES - 1)) >> 3


def low_lanes(rows):
    return (lane_of(rows) & 7) < HI


def cubic_weights(t):
    t2 = t * t
    t3 = t2 * t
    return (
        0.5 * (2.0 * t2 - t3 - t),
        0.5 * (3.0 * t3 - 5.0 * t2 + 2.0),
        0.5 * (4.0 * t2 - 3.0 * t3 + t),
        0.5 * (t3 - t2),
    )


def cubic_slopes(t):
    t2 = t * t
    return (
        0.5 * (4.0 * t - 3.0 * t2 - 1.0),
        0.5 * (9.0 * t2 - 10.0 * t),
        0.5 * (8.0 * t - 9.0 * t2 + 1.0),
        0.5 * (3.0 * t2 - 2.0 * t),
    )


def write_tables(cells, fracs, weights=None, slopes=None):
    def plane(x, carry):
        entries = []
        for c in range(3):
            k = cells[c, x]
            t = fracs[c, x]
            hits = {s: k == s for s in range(-2, 3)}
            for ref, taps in ((weights, cubic_weights), (slopes, cubic_slopes)):
                if ref is None:
                    continue
                values = taps(t)
                for j in range(SHIFTS):
                    entry = jnp.zeros_like(t)
                    for a in range(4):
                        s = j - 3 - (a - 1)
                        if -2 <= s <= 2:
                            entry = jnp.where(hits[s], values[a], entry)
                    entries.append((ref, c, j, entry))
        for ref, c, j, entry in entries:
            ref[c, j, x] = entry
        return carry

    lax.fori_loop(0, cells.shape[1], plane, 0)


def shift_planes(extended, rim, ends, shifted):
    planes, rows, _ = extended.shape
    lane = lane_of(rows)
    for X in range(planes):
        ends[X] = pltpu.roll(rim, (-8 * X) % LANES, 1)
    for X in range(planes):
        core, end = extended[X], ends[X]
        for j in range(SHIFTS):
            d = j - LO
            if d == 0:
                shifted[j, X] = core
            else:
                wraps = lane >= LANES + d if d < 0 else lane < d
                shifted[j, X] = pltpu.roll(jnp.where(wraps, end, core), (-d) % LANES, 1)


def interpolate(shifted, weights, slopes, nx, ny, emit, with_value):
    pair = 2 if nx % 2 == 0 else 1

    def plane(step, carry):
        x0 = step * pair
        tz = [[weights[2, j, x0 + p] for j in range(SHIFTS)] for p in range(pair)]
        sz = [[slopes[2, j, x0 + p] for j in range(SHIFTS)] for p in range(pair)]

        def row(sy, sums):
            a, b, c = [None] * pair, [None] * pair, [None] * pair
            for q in range(SHIFTS + pair - 1):
                window = [shifted[j, x0 + q, pl.ds(sy + 1, ny), :] for j in range(SHIFTS)]
                for p in range(pair):
                    sx = q - p
                    if not 0 <= sx < SHIFTS:
                        continue
                    x = x0 + p
                    column = total([tz[p][j] * window[j] for j in range(SHIFTS)])
                    tx = weights[0, sx, x]
                    a[p] = plus(a[p], tx * column)
                    b[p] = plus(b[p], slopes[0, sx, x] * column)
                    c[p] = plus(c[p], tx * total([sz[p][j] * window[j] for j in range(SHIFTS)]))
            out = []
            for p in range(pair):
                ty = weights[1, sy, x0 + p]
                terms = [ty * b[p], slopes[1, sy, x0 + p] * a[p], ty * c[p]]
                if with_value:
                    terms.append(ty * a[p])
                out.append(tuple(old + new for old, new in zip(sums[p], terms)))
            return tuple(out)

        zero = jnp.zeros((ny, LANES), F32)
        sums = lax.fori_loop(0, SHIFTS, row, ((zero,) * (4 if with_value else 3),) * pair)
        for p in range(pair):
            emit(x0 + p, sums[p])
        return carry

    lax.fori_loop(0, nx // pair, plane, 0)


def total(terms):
    while len(terms) > 1:
        odd = terms[len(terms) & ~1 :]
        terms = [terms[i] + terms[i + 1] for i in range(0, len(terms) - 1, 2)] + odd
    return terms[0]


def plus(a, b):
    return b if a is None else a + b


def deposit(sources, weights, scaled, piles, ys, js, fresh=True):
    channels, nx, ny, _ = sources.shape
    planes = nx + LO + HI
    if fresh:
        piles[...] = jnp.zeros(piles.shape, F32)

    def scale(sy, carry):
        tys = [weights[1, sy, x] for x in range(nx)]
        products = [(c, x, sources[c, x] * tys[x]) for c in range(channels) for x in range(nx)]
        for c, x, product in products:
            scaled[c, sy, x] = product
        return carry

    lax.fori_loop(0, SHIFTS, scale, 0)

    def row(step, carry):
        first = step * ys
        pending = []

        def flush(count):
            for _ in range(min(count, len(pending))):
                c, y, j, X, value = pending.pop(0)
                piles[c, j, X, pl.ds(first + y + 1, ny), :] += value

        for X in range(planes):
            xs = range(max(0, X - SHIFTS + 1), min(nx - 1, X) + 1)
            for j0 in range(0, SHIFTS, js):
                pace = -(-len(pending) // len(xs))
                sums = {}
                for x in xs:
                    tx = weights[0, X - x, x]
                    parts = {(c, y): scaled[c, first + y, x] * tx for c in range(channels) for y in range(ys)}
                    for j in range(j0, j0 + js):
                        tz = weights[2, j, x]
                        for at, part in parts.items():
                            sums[at + (j,)] = plus(sums.get(at + (j,)), part * tz)
                    flush(pace)
                flush(len(pending))
                pending.extend(at + (X, value) for at, value in sums.items())
        flush(len(pending))
        return carry

    lax.fori_loop(0, SHIFTS // ys, row, 0)


def settle(piles, ends, out, rims):
    channels, planes, rows, _ = out.shape
    lane = lane_of(rows)
    for c in range(channels):
        for X in range(planes):
            inside, outside = [piles[c, LO, X]], []
            for j in range(SHIFTS):
                d = j - LO
                if d == 0:
                    continue
                moved = pltpu.roll(piles[c, j, X], d % LANES, 1)
                wraps = lane >= LANES + d if d < 0 else lane < d
                inside.append(jnp.where(wraps, 0.0, moved))
                outside.append(jnp.where(wraps, moved, 0.0))
            out[c, X] = total(inside)
            ends[c, X] = total(outside)
    for c in range(channels):
        rims[c] = pack_rim(ends.at[c])


def pack_rim(extended):
    planes, rows, _ = extended.shape
    group = group_of(rows)
    rim = jnp.zeros((rows, LANES), F32)
    for X in range(planes):
        rim = jnp.where(group == X, pltpu.roll(extended[X], (8 * X) % LANES, 1), rim)
    return rim


def unpack_rim(rim, X):
    lane = lane_of(rim.shape[0])
    return jnp.where((lane < HI) | (lane >= LANES - LO), pltpu.roll(rim, (-8 * X) % LANES, 1), 0.0)


def fold_rows(message, ny):
    if ny == 2 * ROWS:
        return pltpu.roll(message, ROWS, 0)
    below, above = message[:ROWS], message[ROWS:]
    if ny == ROWS:
        return below + above
    return jnp.concatenate([above, jnp.zeros((ny - 2 * ROWS, LANES), F32), below], axis=0)


def put_edges(out, at, plane, ny):
    if ny == 2 * ROWS:
        out[at] = plane
    else:
        out[at, 0:ROWS] = plane[0:ROWS]
        out[at, ROWS : 2 * ROWS] = plane[ny - ROWS : ny]


def put_rims(out, at, plane, ny):
    out[at, 0:ROWS] = plane[0:ROWS]
    out[at, ROWS : 2 * ROWS] = plane[ROWS + ny : 2 * ROWS + ny]


def split_deposits(piled, outs, at, nx, ny):
    to_y, to_left, to_right, to_left_y, to_right_y, own = outs
    at_y, at_left, at_right, at_own = at
    planes = nx + LO + HI
    core = slice(ROWS, ROWS + ny)
    for i, X in enumerate(list(range(LO, LO + nx)) + [planes]):
        own[at_own + i] = piled[X, core]
        put_rims(to_y, at_y + i, piled[X], ny)
    for i, X in enumerate(list(range(LO)) + [planes]):
        to_left[at_left + i] = piled[X, core]
        put_rims(to_left_y, at_left + i, piled[X], ny)
    for i, X in enumerate(list(range(LO + nx, planes)) + [planes]):
        to_right[at_right + i] = piled[X, core]
        put_rims(to_right_y, at_right + i, piled[X], ny)


def join_deposits(ins, at, nx, ny, put):
    from_y, from_right, from_left, from_right_y, from_left_y, own = ins
    at_y, at_left, at_right, at_own = at

    def right(i):
        return from_right[at_left + i] + fold_rows(from_right_y[at_left + i], ny)

    def left(i):
        return from_left[at_right + i] + fold_rows(from_left_y[at_right + i], ny)

    for x in range(nx):
        plane = own[at_own + x] + fold_rows(from_y[at_y + x], ny)
        if x >= nx - LO:
            plane = plane + right(x - (nx - LO))
        if x < HI:
            plane = plane + left(x)
        put(x, plane)
    group = group_of(ny)
    rim = own[at_own + nx] + fold_rows(from_y[at_y + nx], ny)
    turn = 8 * nx
    high = pltpu.roll(right(LO), turn % LANES, 1)
    low = pltpu.roll(left(HI), (-turn) % LANES, 1)
    rim = rim + jnp.where((group >= nx) & (group < nx + LO), high, 0.0)
    return rim + jnp.where((group >= LO) & (group < LO + HI), low, 0.0)


def join_halo(field, ins, extended, nx, ny):
    from_y, from_right, from_left, from_right_y, from_left_y = ins

    def place(X, core, edges):
        extended[X, 0:ROWS] = edges[ROWS : 2 * ROWS]
        extended[X, ROWS : ROWS + ny] = core
        extended[X, ROWS + ny : 2 * ROWS + ny] = edges[0:ROWS]

    for x in range(nx):
        place(LO + x, field[x], from_y[x])
    for i in range(HI):
        place(LO + nx + i, from_right[i], from_right_y[i])
    for i in range(LO):
        place(i, from_left[i], from_left_y[i])


def split_halo(field, outs, nx, ny):
    to_y, to_left, to_right, to_left_y, to_right_y = outs
    for x in range(nx):
        put_edges(to_y, x, field[x], ny)
    for i in range(HI):
        to_left[i] = field[i]
        put_edges(to_left_y, i, field[i], ny)
    for i in range(LO):
        to_right[i] = field[nx - LO + i]
        put_edges(to_right_y, i, field[nx - LO + i], ny)


def table_kernel(nx, ny, cells, fracs, late, early, early_slopes):
    write_tables(cells.at[1, 1], fracs.at[1, 1], late)
    write_tables(cells.at[0, 1], fracs.at[0, 1], early, early_slopes)


def first_kernel(
    nx, ny, pair, weights,
    to_y, to_l, to_r, to_ly, to_ry, own,
    scaled, piles, ends, piled, rims,
):
    deposit(pair.at[1:2], weights, scaled, piles, 2, SHIFTS)
    settle(piles, ends, piled.at[:, 0 : nx + LO + HI], rims)
    piled[0, nx + LO + HI] = rims[0]
    split_halo(pair.at[0], (to_y, to_l, to_r, to_ly, to_ry), nx, ny)
    split_deposits(piled.at[0], (to_y, to_l, to_r, to_ly, to_ry, own), (nx, HI, LO, 0), nx, ny)


def first_join_kernel(nx, ny, pair, from_y, from_r, from_l, from_ry, from_ly, own, extended, part, rims):
    rows = ny + 2 * ROWS
    join_halo(pair.at[0], (from_y, from_r, from_l, from_ry, from_ly), extended, nx, ny)
    rims[0:rows] = pack_rim(extended)

    def put(x, plane):
        part[x] = plane

    rims[rows : rows + ny] = join_deposits((from_y, from_r, from_l, from_ry, from_ly, own), (nx, HI, LO, 0), nx, ny, put)


def middle_kernel(
    nx, ny, extended, rims_l, rims_r, part, weights, slopes,
    image, to_y, to_l, to_r, to_ly, to_ry, adjoint, gradient,
    shifted, ends,
):
    rows = ny + 2 * ROWS
    rim = jnp.where(low_lanes(rows), rims_r[0:rows], rims_l[0:rows])
    shift_planes(extended, rim, ends, shifted)

    def emit(x, sums):
        image[x] = sums[3]
        for c in range(3):
            gradient[c, x] = sums[c]

    interpolate(shifted, weights, slopes, nx, ny, emit, True)
    split_halo(image, (to_y, to_l, to_r, to_ly, to_ry), nx, ny)
    back = jnp.where(low_lanes(ny), rims_l[rows : rows + ny], rims_r[rows : rows + ny])
    for x in range(nx):
        adjoint[0, x] = part[x] + unpack_rim(back, LO + x)


def adjoint_kernel(
    nx, ny, adjoint, weights, cells, fracs,
    piled, rims, early_mid, late_slopes, late_mid, cleared,
    scaled, piles, ends,
):
    deposit(adjoint, weights, scaled, piles, 2, SHIFTS)
    settle(piles, ends, piled, rims)
    write_tables(cells.at[0, 0], fracs.at[0, 0], early_mid)
    write_tables(cells.at[1, 1], fracs.at[1, 1], None, late_slopes)
    write_tables(cells.at[1, 0], fracs.at[1, 0], late_mid)
    cleared[...] = jnp.zeros(cleared.shape, F32)


def early_kernel(nx, ny, gradient, adjoint, weights, cleared, piles, product, scaled):
    for c in range(3):
        for x in range(nx):
            product[c, x] = adjoint[0, x] * gradient[c, x]
    deposit(product, weights, scaled, piles, 1, SHIFTS // 2, fresh=False)


def second_join_kernel(nx, ny, image, from_y, from_r, from_l, from_ry, from_ly, earlier, extended, rims):
    join_halo(image, (from_y, from_r, from_l, from_ry, from_ly), extended, nx, ny)
    rims[...] = pack_rim(extended)


def late_kernel(
    nx, ny, extended, rims_l, rims_r, pair, weights, slopes, mid_weights, adjoint_rims, early_piles,
    piled, rims, piles,
    shifted, ends, product, scaled, rims_here,
):
    rows = ny + 2 * ROWS
    shift_planes(extended, jnp.where(low_lanes(rows), rims_r[...], rims_l[...]), ends.at[0], shifted)

    def emit(x, sums):
        for c in range(3):
            product[c, x] = pair[1, x] * sums[c]

    interpolate(shifted, weights, slopes, nx, ny, emit, False)
    deposit(product, mid_weights, scaled, piles, 1, SHIFTS // 2, fresh=False)
    settle(piles, ends, piled, rims_here)
    for c in range(3):
        rims[c * rows : (c + 1) * rows] = rims_here[c]
    rims[3 * rows : 4 * rows] = adjoint_rims[0]


def last_z_kernel(nx, ny, velocity, adjoint, rims_l, rims_r, to_y, to_l, to_r, to_ly, to_ry, own):
    rows = ny + 2 * ROWS
    low = low_lanes(rows)
    core = slice(ROWS, ROWS + ny)
    for c in range(4):
        here = slice(c * rows, (c + 1) * rows)
        back = jnp.where(low, rims_l[here], rims_r[here])
        for X in range(nx + LO + HI):
            plane = (velocity[c, X] if c < 3 else adjoint[0, X]) + unpack_rim(back, X)
            if X < LO:
                straight, corner, at = to_l, to_ly, c * LO + X
            elif X < LO + nx:
                straight, corner, at = own, to_y, c * nx + X - LO
            else:
                straight, corner, at = to_r, to_ry, c * HI + X - LO - nx
            straight[at] = plane[core]
            put_rims(corner, at, plane, ny)


def last_kernel(nx, ny, own, from_y, from_r, from_l, from_ry, from_ly, intensity_adjoint, velocity_adjoint):
    for c in range(4):
        for x in range(nx):
            at = c * nx + x
            plane = own[at] + fold_rows(from_y[at], ny)
            if x >= nx - LO:
                at = c * LO + x - (nx - LO)
                plane = plane + from_r[at] + fold_rows(from_ry[at], ny)
            if x < HI:
                at = c * HI + x
                plane = plane + from_l[at] + fold_rows(from_ly[at], ny)
            if c == 3:
                intensity_adjoint[x] = plane
            else:
                velocity_adjoint[c, x] = plane


def call(kernel, args, outs, scratch, flops, spaces=None, aliases=None):
    def struct(shape):
        return jax.ShapeDtypeStruct(shape, F32)

    in_vmem = pl.BlockSpec(memory_space=pltpu.VMEM)
    in_specs = [in_vmem] * len(args)
    for i, space in (spaces or {}).items():
        in_specs[i] = pl.BlockSpec(memory_space=space)
    moved = 4 * sum(a.size for a in args)
    return pl.pallas_call(
        kernel,
        out_shape=[struct(s) for s in outs],
        in_specs=in_specs,
        out_specs=[in_vmem] * len(outs),
        scratch_shapes=[pltpu.VMEM(s, F32) if isinstance(s, tuple) else s for s in scratch],
        input_output_aliases=aliases or {},
        compiler_params=pltpu.CompilerParams(vmem_limit_bytes=24 * 1024 * 1024),
        cost_estimate=pl.CostEstimate(flops=flops, bytes_accessed=moved, transcendentals=0),
    )(*args)


def send(message, moves):
    axes = tuple(axis for axis, _ in moves)
    sizes = [lax.axis_size(axis) for axis in axes]
    if len(axes) == 1:
        pairs = [(i, (i + moves[0][1]) % sizes[0]) for i in range(sizes[0])]
        return lax.ppermute(message, axes[0], pairs)
    pairs = [
        (i * sizes[1] + j, (i + moves[0][1]) % sizes[0] * sizes[1] + (j + moves[1][1]) % sizes[1])
        for i in range(sizes[0])
        for j in range(sizes[1])
    ]
    return lax.ppermute(message, axes, pairs)


def send_y(message, *moves):
    if lax.axis_size("gy") == 2:
        return send(message, moves + (("gy", 1),))
    down = send(message[:, :ROWS], moves + (("gy", -1),))
    up = send(message[:, ROWS:], moves + (("gy", 1),))
    return jnp.concatenate([down, up], axis=1)


def send_sides(to_y, to_l, to_r, to_ly, to_ry):
    left, right = ("gx", -1), ("gx", 1)
    return (
        send_y(to_y),
        send(to_l, (left,)),
        send(to_r, (right,)),
        send_y(to_ly, left),
        send_y(to_ry, right),
    )


def send_z(rims):
    return send(rims, (("gz", 1),)), send(rims, (("gz", -1),))


def body(intensity, cotangent, cells, fracs):
    nx, ny, nz = intensity.shape
    rows = ny + 2 * ROWS
    planes = nx + LO + HI
    ring = 2 * ROWS
    field = (nx, ny, nz)
    table = (3, SHIFTS) + field
    pair = jnp.stack([intensity, cotangent])
    unit = nx * ny * nz * 512

    def run(kernel, *rest, **more):
        return call(functools.partial(kernel, nx, ny), *rest, **more)

    def pile(channels):
        return [(channels, SHIFTS) + field, (channels, SHIFTS, planes, rows, nz)]

    def piled(channels):
        return [(channels, planes, rows, nz), (channels, rows, nz)]

    def messages(y, l, r):
        return [(y, ring, nz), (l, ny, nz), (r, ny, nz), (l, ring, nz), (r, ring, nz)]

    late, early, early_slopes = run(
        table_kernel,
        (cells, fracs),
        [table, table, table],
        [],
        unit // 16,
    )
    *outs, own = run(
        first_kernel,
        (pair, late),
        messages(2 * nx + 1, HI + LO + 1, LO + HI + 1) + [(nx + 1, ny, nz)],
        pile(1) + [(1, planes, rows, nz), (1, planes + 1, rows, nz), (1, rows, nz)],
        2 * unit,
    )
    extended, folded, rims = run(
        first_join_kernel,
        (pair,) + send_sides(*outs) + (own,),
        [(planes, rows, nz), field, (rows + ny, nz)],
        [],
        unit // 16,
    )
    image, *outs, adjoint, gradient = run(
        middle_kernel,
        (extended,) + send_z(rims) + (folded, early, early_slopes),
        [field] + messages(nx, HI, LO) + [(1,) + field, (3,) + field],
        [(SHIFTS, planes, rows, nz), (planes, rows, nz)],
        5 * unit,
    )

    sides = send_sides(*outs)
    scaled_3, piles_3 = pile(3)
    piled_adjoint, adjoint_rims, early_mid, late_slopes, late_mid, cleared = run(
        adjoint_kernel,
        (adjoint, early, cells, fracs),
        piled(1) + [table, table, table, piles_3],
        pile(1) + [(1, planes, rows, nz)],
        2 * unit,
    )
    extended, rims = run(
        second_join_kernel,
        (image,) + sides + (piled_adjoint,),
        [(planes, rows, nz), (rows, nz)],
        [],
        unit // 16,
        spaces={6: pl.ANY},
    )
    rims_l, rims_r = send_z(rims)
    (piles,) = run(
        early_kernel,
        (gradient, adjoint, early_mid, cleared),
        [piles_3],
        [(3,) + field, scaled_3],
        6 * unit,
        aliases={3: 0},
    )

    velocity, rims, _ = run(
        late_kernel,
        (extended, rims_l, rims_r, pair, late, late_slopes, late_mid, adjoint_rims, piles),
        [(3, planes, rows, nz), (4 * rows, nz), piles_3],
        [(SHIFTS, planes, rows, nz), (3, planes, rows, nz), (3,) + field, scaled_3, (3, rows, nz)],
        11 * unit,
        aliases={8: 2},
    )
    *outs, own = run(
        last_z_kernel,
        (velocity, piled_adjoint) + send_z(rims),
        messages(4 * nx, 4 * LO, 4 * HI) + [(4 * nx, ny, nz)],
        [],
        unit // 16,
    )
    return tuple(
        run(
            last_kernel,
            (own,) + send_sides(*outs),
            [field, (3,) + field],
            [],
            unit // 16,
        )
    )


def solution(mesh):
    in_specs = (
        P("gx", "gy", "gz"),
        P("gx", "gy", "gz"),
        P(None, None, None, "gx", "gy", "gz"),
        P(None, None, None, "gx", "gy", "gz"),
    )
    out_specs = (P("gx", "gy", "gz"), P(None, "gx", "gy", "gz"))
    return jax.shard_map(body, mesh=mesh, in_specs=in_specs, out_specs=out_specs, check_vma=False)
```

```python
import functools

import jax
import jax.numpy as jnp
from jax import lax
from jax.experimental import pallas as pl
from jax.experimental.pallas import tpu as pltpu
from jax.sharding import PartitionSpec as P

LO = 3
HI = 4
ROWS = 4
SHIFTS = 8
LANES = 128
F32 = jnp.float32


def lane_of(rows):
    return lax.broadcasted_iota(jnp.int32, (rows, LANES), 1)


def group_of(rows):
    return ((lane_of(rows) + LO) & (LANES - 1)) >> 3


def low_lanes(rows):
    return (lane_of(rows) & 7) < HI


def cubic_weights(t):
    t2 = t * t
    t3 = t2 * t
    return (
        0.5 * (2.0 * t2 - t3 - t),
        0.5 * (3.0 * t3 - 5.0 * t2 + 2.0),
        0.5 * (4.0 * t2 - 3.0 * t3 + t),
        0.5 * (t3 - t2),
    )


def cubic_slopes(t):
    t2 = t * t
    return (
        0.5 * (4.0 * t - 3.0 * t2 - 1.0),
        0.5 * (9.0 * t2 - 10.0 * t),
        0.5 * (8.0 * t - 9.0 * t2 + 1.0),
        0.5 * (3.0 * t2 - 2.0 * t),
    )


def write_tables(cells, fracs, weights=None, slopes=None):
    def plane(x, carry):
        entries = []
        for c in range(3):
            k = cells[c, x]
            t = fracs[c, x]
            hits = {s: k == s for s in range(-2, 3)}
            for ref, taps in ((weights, cubic_weights), (slopes, cubic_slopes)):
                if ref is None:
                    continue
                values = taps(t)
                for j in range(SHIFTS):
                    entry = jnp.zeros_like(t)
                    for a in range(4):
                        s = j - 3 - (a - 1)
                        if -2 <= s <= 2:
                            entry = jnp.where(hits[s], values[a], entry)
                    entries.append((ref, c, j, entry))
        for ref, c, j, entry in entries:
            ref[c, j, x] = entry
        return carry

    lax.fori_loop(0, cells.shape[1], plane, 0)


def shift_planes(extended, rim, ends, shifted):
    planes, rows, _ = extended.shape
    lane = lane_of(rows)
    for X in range(planes):
        ends[X] = pltpu.roll(rim, (-8 * X) % LANES, 1)
    for X in range(planes):
        core, end = extended[X], ends[X]
        for j in range(SHIFTS):
            d = j - LO
            if d == 0:
                shifted[j, X] = core
            else:
                wraps = lane >= LANES + d if d < 0 else lane < d
                shifted[j, X] = pltpu.roll(jnp.where(wraps, end, core), (-d) % LANES, 1)


def interpolate(shifted, weights, slopes, nx, ny, emit, with_value):
    pair = 2 if nx % 2 == 0 else 1

    def plane(step, carry):
        x0 = step * pair
        tz = [[weights[2, j, x0 + p] for j in range(SHIFTS)] for p in range(pair)]
        sz = [[slopes[2, j, x0 + p] for j in range(SHIFTS)] for p in range(pair)]

        def row(sy, sums):
            a, b, c = [None] * pair, [None] * pair, [None] * pair
            for q in range(SHIFTS + pair - 1):
                window = [shifted[j, x0 + q, pl.ds(sy + 1, ny), :] for j in range(SHIFTS)]
                for p in range(pair):
                    sx = q - p
                    if not 0 <= sx < SHIFTS:
                        continue
                    x = x0 + p
                    column = total([tz[p][j] * window[j] for j in range(SHIFTS)])
                    tx = weights[0, sx, x]
                    a[p] = plus(a[p], tx * column)
                    b[p] = plus(b[p], slopes[0, sx, x] * column)
                    c[p] = plus(c[p], tx * total([sz[p][j] * window[j] for j in range(SHIFTS)]))
            out = []
            for p in range(pair):
                ty = weights[1, sy, x0 + p]
                terms = [ty * b[p], slopes[1, sy, x0 + p] * a[p], ty * c[p]]
                if with_value:
                    terms.append(ty * a[p])
                out.append(tuple(old + new for old, new in zip(sums[p], terms)))
            return tuple(out)

        zero = jnp.zeros((ny, LANES), F32)
        sums = lax.fori_loop(0, SHIFTS, row, ((zero,) * (4 if with_value else 3),) * pair)
        for p in range(pair):
            emit(x0 + p, sums[p])
        return carry

    lax.fori_loop(0, nx // pair, plane, 0)


def total(terms):
    while len(terms) > 1:
        odd = terms[len(terms) & ~1 :]
        terms = [terms[i] + terms[i + 1] for i in range(0, len(terms) - 1, 2)] + odd
    return terms[0]


def plus(a, b):
    return b if a is None else a + b


def deposit(sources, weights, scaled, piles, ys, js, fresh=True):
    channels, nx, ny, _ = sources.shape
    planes = nx + LO + HI
    if fresh:
        piles[...] = jnp.zeros(piles.shape, F32)

    def scale(sy, carry):
        tys = [weights[1, sy, x] for x in range(nx)]
        products = [(c, x, sources[c, x] * tys[x]) for c in range(channels) for x in range(nx)]
        for c, x, product in products:
            scaled[c, sy, x] = product
        return carry

    lax.fori_loop(0, SHIFTS, scale, 0)

    def row(step, carry):
        first = step * ys
        pending = []

        def flush(count):
            for _ in range(min(count, len(pending))):
                c, y, j, X, value = pending.pop(0)
                piles[c, j, X, pl.ds(first + y + 1, ny), :] += value

        for X in range(planes):
            xs = range(max(0, X - SHIFTS + 1), min(nx - 1, X) + 1)
            for j0 in range(0, SHIFTS, js):
                pace = -(-len(pending) // len(xs))
                sums = {}
                for x in xs:
                    tx = weights[0, X - x, x]
                    parts = {(c, y): scaled[c, first + y, x] * tx for c in range(channels) for y in range(ys)}
                    for j in range(j0, j0 + js):
                        tz = weights[2, j, x]
                        for at, part in parts.items():
                            sums[at + (j,)] = plus(sums.get(at + (j,)), part * tz)
                    flush(pace)
                flush(len(pending))
                pending.extend(at + (X, value) for at, value in sums.items())
        flush(len(pending))
        return carry

    lax.fori_loop(0, SHIFTS // ys, row, 0)


def settle(piles, ends, out, rims):
    channels, planes, rows, _ = out.shape
    lane = lane_of(rows)
    for c in range(channels):
        for X in range(planes):
            inside, outside = [piles[c, LO, X]], []
            for j in range(SHIFTS):
                d = j - LO
                if d == 0:
                    continue
                moved = pltpu.roll(piles[c, j, X], d % LANES, 1)
                wraps = lane >= LANES + d if d < 0 else lane < d
                inside.append(jnp.where(wraps, 0.0, moved))
                outside.append(jnp.where(wraps, moved, 0.0))
            out[c, X] = total(inside)
            ends[c, X] = total(outside)
    for c in range(channels):
        rims[c] = pack_rim(ends.at[c])


def pack_rim(extended):
    planes, rows, _ = extended.shape
    group = group_of(rows)
    rim = jnp.zeros((rows, LANES), F32)
    for X in range(planes):
        rim = jnp.where(group == X, pltpu.roll(extended[X], (8 * X) % LANES, 1), rim)
    return rim


def unpack_rim(rim, X):
    lane = lane_of(rim.shape[0])
    return jnp.where((lane < HI) | (lane >= LANES - LO), pltpu.roll(rim, (-8 * X) % LANES, 1), 0.0)


def fold_rows(message, ny):
    if ny == 2 * ROWS:
        return pltpu.roll(message, ROWS, 0)
    below, above = message[:ROWS], message[ROWS:]
    if ny == ROWS:
        return below + above
    return jnp.concatenate([above, jnp.zeros((ny - 2 * ROWS, LANES), F32), below], axis=0)


def put_edges(out, at, plane, ny):
    if ny == 2 * ROWS:
        out[at] = plane
    else:
        out[at, 0:ROWS] = plane[0:ROWS]
        out[at, ROWS : 2 * ROWS] = plane[ny - ROWS : ny]


def put_rims(out, at, plane, ny):
    out[at, 0:ROWS] = plane[0:ROWS]
    out[at, ROWS : 2 * ROWS] = plane[ROWS + ny : 2 * ROWS + ny]


def split_deposits(piled, outs, at, nx, ny):
    to_y, to_left, to_right, to_left_y, to_right_y, own = outs
    at_y, at_left, at_right, at_own = at
    planes = nx + LO + HI
    core = slice(ROWS, ROWS + ny)
    for i, X in enumerate(list(range(LO, LO + nx)) + [planes]):
        own[at_own + i] = piled[X, core]
        put_rims(to_y, at_y + i, piled[X], ny)
    for i, X in enumerate(list(range(LO)) + [planes]):
        to_left[at_left + i] = piled[X, core]
        put_rims(to_left_y, at_left + i, piled[X], ny)
    for i, X in enumerate(list(range(LO + nx, planes)) + [planes]):
        to_right[at_right + i] = piled[X, core]
        put_rims(to_right_y, at_right + i, piled[X], ny)


def join_deposits(ins, at, nx, ny, put):
    from_y, from_right, from_left, from_right_y, from_left_y, own = ins
    at_y, at_left, at_right, at_own = at

    def right(i):
        return from_right[at_left + i] + fold_rows(from_right_y[at_left + i], ny)

    def left(i):
        return from_left[at_right + i] + fold_rows(from_left_y[at_right + i], ny)

    for x in range(nx):
        plane = own[at_own + x] + fold_rows(from_y[at_y + x], ny)
        if x >= nx - LO:
            plane = plane + right(x - (nx - LO))
        if x < HI:
            plane = plane + left(x)
        put(x, plane)
    group = group_of(ny)
    rim = own[at_own + nx] + fold_rows(from_y[at_y + nx], ny)
    turn = 8 * nx
    high = pltpu.roll(right(LO), turn % LANES, 1)
    low = pltpu.roll(left(HI), (-turn) % LANES, 1)
    rim = rim + jnp.where((group >= nx) & (group < nx + LO), high, 0.0)
    return rim + jnp.where((group >= LO) & (group < LO + HI), low, 0.0)


def join_halo(field, ins, extended, nx, ny):
    from_y, from_right, from_left, from_right_y, from_left_y = ins

    def place(X, core, edges):
        extended[X, 0:ROWS] = edges[ROWS : 2 * ROWS]
        extended[X, ROWS : ROWS + ny] = core
        extended[X, ROWS + ny : 2 * ROWS + ny] = edges[0:ROWS]

    for x in range(nx):
        place(LO + x, field[x], from_y[x])
    for i in range(HI):
        place(LO + nx + i, from_right[i], from_right_y[i])
    for i in range(LO):
        place(i, from_left[i], from_left_y[i])


def fill(size, used, *messages):
    for message in messages:
        for i in range(used, size):
            message[i] = jnp.zeros(message.shape[1:], F32)


def split_halo(field, outs, nx, ny):
    to_y, to_left, to_right, to_left_y, to_right_y = outs
    for x in range(nx):
        put_edges(to_y, x, field[x], ny)
    for i in range(HI):
        to_left[i] = field[i]
        put_edges(to_left_y, i, field[i], ny)
    for i in range(LO):
        to_right[i] = field[nx - LO + i]
        put_edges(to_right_y, i, field[nx - LO + i], ny)


def table_kernel(nx, ny, cells, fracs, late, early, early_slopes):
    write_tables(cells.at[1, 1], fracs.at[1, 1], late)
    write_tables(cells.at[0, 1], fracs.at[0, 1], early, early_slopes)


def first_kernel(
    nx, ny, pair, weights,
    to_y, to_l, to_r, to_ly, to_ry, own,
    scaled, piles, ends, piled, rims,
):
    deposit(pair.at[1:2], weights, scaled, piles, 2, SHIFTS)
    settle(piles, ends, piled.at[:, 0 : nx + LO + HI], rims)
    piled[0, nx + LO + HI] = rims[0]
    split_halo(pair.at[0], (to_y, to_l, to_r, to_ly, to_ry), nx, ny)
    split_deposits(piled.at[0], (to_y, to_l, to_r, to_ly, to_ry, own), (nx, HI, LO, 0), nx, ny)


def first_join_kernel(nx, ny, pair, from_y, from_r, from_l, from_ry, from_ly, own, extended, part, rims):
    rows = ny + 2 * ROWS
    join_halo(pair.at[0], (from_y, from_r, from_l, from_ry, from_ly), extended, nx, ny)
    rims[0:rows] = pack_rim(extended)

    def put(x, plane):
        part[x] = plane

    rims[rows : rows + ny] = join_deposits((from_y, from_r, from_l, from_ry, from_ly, own), (nx, HI, LO, 0), nx, ny, put)


def middle_kernel(
    nx, ny, extended, rims_l, rims_r, part, weights, slopes,
    image, to_y, to_l, to_r, to_ly, to_ry, adjoint, gradient,
    shifted, ends,
):
    rows = ny + 2 * ROWS
    rim = jnp.where(low_lanes(rows), rims_r[0:rows], rims_l[0:rows])
    shift_planes(extended, rim, ends, shifted)

    def emit(x, sums):
        image[x] = sums[3]
        for c in range(3):
            gradient[c, x] = sums[c]

    interpolate(shifted, weights, slopes, nx, ny, emit, True)
    split_halo(image, (to_y, to_l, to_r, to_ly, to_ry), nx, ny)
    fill(HI, LO, to_r, to_ry)
    back = jnp.where(low_lanes(ny), rims_l[rows : rows + ny], rims_r[rows : rows + ny])
    for x in range(nx):
        adjoint[0, x] = part[x] + unpack_rim(back, LO + x)


def adjoint_kernel(
    nx, ny, adjoint, weights, cells, fracs,
    piled, rims, early_mid, late_slopes, late_mid, cleared,
    scaled, piles, ends,
):
    deposit(adjoint, weights, scaled, piles, 2, SHIFTS)
    settle(piles, ends, piled, rims)
    write_tables(cells.at[0, 0], fracs.at[0, 0], early_mid)
    write_tables(cells.at[1, 1], fracs.at[1, 1], None, late_slopes)
    write_tables(cells.at[1, 0], fracs.at[1, 0], late_mid)
    cleared[...] = jnp.zeros(cleared.shape, F32)


def early_kernel(nx, ny, gradient, adjoint, weights, cleared, piles, product, scaled):
    for c in range(3):
        for x in range(nx):
            product[c, x] = adjoint[0, x] * gradient[c, x]
    deposit(product, weights, scaled, piles, 1, SHIFTS // 2, fresh=False)


def second_join_kernel(nx, ny, image, from_y, from_r, from_l, from_ry, from_ly, earlier, extended, rims):
    join_halo(image, (from_y, from_r, from_l, from_ry, from_ly), extended, nx, ny)
    rims[...] = pack_rim(extended)


def late_kernel(
    nx, ny, extended, rims_l, rims_r, pair, weights, slopes, mid_weights, adjoint_rims, early_piles,
    piled, rims, piles,
    shifted, ends, product, scaled, rims_here,
):
    rows = ny + 2 * ROWS
    shift_planes(extended, jnp.where(low_lanes(rows), rims_r[...], rims_l[...]), ends.at[0], shifted)

    def emit(x, sums):
        for c in range(3):
            product[c, x] = pair[1, x] * sums[c]

    interpolate(shifted, weights, slopes, nx, ny, emit, False)
    deposit(product, mid_weights, scaled, piles, 1, SHIFTS // 2, fresh=False)
    settle(piles, ends, piled, rims_here)
    for c in range(3):
        rims[c * rows : (c + 1) * rows] = rims_here[c]
    rims[3 * rows : 4 * rows] = adjoint_rims[0]


def last_z_kernel(nx, ny, velocity, adjoint, rims_l, rims_r, to_y, to_l, to_r, to_ly, to_ry, own):
    rows = ny + 2 * ROWS
    low = low_lanes(rows)
    core = slice(ROWS, ROWS + ny)
    for c in range(4):
        here = slice(c * rows, (c + 1) * rows)
        back = jnp.where(low, rims_l[here], rims_r[here])
        for X in range(nx + LO + HI):
            plane = (velocity[c, X] if c < 3 else adjoint[0, X]) + unpack_rim(back, X)
            if X < LO:
                straight, corner, at = to_l, to_ly, c * LO + X
            elif X < LO + nx:
                straight, corner, at = own, to_y, c * nx + X - LO
            else:
                straight, corner, at = to_r, to_ry, c * HI + X - LO - nx
            straight[at] = plane[core]
            put_rims(corner, at, plane, ny)
    fill(4 * HI, 4 * LO, to_l, to_ly)


def last_kernel(nx, ny, own, from_y, from_r, from_l, from_ry, from_ly, intensity_adjoint, velocity_adjoint):
    for c in range(4):
        for x in range(nx):
            at = c * nx + x
            plane = own[at] + fold_rows(from_y[at], ny)
            if x >= nx - LO:
                at = c * LO + x - (nx - LO)
                plane = plane + from_r[at] + fold_rows(from_ry[at], ny)
            if x < HI:
                at = c * HI + x
                plane = plane + from_l[at] + fold_rows(from_ly[at], ny)
            if c == 3:
                intensity_adjoint[x] = plane
            else:
                velocity_adjoint[c, x] = plane


def call(kernel, args, outs, scratch, flops, spaces=None, aliases=None):
    def struct(shape):
        return jax.ShapeDtypeStruct(shape, F32)

    in_vmem = pl.BlockSpec(memory_space=pltpu.VMEM)
    in_specs = [in_vmem] * len(args)
    for i, space in (spaces or {}).items():
        in_specs[i] = pl.BlockSpec(memory_space=space)
    moved = 4 * sum(a.size for a in args)
    return pl.pallas_call(
        kernel,
        out_shape=[struct(s) for s in outs],
        in_specs=in_specs,
        out_specs=[in_vmem] * len(outs),
        scratch_shapes=[pltpu.VMEM(s, F32) if isinstance(s, tuple) else s for s in scratch],
        input_output_aliases=aliases or {},
        compiler_params=pltpu.CompilerParams(vmem_limit_bytes=24 * 1024 * 1024),
        cost_estimate=pl.CostEstimate(flops=flops, bytes_accessed=moved, transcendentals=0),
    )(*args)


def send(message, moves):
    axes = tuple(axis for axis, _ in moves)
    sizes = [lax.axis_size(axis) for axis in axes]
    if len(axes) == 1:
        pairs = [(i, (i + moves[0][1]) % sizes[0]) for i in range(sizes[0])]
        return lax.ppermute(message, axes[0], pairs)
    pairs = [
        (i * sizes[1] + j, (i + moves[0][1]) % sizes[0] * sizes[1] + (j + moves[1][1]) % sizes[1])
        for i in range(sizes[0])
        for j in range(sizes[1])
    ]
    return lax.ppermute(message, axes, pairs)


def send_y(message, *moves):
    if lax.axis_size("gy") == 2:
        return send(message, moves + (("gy", 1),))
    down = send(message[:, :ROWS], moves + (("gy", -1),))
    up = send(message[:, ROWS:], moves + (("gy", 1),))
    return jnp.concatenate([down, up], axis=1)


def send_sides(to_y, to_l, to_r, to_ly, to_ry):
    left, right = ("gx", -1), ("gx", 1)
    return (
        send_y(to_y),
        send(to_l, (left,)),
        send(to_r, (right,)),
        send_y(to_ly, left),
        send_y(to_ry, right),
    )


def send_z(rims):
    return send(rims, (("gz", 1),)), send(rims, (("gz", -1),))


def body(intensity, cotangent, cells, fracs):
    nx, ny, nz = intensity.shape
    rows = ny + 2 * ROWS
    planes = nx + LO + HI
    ring = 2 * ROWS
    field = (nx, ny, nz)
    table = (3, SHIFTS) + field
    pair = jnp.stack([intensity, cotangent])
    unit = nx * ny * nz * 512

    def run(kernel, *rest, **more):
        return call(functools.partial(kernel, nx, ny), *rest, **more)

    def pile(channels):
        return [(channels, SHIFTS) + field, (channels, SHIFTS, planes, rows, nz)]

    def piled(channels):
        return [(channels, planes, rows, nz), (channels, rows, nz)]

    def messages(y, l, r):
        return [(y, ring, nz), (l, ny, nz), (r, ny, nz), (l, ring, nz), (r, ring, nz)]

    late, early, early_slopes = run(
        table_kernel,
        (cells, fracs),
        [table, table, table],
        [],
        unit // 16,
    )
    *outs, own = run(
        first_kernel,
        (pair, late),
        messages(2 * nx + 1, HI + LO + 1, LO + HI + 1) + [(nx + 1, ny, nz)],
        pile(1) + [(1, planes, rows, nz), (1, planes + 1, rows, nz), (1, rows, nz)],
        2 * unit,
    )
    extended, folded, rims = run(
        first_join_kernel,
        (pair,) + send_sides(*outs) + (own,),
        [(planes, rows, nz), field, (rows + ny, nz)],
        [],
        unit // 16,
    )
    image, *outs, adjoint, gradient = run(
        middle_kernel,
        (extended,) + send_z(rims) + (folded, early, early_slopes),
        [field] + messages(nx, HI, HI) + [(1,) + field, (3,) + field],
        [(SHIFTS, planes, rows, nz), (planes, rows, nz)],
        5 * unit,
    )

    sides = send_sides(*outs)
    scaled_3, piles_3 = pile(3)
    piled_adjoint, adjoint_rims, early_mid, late_slopes, late_mid, cleared = run(
        adjoint_kernel,
        (adjoint, early, cells, fracs),
        piled(1) + [table, table, table, piles_3],
        pile(1) + [(1, planes, rows, nz)],
        2 * unit,
    )
    extended, rims = run(
        second_join_kernel,
        (image,) + sides + (piled_adjoint,),
        [(planes, rows, nz), (rows, nz)],
        [],
        unit // 16,
        spaces={6: pl.ANY},
    )
    rims_l, rims_r = send_z(rims)
    (piles,) = run(
        early_kernel,
        (gradient, adjoint, early_mid, cleared),
        [piles_3],
        [(3,) + field, scaled_3],
        6 * unit,
        aliases={3: 0},
    )

    velocity, rims, _ = run(
        late_kernel,
        (extended, rims_l, rims_r, pair, late, late_slopes, late_mid, adjoint_rims, piles),
        [(3, planes, rows, nz), (4 * rows, nz), piles_3],
        [(SHIFTS, planes, rows, nz), (3, planes, rows, nz), (3,) + field, scaled_3, (3, rows, nz)],
        11 * unit,
        aliases={8: 2},
    )
    *outs, own = run(
        last_z_kernel,
        (velocity, piled_adjoint) + send_z(rims),
        messages(4 * nx, 4 * HI, 4 * HI) + [(4 * nx, ny, nz)],
        [],
        unit // 16,
    )
    return tuple(
        run(
            last_kernel,
            (own,) + send_sides(*outs),
            [field, (3,) + field],
            [],
            unit // 16,
        )
    )


def solution(mesh):
    in_specs = (
        P("gx", "gy", "gz"),
        P("gx", "gy", "gz"),
        P(None, None, None, "gx", "gy", "gz"),
        P(None, None, None, "gx", "gy", "gz"),
    )
    out_specs = (P("gx", "gy", "gz"), P(None, "gx", "gy", "gz"))
    return jax.shard_map(body, mesh=mesh, in_specs=in_specs, out_specs=out_specs, check_vma=False)
```

```python
import functools

import jax
import jax.numpy as jnp
from jax import lax
from jax.experimental import pallas as pl
from jax.experimental.pallas import tpu as pltpu
from jax.sharding import PartitionSpec as P

LO = 3
HI = 4
ROWS = 4
SHIFTS = 8
LANES = 128
F32 = jnp.float32


def lane_of(rows):
    return lax.broadcasted_iota(jnp.int32, (rows, LANES), 1)


def group_of(rows):
    return ((lane_of(rows) + LO) & (LANES - 1)) >> 3


def low_lanes(rows):
    return (lane_of(rows) & 7) < HI


def cubic_weights(t):
    t2 = t * t
    t3 = t2 * t
    return (
        0.5 * (2.0 * t2 - t3 - t),
        0.5 * (3.0 * t3 - 5.0 * t2 + 2.0),
        0.5 * (4.0 * t2 - 3.0 * t3 + t),
        0.5 * (t3 - t2),
    )


def cubic_slopes(t):
    t2 = t * t
    return (
        0.5 * (4.0 * t - 3.0 * t2 - 1.0),
        0.5 * (9.0 * t2 - 10.0 * t),
        0.5 * (8.0 * t - 9.0 * t2 + 1.0),
        0.5 * (3.0 * t2 - 2.0 * t),
    )


def write_tables(cells, fracs, weights=None, slopes=None):
    def plane(x, carry):
        entries = []
        for c in range(3):
            k = cells[c, x]
            t = fracs[c, x]
            hits = {s: k == s for s in range(-2, 3)}
            for ref, taps in ((weights, cubic_weights), (slopes, cubic_slopes)):
                if ref is None:
                    continue
                values = taps(t)
                for j in range(SHIFTS):
                    entry = jnp.zeros_like(t)
                    for a in range(4):
                        s = j - 3 - (a - 1)
                        if -2 <= s <= 2:
                            entry = jnp.where(hits[s], values[a], entry)
                    entries.append((ref, c, j, entry))
        for ref, c, j, entry in entries:
            ref[c, j, x] = entry
        return carry

    lax.fori_loop(0, cells.shape[1], plane, 0)


def shift_planes(extended, rim, ends, shifted):
    planes, rows, _ = extended.shape
    lane = lane_of(rows)
    for X in range(planes):
        ends[X] = pltpu.roll(rim, (-8 * X) % LANES, 1)
    for X in range(planes):
        core, end = extended[X], ends[X]
        for j in range(SHIFTS):
            d = j - LO
            if d == 0:
                shifted[j, X] = core
            else:
                wraps = lane >= LANES + d if d < 0 else lane < d
                shifted[j, X] = pltpu.roll(jnp.where(wraps, end, core), (-d) % LANES, 1)


def interpolate(shifted, weights, slopes, nx, ny, emit, with_value):
    pair = 2 if nx % 2 == 0 else 1

    def plane(step, carry):
        x0 = step * pair
        tz = [[weights[2, j, x0 + p] for j in range(SHIFTS)] for p in range(pair)]
        sz = [[slopes[2, j, x0 + p] for j in range(SHIFTS)] for p in range(pair)]

        def row(sy, sums):
            a, b, c = [None] * pair, [None] * pair, [None] * pair
            for q in range(SHIFTS + pair - 1):
                window = [shifted[j, x0 + q, pl.ds(sy + 1, ny), :] for j in range(SHIFTS)]
                for p in range(pair):
                    sx = q - p
                    if not 0 <= sx < SHIFTS:
                        continue
                    x = x0 + p
                    column = total([tz[p][j] * window[j] for j in range(SHIFTS)])
                    tx = weights[0, sx, x]
                    a[p] = plus(a[p], tx * column)
                    b[p] = plus(b[p], slopes[0, sx, x] * column)
                    c[p] = plus(c[p], tx * total([sz[p][j] * window[j] for j in range(SHIFTS)]))
            out = []
            for p in range(pair):
                ty = weights[1, sy, x0 + p]
                terms = [ty * b[p], slopes[1, sy, x0 + p] * a[p], ty * c[p]]
                if with_value:
                    terms.append(ty * a[p])
                out.append(tuple(old + new for old, new in zip(sums[p], terms)))
            return tuple(out)

        zero = jnp.zeros((ny, LANES), F32)
        sums = lax.fori_loop(0, SHIFTS, row, ((zero,) * (4 if with_value else 3),) * pair)
        for p in range(pair):
            emit(x0 + p, sums[p])
        return carry

    lax.fori_loop(0, nx // pair, plane, 0)


def total(terms):
    while len(terms) > 1:
        odd = terms[len(terms) & ~1 :]
        terms = [terms[i] + terms[i + 1] for i in range(0, len(terms) - 1, 2)] + odd
    return terms[0]


def plus(a, b):
    return b if a is None else a + b


def deposit(sources, weights, scaled, piles, ys, js, fresh=True):
    channels, nx, ny, _ = sources.shape
    planes = nx + LO + HI
    if fresh:
        piles[...] = jnp.zeros(piles.shape, F32)

    def scale(sy, carry):
        tys = [weights[1, sy, x] for x in range(nx)]
        products = [(c, x, sources[c, x] * tys[x]) for c in range(channels) for x in range(nx)]
        for c, x, product in products:
            scaled[c, sy, x] = product
        return carry

    lax.fori_loop(0, SHIFTS, scale, 0)

    def row(step, carry):
        first = step * ys
        pending = []

        def flush(count):
            for _ in range(min(count, len(pending))):
                c, y, j, X, value = pending.pop(0)
                piles[c, j, X, pl.ds(first + y + 1, ny), :] += value

        for X in range(planes):
            xs = range(max(0, X - SHIFTS + 1), min(nx - 1, X) + 1)
            for j0 in range(0, SHIFTS, js):
                pace = -(-len(pending) // len(xs))
                sums = {}
                for x in xs:
                    tx = weights[0, X - x, x]
                    parts = {(c, y): scaled[c, first + y, x] * tx for c in range(channels) for y in range(ys)}
                    for j in range(j0, j0 + js):
                        tz = weights[2, j, x]
                        for at, part in parts.items():
                            sums[at + (j,)] = plus(sums.get(at + (j,)), part * tz)
                    flush(pace)
                flush(len(pending))
                pending.extend(at + (X, value) for at, value in sums.items())
        flush(len(pending))
        return carry

    lax.fori_loop(0, SHIFTS // ys, row, 0)


def settle(piles, ends, out, rims):
    channels, planes, rows, _ = out.shape
    lane = lane_of(rows)
    for c in range(channels):
        for X in range(planes):
            inside, outside = [piles[c, LO, X]], []
            for j in range(SHIFTS):
                d = j - LO
                if d == 0:
                    continue
                moved = pltpu.roll(piles[c, j, X], d % LANES, 1)
                wraps = lane >= LANES + d if d < 0 else lane < d
                inside.append(jnp.where(wraps, 0.0, moved))
                outside.append(jnp.where(wraps, moved, 0.0))
            out[c, X] = total(inside)
            ends[c, X] = total(outside)
    for c in range(channels):
        rims[c] = pack_rim(ends.at[c])


def pack_rim(extended):
    planes, rows, _ = extended.shape
    group = group_of(rows)
    rim = jnp.zeros((rows, LANES), F32)
    for X in range(planes):
        rim = jnp.where(group == X, pltpu.roll(extended[X], (8 * X) % LANES, 1), rim)
    return rim


def unpack_rim(rim, X):
    lane = lane_of(rim.shape[0])
    return jnp.where((lane < HI) | (lane >= LANES - LO), pltpu.roll(rim, (-8 * X) % LANES, 1), 0.0)


def fold_rows(message, ny):
    if ny == 2 * ROWS:
        return pltpu.roll(message, ROWS, 0)
    below, above = message[:ROWS], message[ROWS:]
    if ny == ROWS:
        return below + above
    return jnp.concatenate([above, jnp.zeros((ny - 2 * ROWS, LANES), F32), below], axis=0)


def put_edges(out, at, plane, ny):
    if ny == 2 * ROWS:
        out[at] = plane
    else:
        out[at, 0:ROWS] = plane[0:ROWS]
        out[at, ROWS : 2 * ROWS] = plane[ny - ROWS : ny]


def put_rims(out, at, plane, ny):
    out[at, 0:ROWS] = plane[0:ROWS]
    out[at, ROWS : 2 * ROWS] = plane[ROWS + ny : 2 * ROWS + ny]


def split_deposits(piled, outs, at, nx, ny):
    to_y, to_left, to_right, to_left_y, to_right_y, own = outs
    at_y, at_left, at_right, at_own = at
    planes = nx + LO + HI
    core = slice(ROWS, ROWS + ny)
    for i, X in enumerate(list(range(LO, LO + nx)) + [planes]):
        own[at_own + i] = piled[X, core]
        put_rims(to_y, at_y + i, piled[X], ny)
    for i, X in enumerate(list(range(LO)) + [planes]):
        to_left[at_left + i] = piled[X, core]
        put_rims(to_left_y, at_left + i, piled[X], ny)
    for i, X in enumerate(list(range(LO + nx, planes)) + [planes]):
        to_right[at_right + i] = piled[X, core]
        put_rims(to_right_y, at_right + i, piled[X], ny)


def join_deposits(ins, at, nx, ny, put):
    from_y, from_right, from_left, from_right_y, from_left_y, own = ins
    at_y, at_left, at_right, at_own = at

    def right(i):
        return from_right[at_left + i] + fold_rows(from_right_y[at_left + i], ny)

    def left(i):
        return from_left[at_right + i] + fold_rows(from_left_y[at_right + i], ny)

    for x in range(nx):
        plane = own[at_own + x] + fold_rows(from_y[at_y + x], ny)
        if x >= nx - LO:
            plane = plane + right(x - (nx - LO))
        if x < HI:
            plane = plane + left(x)
        put(x, plane)
    group = group_of(ny)
    rim = own[at_own + nx] + fold_rows(from_y[at_y + nx], ny)
    turn = 8 * nx
    high = pltpu.roll(right(LO), turn % LANES, 1)
    low = pltpu.roll(left(HI), (-turn) % LANES, 1)
    rim = rim + jnp.where((group >= nx) & (group < nx + LO), high, 0.0)
    return rim + jnp.where((group >= LO) & (group < LO + HI), low, 0.0)


def join_halo(field, ins, extended, nx, ny):
    from_y, from_right, from_left, from_right_y, from_left_y = ins

    def place(X, core, edges):
        extended[X, 0:ROWS] = edges[ROWS : 2 * ROWS]
        extended[X, ROWS : ROWS + ny] = core
        extended[X, ROWS + ny : 2 * ROWS + ny] = edges[0:ROWS]

    for x in range(nx):
        place(LO + x, field[x], from_y[x])
    for i in range(HI):
        place(LO + nx + i, from_right[i], from_right_y[i])
    for i in range(LO):
        place(i, from_left[i], from_left_y[i])


def fill(size, used, *messages):
    for message in messages:
        for i in range(used, size):
            message[i] = jnp.zeros(message.shape[1:], F32)


def split_halo(field, outs, nx, ny):
    to_y, to_left, to_right, to_left_y, to_right_y = outs
    for x in range(nx):
        put_edges(to_y, x, field[x], ny)
    for i in range(HI):
        to_left[i] = field[i]
        put_edges(to_left_y, i, field[i], ny)
    for i in range(LO):
        to_right[i] = field[nx - LO + i]
        put_edges(to_right_y, i, field[nx - LO + i], ny)


def table_kernel(nx, ny, departures, late, early, early_slopes):
    cells, fracs = departures.at[0], departures.at[1]
    write_tables(cells.at[1, 1], fracs.at[1, 1], late)
    write_tables(cells.at[0, 1], fracs.at[0, 1], early, early_slopes)


def first_kernel(
    nx, ny, pair, weights,
    to_y, to_l, to_r, to_ly, to_ry, own,
    scaled, piles, ends, piled, rims,
):
    deposit(pair.at[1:2], weights, scaled, piles, 2, SHIFTS)
    settle(piles, ends, piled.at[:, 0 : nx + LO + HI], rims)
    piled[0, nx + LO + HI] = rims[0]
    split_halo(pair.at[0], (to_y, to_l, to_r, to_ly, to_ry), nx, ny)
    split_deposits(piled.at[0], (to_y, to_l, to_r, to_ly, to_ry, own), (nx, HI, LO, 0), nx, ny)


def first_join_kernel(nx, ny, pair, from_y, from_r, from_l, from_ry, from_ly, own, extended, part, rims):
    rows = ny + 2 * ROWS
    join_halo(pair.at[0], (from_y, from_r, from_l, from_ry, from_ly), extended, nx, ny)
    rims[0:rows] = pack_rim(extended)

    def put(x, plane):
        part[x] = plane

    rims[rows : rows + ny] = join_deposits((from_y, from_r, from_l, from_ry, from_ly, own), (nx, HI, LO, 0), nx, ny, put)


def middle_kernel(
    nx, ny, extended, rims_l, rims_r, part, weights, slopes,
    image, to_y, to_l, to_r, to_ly, to_ry, adjoint, gradient,
    shifted, ends,
):
    rows = ny + 2 * ROWS
    rim = jnp.where(low_lanes(rows), rims_r[0:rows], rims_l[0:rows])
    shift_planes(extended, rim, ends, shifted)

    def emit(x, sums):
        image[x] = sums[3]
        for c in range(3):
            gradient[c, x] = sums[c]

    interpolate(shifted, weights, slopes, nx, ny, emit, True)
    split_halo(image, (to_y, to_l, to_r, to_ly, to_ry), nx, ny)
    fill(HI, LO, to_r, to_ry)
    back = jnp.where(low_lanes(ny), rims_l[rows : rows + ny], rims_r[rows : rows + ny])
    for x in range(nx):
        adjoint[0, x] = part[x] + unpack_rim(back, LO + x)


def adjoint_kernel(
    nx, ny, adjoint, weights, departures,
    piled, rims, early_mid, late_slopes, late_mid, cleared,
    scaled, piles, ends,
):
    cells, fracs = departures.at[0], departures.at[1]
    deposit(adjoint, weights, scaled, piles, 2, SHIFTS)
    settle(piles, ends, piled, rims)
    write_tables(cells.at[0, 0], fracs.at[0, 0], early_mid)
    write_tables(cells.at[1, 1], fracs.at[1, 1], None, late_slopes)
    write_tables(cells.at[1, 0], fracs.at[1, 0], late_mid)
    cleared[...] = jnp.zeros(cleared.shape, F32)


def early_kernel(nx, ny, gradient, adjoint, weights, cleared, piles, product, scaled):
    for c in range(3):
        for x in range(nx):
            product[c, x] = adjoint[0, x] * gradient[c, x]
    deposit(product, weights, scaled, piles, 1, SHIFTS // 2, fresh=False)


def second_join_kernel(nx, ny, image, from_y, from_r, from_l, from_ry, from_ly, earlier, extended, rims):
    join_halo(image, (from_y, from_r, from_l, from_ry, from_ly), extended, nx, ny)
    rims[...] = pack_rim(extended)


def late_kernel(
    nx, ny, extended, rims_l, rims_r, pair, weights, slopes, mid_weights, adjoint_rims, early_piles,
    piled, rims, piles,
    shifted, ends, product, scaled, rims_here,
):
    rows = ny + 2 * ROWS
    shift_planes(extended, jnp.where(low_lanes(rows), rims_r[...], rims_l[...]), ends.at[0], shifted)

    def emit(x, sums):
        for c in range(3):
            product[c, x] = pair[1, x] * sums[c]

    interpolate(shifted, weights, slopes, nx, ny, emit, False)
    deposit(product, mid_weights, scaled, piles, 1, SHIFTS // 2, fresh=False)
    settle(piles, ends, piled, rims_here)
    for c in range(3):
        rims[c * rows : (c + 1) * rows] = rims_here[c]
    rims[3 * rows : 4 * rows] = adjoint_rims[0]


def last_z_kernel(nx, ny, velocity, adjoint, rims_l, rims_r, to_y, to_l, to_r, to_ly, to_ry, own):
    rows = ny + 2 * ROWS
    low = low_lanes(rows)
    core = slice(ROWS, ROWS + ny)
    for c in range(4):
        here = slice(c * rows, (c + 1) * rows)
        back = jnp.where(low, rims_l[here], rims_r[here])
        for X in range(nx + LO + HI):
            plane = (velocity[c, X] if c < 3 else adjoint[0, X]) + unpack_rim(back, X)
            if X < LO:
                straight, corner, at = to_l, to_ly, c * LO + X
            elif X < LO + nx:
                straight, corner, at = own, to_y, c * nx + X - LO
            else:
                straight, corner, at = to_r, to_ry, c * HI + X - LO - nx
            straight[at] = plane[core]
            put_rims(corner, at, plane, ny)
    fill(4 * HI, 4 * LO, to_l, to_ly)


def last_kernel(nx, ny, own, from_y, from_r, from_l, from_ry, from_ly, intensity_adjoint, velocity_adjoint):
    for c in range(4):
        for x in range(nx):
            at = c * nx + x
            plane = own[at] + fold_rows(from_y[at], ny)
            if x >= nx - LO:
                at = c * LO + x - (nx - LO)
                plane = plane + from_r[at] + fold_rows(from_ry[at], ny)
            if x < HI:
                at = c * HI + x
                plane = plane + from_l[at] + fold_rows(from_ly[at], ny)
            if c == 3:
                intensity_adjoint[x] = plane
            else:
                velocity_adjoint[c, x] = plane


def call(kernel, args, outs, scratch, flops, spaces=None, aliases=None):
    def struct(shape):
        return jax.ShapeDtypeStruct(shape, F32)

    in_vmem = pl.BlockSpec(memory_space=pltpu.VMEM)
    in_specs = [in_vmem] * len(args)
    for i, space in (spaces or {}).items():
        in_specs[i] = pl.BlockSpec(memory_space=space)
    moved = 4 * sum(a.size for a in args)
    return pl.pallas_call(
        kernel,
        out_shape=[struct(s) for s in outs],
        in_specs=in_specs,
        out_specs=[in_vmem] * len(outs),
        scratch_shapes=[pltpu.VMEM(s, F32) if isinstance(s, tuple) else s for s in scratch],
        input_output_aliases=aliases or {},
        compiler_params=pltpu.CompilerParams(vmem_limit_bytes=24 * 1024 * 1024),
        cost_estimate=pl.CostEstimate(flops=flops, bytes_accessed=moved, transcendentals=0),
    )(*args)


def send(message, moves):
    axes = tuple(axis for axis, _ in moves)
    sizes = [lax.axis_size(axis) for axis in axes]
    if len(axes) == 1:
        pairs = [(i, (i + moves[0][1]) % sizes[0]) for i in range(sizes[0])]
        return lax.ppermute(message, axes[0], pairs)
    pairs = [
        (i * sizes[1] + j, (i + moves[0][1]) % sizes[0] * sizes[1] + (j + moves[1][1]) % sizes[1])
        for i in range(sizes[0])
        for j in range(sizes[1])
    ]
    return lax.ppermute(message, axes, pairs)


def send_y(message, *moves):
    if lax.axis_size("gy") == 2:
        return send(message, moves + (("gy", 1),))
    down = send(message[:, :ROWS], moves + (("gy", -1),))
    up = send(message[:, ROWS:], moves + (("gy", 1),))
    return jnp.concatenate([down, up], axis=1)


def send_sides(to_y, to_l, to_r, to_ly, to_ry):
    left, right = ("gx", -1), ("gx", 1)
    return (
        send_y(to_y),
        send(to_l, (left,)),
        send(to_r, (right,)),
        send_y(to_ly, left),
        send_y(to_ry, right),
    )


def send_z(rims):
    return send(rims, (("gz", 1),)), send(rims, (("gz", -1),))


def body(intensity, cotangent, cells, fracs):
    nx, ny, nz = intensity.shape
    rows = ny + 2 * ROWS
    planes = nx + LO + HI
    ring = 2 * ROWS
    field = (nx, ny, nz)
    table = (3, SHIFTS) + field
    pair = jnp.stack([intensity, cotangent])
    departures = jnp.stack([cells.astype(F32), fracs])
    unit = nx * ny * nz * 512

    def run(kernel, *rest, **more):
        return call(functools.partial(kernel, nx, ny), *rest, **more)

    def pile(channels):
        return [(channels, SHIFTS) + field, (channels, SHIFTS, planes, rows, nz)]

    def piled(channels):
        return [(channels, planes, rows, nz), (channels, rows, nz)]

    def messages(y, l, r):
        return [(y, ring, nz), (l, ny, nz), (r, ny, nz), (l, ring, nz), (r, ring, nz)]

    late, early, early_slopes = run(
        table_kernel,
        (departures,),
        [table, table, table],
        [],
        unit // 16,
    )
    *outs, own = run(
        first_kernel,
        (pair, late),
        messages(2 * nx + 1, HI + LO + 1, LO + HI + 1) + [(nx + 1, ny, nz)],
        pile(1) + [(1, planes, rows, nz), (1, planes + 1, rows, nz), (1, rows, nz)],
        2 * unit,
    )
    extended, folded, rims = run(
        first_join_kernel,
        (pair,) + send_sides(*outs) + (own,),
        [(planes, rows, nz), field, (rows + ny, nz)],
        [],
        unit // 16,
    )
    image, *outs, adjoint, gradient = run(
        middle_kernel,
        (extended,) + send_z(rims) + (folded, early, early_slopes),
        [field] + messages(nx, HI, HI) + [(1,) + field, (3,) + field],
        [(SHIFTS, planes, rows, nz), (planes, rows, nz)],
        5 * unit,
    )

    sides = send_sides(*outs)
    scaled_3, piles_3 = pile(3)
    piled_adjoint, adjoint_rims, early_mid, late_slopes, late_mid, cleared = run(
        adjoint_kernel,
        (adjoint, early, departures),
        piled(1) + [table, table, table, piles_3],
        pile(1) + [(1, planes, rows, nz)],
        2 * unit,
    )
    extended, rims = run(
        second_join_kernel,
        (image,) + sides + (piled_adjoint,),
        [(planes, rows, nz), (rows, nz)],
        [],
        unit // 16,
        spaces={6: pl.ANY},
    )
    rims_l, rims_r = send_z(rims)
    (piles,) = run(
        early_kernel,
        (gradient, adjoint, early_mid, cleared),
        [piles_3],
        [(3,) + field, scaled_3],
        6 * unit,
        aliases={3: 0},
    )

    velocity, rims, _ = run(
        late_kernel,
        (extended, rims_l, rims_r, pair, late, late_slopes, late_mid, adjoint_rims, piles),
        [(3, planes, rows, nz), (4 * rows, nz), piles_3],
        [(SHIFTS, planes, rows, nz), (3, planes, rows, nz), (3,) + field, scaled_3, (3, rows, nz)],
        11 * unit,
        aliases={8: 2},
    )
    *outs, own = run(
        last_z_kernel,
        (velocity, piled_adjoint) + send_z(rims),
        messages(4 * nx, 4 * HI, 4 * HI) + [(4 * nx, ny, nz)],
        [],
        unit // 16,
    )
    return tuple(
        run(
            last_kernel,
            (own,) + send_sides(*outs),
            [field, (3,) + field],
            [],
            unit // 16,
        )
    )


def solution(mesh):
    in_specs = (
        P("gx", "gy", "gz"),
        P("gx", "gy", "gz"),
        P(None, None, None, "gx", "gy", "gz"),
        P(None, None, None, "gx", "gy", "gz"),
    )
    out_specs = (P("gx", "gy", "gz"), P(None, "gx", "gy", "gz"))
    return jax.shard_map(body, mesh=mesh, in_specs=in_specs, out_specs=out_specs, check_vma=False)
```
